32 devices in a mesh: inner: 4 (over y, x), outer: 8 (over z, core).
Axes of the slice: x: 2, y: 2, z: 4, core: 2. Of those that a mesh axis runs over, the one named last changes fastest.
Arguments:
- queries: bfloat16 [8, 2048, 768], P('outer', 'inner'), may hold values from -8 to 8
- key_rows: bfloat16 [8, 2048, 768], P('outer', 'inner'), may hold values from -8 to 8
- values: bfloat16 [8, 2048, 768], P('outer', 'inner'), may hold values from -6 to 6
- out_weight: bfloat16 [768, 768], replicated, may hold values from -0.21875 to 0.21875
Outputs:
- attention_out: bfloat16 [8, 2048, 768], P('outer', 'inner')
The draws below stay inside these ranges and needn't reach their ends.
All inputs are finite; a program needn't handle non-finite values.
Results may differ from the reference program's by a relative error of at most 0.0052.
Values may be sent and summed in bfloat16 or wider, within the bound.
No kernel may reach another device: no remote copies, remote signals or barrier semaphores. Data moves between devices by JAX's collectives and lax.ppermute only.
A program may use at most 64 MiB of HBM per device.

```python
import jax
import jax.numpy as jnp
from jax import lax

HEADS = 12
HEAD_DIM = 64
D = 768
TOK_DEV = 512
GSTEP = 64
IBITS = 2
SEG_ROWS = 2048
N_INNER = 4
N_OUTER = 8


def base_rows(key):
    shape_rows = (N_OUTER, N_INNER, TOK_DEV, D)
    rows = 2.0 * jnp.clip(jax.random.normal(key, shape_rows, jnp.float32), -4.0, 4.0)
    return rows


def draw_key_rows(key, part):
    rows = base_rows(jax.random.fold_in(key, 31))
    return rows.reshape(N_OUTER, N_INNER * TOK_DEV, D).astype(jnp.bfloat16)


def draw_queries(key, part):
    rows = base_rows(jax.random.fold_in(key, 41))
    return rows.reshape(N_OUTER, N_INNER * TOK_DEV, D).astype(jnp.bfloat16)


def shard_levels(rng, extent, cuts, least, top_value):
    level, own = 1.0, jax.random.fold_in(rng, 6)
    for axis_at, blocks in cuts:
        heights = jnp.exp(jax.random.uniform(jax.random.fold_in(own, axis_at), (blocks,), jnp.float32, least / len(cuts), top_value / len(cuts)))
        level = level * jnp.repeat(heights, extent[axis_at] // blocks).reshape([-1 if axis == axis_at else 1 for axis in range(len(extent))])
    return level


def normal_values(own_key, shape, deviation, reach, pieces=(), kind=jnp.bfloat16):
    factor_of = shard_levels(own_key, shape, pieces, -0.22, 0.18) if pieces else 1.0
    values = jax.random.normal(own_key, shape, jnp.float32) * deviation * factor_of
    return jnp.minimum(jnp.maximum(values, -reach), reach).astype(kind)


def setup_inputs(seed: int = 0) -> dict:
    seeds = jax.random.split(jax.random.key(seed), 5)
    return {
        "queries": draw_queries(jax.random.fold_in(seeds[4], 71), 0),
        "key_rows": draw_key_rows(jax.random.fold_in(seeds[4], 71), 0),
        "values": normal_values(seeds[2], (N_OUTER, SEG_ROWS, D), 1.0, 6.0, ((0, 8), (1, 4))),
        "out_weight": normal_values(seeds[3], (D, D), D ** -0.5, 0.21875),
    }


def level_terms(query_rows, key_set, value_set):
    scale_factor = HEAD_DIM ** -0.5
    head_query = query_rows.astype(jnp.float32).reshape(TOK_DEV, HEADS, HEAD_DIM)
    head_keys = key_set.astype(jnp.float32).reshape(-1, HEADS, HEAD_DIM)
    head_values = value_set.astype(jnp.float32).reshape(-1, HEADS, HEAD_DIM)
    scores = jnp.einsum("thd,nhd->htn", head_query, head_keys) * scale_factor
    row_peak = jnp.max(scores, axis=2, keepdims=True)
    expo_rows = jnp.exp(scores - row_peak)
    row_total = jnp.sum(expo_rows, axis=2, keepdims=True)
    weights = lax.optimization_barrier(expo_rows.astype(jnp.bfloat16)).astype(jnp.float32)
    numerator = jnp.einsum("htn,nhd->htd", weights, head_values)
    return row_peak, row_total, numerator


def merge_levels(all_terms):
    overall_peak = jnp.max(jnp.stack([entry[0] for entry in all_terms]), axis=0)
    numer_sum = jnp.zeros_like(all_terms[0][2])
    denom_sum = jnp.zeros_like(all_terms[0][1])
    for entry in all_terms:
        factor = jnp.exp(entry[0] - overall_peak)
        numer_sum = numer_sum + factor * entry[2]
        denom_sum = denom_sum + factor * entry[1]
    return numer_sum / denom_sum


def reference(queries, key_rows, values, out_weight):
    flat_queries = queries.reshape(-1, D)
    flat_keys = key_rows.reshape(-1, D)
    flat_values = values.reshape(-1, D)
    global_keys = flat_keys[::GSTEP]
    global_values = flat_values[::GSTEP]
    device_count = N_INNER * N_OUTER

    def per_device(device):
        device = device.astype(jnp.int32)
        query_rows = lax.dynamic_slice_in_dim(flat_queries, (device * TOK_DEV).astype(jnp.int32), TOK_DEV, 0)
        collected = []
        for level_index in range(IBITS + 2):
            stride = 2 ** level_index
            span_rows = stride * TOK_DEV
            row_start = ((device // stride) * span_rows).astype(jnp.int32)
            seg_keys = lax.dynamic_slice_in_dim(flat_keys, row_start, span_rows, 0)[::stride]
            seg_values = lax.dynamic_slice_in_dim(flat_values, row_start, span_rows, 0)[::stride]
            collected.append(level_terms(query_rows, seg_keys, seg_values))
        collected.append(level_terms(query_rows, global_keys, global_values))
        merged = merge_levels(collected)
        attended = merged.transpose(1, 0, 2).reshape(TOK_DEV, D).astype(jnp.bfloat16)
        return jnp.dot(attended, out_weight, preferred_element_type=jnp.float32).astype(jnp.bfloat16)

    result = lax.map(per_device, jnp.arange(device_count, dtype=jnp.int32))
    return result.reshape(N_OUTER, N_INNER * TOK_DEV, D)
```

```python
import functools
import math

import jax
import jax.numpy as jnp
import numpy as np
from jax import lax
from jax.experimental import pallas as pl
from jax.experimental.pallas import tpu as pltpu
from jax.sharding import PartitionSpec as P

HEAD_DIM = 64
GSTEP = 64
PAIR = 2 * HEAD_DIM
CHUNK = 256
LOG2E = math.log2(math.e)
VMEM_BYTES = 56 * 1024 * 1024


def across(block, axis, bit):
    count = lax.axis_size(axis)
    return lax.ppermute(block, axis, [(i, i ^ (1 << bit)) for i in range(count)])


def nested_order(tokens, strides):
    rows = np.arange(tokens)
    rank = sum((rows % s == 0).astype(np.int64) for s in strides)
    return np.lexsort((rows, -rank)), rank


def runs(counts):
    found = []
    for at, value in enumerate(counts):
        if found and found[-1][2] == value:
            found[-1][1] = at + 1
        else:
            found.append([at, at + 1, int(value)])
    return [tuple(entry) for entry in found]


def order_rows(select, key_rows, values, prefixes):
    tokens, width = key_rows.shape

    def kernel(select_ref, key_ref, value_ref, all_ref, *prefix_refs):
        for half, ref in enumerate((key_ref, value_ref)):
            moved = jnp.dot(
                select_ref[...], ref[...], preferred_element_type=jnp.float32
            ).astype(jnp.bfloat16)
            cols = slice(half * width, (half + 1) * width)
            all_ref[:, cols] = moved
            for (low, high), prefix_ref in zip(prefixes, prefix_refs):
                prefix_ref[:, cols] = moved[low:high]

    shapes = [(tokens, 2 * width)] + [(high - low, 2 * width) for low, high in prefixes]
    return pl.pallas_call(
        kernel,
        out_shape=[jax.ShapeDtypeStruct(shape, jnp.bfloat16) for shape in shapes],
        compiler_params=pltpu.CompilerParams(vmem_limit_bytes=VMEM_BYTES),
        cost_estimate=pl.CostEstimate(
            flops=4 * tokens * tokens * width, bytes_accessed=10 * tokens * width, transcendentals=0
        ),
    )(select, key_rows, values)


def attend(queries, sets, counts, state=None, out_weight=None):
    tokens, width = queries.shape
    heads, pairs = width // HEAD_DIM, width // PAIR
    sizes = [block.shape[0] for block in sets]
    keys = sum(sizes)
    padded = -(-keys // CHUNK) * CHUNK
    row_runs = runs(counts)
    scale = HEAD_DIM**-0.5 * LOG2E
    final = out_weight is not None
    n_state = 0 if state is None else 3

    def kernel(*refs):
        query_ref, refs = refs[0], refs[1:]
        set_refs, refs = refs[: len(sets)], refs[len(sets) :]
        state_refs, refs = refs[:n_state], refs[n_state:]
        if final:
            weight_ref, out_ref, score_ref, value_ref, attended_ref = refs
        else:
            numer_out, peak_out, total_out, score_ref, value_ref = refs

        ones = jnp.ones((16, padded), jnp.bfloat16)

        def pair_step(pair, carry):
            base = pl.multiple_of(pair * PAIR, PAIR)
            query_pair = query_ref[:, pl.ds(base, PAIR)]
            lane = lax.broadcasted_iota(jnp.int32, query_pair.shape, 1)
            at = 0
            for ref, size in zip(set_refs, sizes):
                value_ref[at : at + size, :] = ref[:, pl.ds(base + width, PAIR)]
                at += size
            if padded > keys:
                value_ref[keys:, :] = jnp.zeros((padded - keys, PAIR), jnp.bfloat16)
            values_t = value_ref[...].T
            for half in range(2):
                head = 2 * pair + half
                own = (lane < HEAD_DIM) if half == 0 else (lane >= HEAD_DIM)
                query_head = jnp.where(own, query_pair, jnp.zeros_like(query_pair))
                running = None
                at = 0
                for ref, size in zip(set_refs, sizes):
                    for low in range(0, size, CHUNK):
                        count = min(CHUNK, size - low)
                        scores = lax.dot_general(
                            ref[low : low + count, pl.ds(base, PAIR)],
                            query_head,
                            (((1,), (1,)), ((), ())),
                            preferred_element_type=jnp.float32,
                        )
                        score_ref[half, at : at + count, :] = scores
                        tallest = jnp.max(scores.reshape(count // 8, 8, tokens), axis=0)
                        running = tallest if running is None else jnp.maximum(running, tallest)
                        at += count
                peak = jnp.max(running, axis=0, keepdims=True) * scale
                if state is not None:
                    before = state_refs[1][pl.ds(head, 1), :]
                    peak = jnp.maximum(peak, before)
                weighted = jnp.concatenate(
                    [values_t[half * HEAD_DIM : (half + 1) * HEAD_DIM], ones], axis=0
                )
                gathered = None
                for low in range(0, padded, CHUNK):
                    high = min(low + CHUNK, keys)
                    pieces = []
                    for first, last, times in row_runs:
                        first, last = max(first, low), min(last, high)
                        if first < last:
                            offset = peak - math.log2(times)
                            pieces.append(
                                jnp.exp2(score_ref[half, first:last, :] * scale - offset)
                            )
                    if low + CHUNK > keys:
                        pieces.append(jnp.zeros((low + CHUNK - keys, tokens), jnp.float32))
                    probs = (
                        pieces[0] if len(pieces) == 1 else jnp.concatenate(pieces, axis=0)
                    ).astype(jnp.bfloat16)
                    product = jnp.dot(
                        weighted[:, low : low + CHUNK], probs, preferred_element_type=jnp.float32
                    )
                    gathered = product if gathered is None else gathered + product
                numer, total = gathered[:HEAD_DIM], gathered[HEAD_DIM : HEAD_DIM + 1]
                rows = pl.ds(pl.multiple_of(base + half * HEAD_DIM, HEAD_DIM), HEAD_DIM)
                if state is not None:
                    factor = jnp.exp2(before - peak)
                    numer = numer + factor * state_refs[0][rows, :]
                    total = total + factor * state_refs[2][pl.ds(head, 1), :]
                if final:
                    attended_ref[rows, :] = (numer / total).astype(jnp.bfloat16)
                else:
                    numer_out[rows, :] = numer
                    peak_out[pl.ds(head, 1), :] = peak
                    total_out[pl.ds(head, 1), :] = total
            return carry

        lax.fori_loop(0, pairs, pair_step, 0)
        if final:
            out_ref[...] = lax.dot_general(
                attended_ref[...],
                weight_ref[...],
                (((0,), (0,)), ((), ())),
                preferred_element_type=jnp.float32,
            ).astype(jnp.bfloat16)

    if final:
        out_shape = jax.ShapeDtypeStruct((tokens, width), jnp.bfloat16)
    else:
        out_shape = [
            jax.ShapeDtypeStruct((width, tokens), jnp.float32),
            jax.ShapeDtypeStruct((heads, tokens), jnp.float32),
            jax.ShapeDtypeStruct((heads, tokens), jnp.float32),
        ]
    scratch = [
        pltpu.VMEM((2, padded, tokens), jnp.float32),
        pltpu.VMEM((padded, PAIR), jnp.bfloat16),
    ]
    if final:
        scratch.append(pltpu.VMEM((width, tokens), jnp.bfloat16))
    operands = [queries, *sets, *(state or []), *([out_weight] if final else [])]
    return pl.pallas_call(
        kernel,
        out_shape=out_shape,
        scratch_shapes=scratch,
        compiler_params=pltpu.CompilerParams(vmem_limit_bytes=VMEM_BYTES),
        cost_estimate=pl.CostEstimate(
            flops=16 * tokens * keys * width,
            bytes_accessed=4 * keys * width + 4 * tokens * width,
            transcendentals=tokens * keys * heads,
        ),
    )(*operands)


def local(queries, key_rows, values, out_weight):
    query_rows = queries[0]
    tokens = query_rows.shape[0]
    inner_bits = lax.axis_size("inner").bit_length() - 1
    outer_bits = lax.axis_size("outer").bit_length() - 1
    strides = [1 << (bit + 1) for bit in range(inner_bits + 1)] + [GSTEP]
    order, rank = nested_order(tokens, strides)
    select = np.zeros((tokens, tokens), np.float32)
    select[np.arange(tokens), order] = 1.0

    def prefix_counts(level, length):
        used = strides[level:]
        return sum((order[:length] % s == 0).astype(np.int64) for s in used)

    sends = [tokens >> (bit + 1) for bit in range(inner_bits + 1)]
    n_global = tokens // GSTEP
    prefixes = [(0, sends[1]), (sends[1], sends[0])]
    prefixes += [(0, count) for count in sends[1:]] + [(0, n_global)]
    ordered = order_rows(jnp.asarray(select, jnp.bfloat16), key_rows[0], values[0], prefixes)
    own, first_a, first_b = ordered[:3]
    own_sends, own_global = ordered[3:-1], ordered[-1]

    near_a = across(first_a, "inner", 0)
    direct = [across(own_sends[bit - 1], "inner", bit) for bit in range(1, inner_bits)]
    far = own_global
    far_parts = []
    for bit in range(1, outer_bits):
        came = across(far, "outer", bit)
        far = jnp.concatenate([far, came], axis=0)
    far = far[n_global:]
    near_b = across(first_b, "inner", 0)
    far = jnp.concatenate([far, across(far, "inner", 0)], axis=0)

    state = attend(query_rows, [own], 1 + rank[order])

    sets, counts = [near_a, near_b], [prefix_counts(0, sends[0])]
    held = [near_a]
    for bit in range(1, inner_bits):
        count = sends[bit]
        moved = jnp.concatenate([block[:count] for block in held] + [far], axis=0)
        came = across(moved, "inner", bit)
        sets += [direct[bit - 1], came]
        n_held = len(held) * count
        counts += [prefix_counts(bit, count)] * (1 + len(held))
        counts.append(np.ones(far.shape[0], np.int64))
        held = held + [direct[bit - 1]] + [
            came[at : at + count] for at in range(0, n_held, count)
        ]
        far = jnp.concatenate([far, came[n_held:]], axis=0)
    count = sends[inner_bits]
    moved = jnp.concatenate(
        [own_sends[inner_bits - 1]] + [block[:count] for block in held] + [far], axis=0
    )
    came = across(moved, "outer", 0)
    sets.append(came)
    counts += [prefix_counts(inner_bits, count)] * (1 + len(held))
    counts.append(np.ones(far.shape[0], np.int64))
    n_near = far.shape[0] >> (inner_bits - 1) if inner_bits > 1 else far.shape[0]
    sets.append(far[:n_near])
    counts.append(np.ones(n_near, np.int64))

    result = attend(query_rows, sets, np.concatenate(counts), state, out_weight)
    return result[None]


def solution(mesh):
    placed = (P("outer", "inner", None), P("outer", "inner", None), P("outer", "inner", None), P())
    return jax.shard_map(
        local, mesh=mesh, in_specs=placed, out_specs=P("outer", "inner", None), check_vma=False
    )
```

```python
import functools
import math

import jax
import jax.numpy as jnp
import numpy as np
from jax import lax
from jax.experimental import pallas as pl
from jax.experimental.pallas import tpu as pltpu
from jax.sharding import PartitionSpec as P

HEAD_DIM = 64
GSTEP = 64
PAIR = 2 * HEAD_DIM
CHUNK = 256
LOG2E = math.log2(math.e)
VMEM_BYTES = 56 * 1024 * 1024


def across(block, axis, bit):
    count = lax.axis_size(axis)
    return lax.ppermute(block, axis, [(i, i ^ (1 << bit)) for i in range(count)])


def nested_order(tokens, strides):
    rows = np.arange(tokens)
    rank = sum((rows % s == 0).astype(np.int64) for s in strides)
    return np.lexsort((rows, -rank)), rank


def runs(counts):
    found = []
    for at, value in enumerate(counts):
        if found and found[-1][2] == value:
            found[-1][1] = at + 1
        else:
            found.append([at, at + 1, int(value)])
    return [tuple(entry) for entry in found]


def order_rows(select, key_rows, values, prefixes):
    tokens, width = key_rows.shape

    def kernel(select_ref, key_ref, value_ref, all_ref, *prefix_refs):
        for half, ref in enumerate((key_ref, value_ref)):
            moved = jnp.dot(
                select_ref[...], ref[...], preferred_element_type=jnp.float32
            ).astype(jnp.bfloat16)
            cols = slice(half * width, (half + 1) * width)
            all_ref[:, cols] = moved
            for (low, high), prefix_ref in zip(prefixes, prefix_refs):
                prefix_ref[:, cols] = moved[low:high]

    shapes = [(tokens, 2 * width)] + [(high - low, 2 * width) for low, high in prefixes]
    return pl.pallas_call(
        kernel,
        out_shape=[jax.ShapeDtypeStruct(shape, jnp.bfloat16) for shape in shapes],
        compiler_params=pltpu.CompilerParams(vmem_limit_bytes=VMEM_BYTES),
        cost_estimate=pl.CostEstimate(
            flops=4 * tokens * tokens * width, bytes_accessed=10 * tokens * width, transcendentals=0
        ),
    )(select, key_rows, values)


def attend(queries, sets, counts, state=None, out_weight=None):
    tokens, width = queries.shape
    heads, pairs = width // HEAD_DIM, width // PAIR
    sizes = [block.shape[0] for block in sets]
    keys = sum(sizes)
    padded = -(-keys // CHUNK) * CHUNK
    row_runs = runs(counts)
    scale = HEAD_DIM**-0.5 * LOG2E
    final = out_weight is not None
    n_state = 0 if state is None else 3

    def kernel(*refs):
        query_ref, refs = refs[0], refs[1:]
        set_refs, refs = refs[: len(sets)], refs[len(sets) :]
        state_refs, refs = refs[:n_state], refs[n_state:]
        if final:
            weight_ref, out_ref, score_ref, value_ref, attended_ref = refs
        else:
            numer_out, peak_out, total_out, score_ref, value_ref = refs

        ones = jnp.ones((16, padded), jnp.bfloat16)
        key_chunks = []
        at = 0
        for ref, size in zip(set_refs, sizes):
            for low in range(0, size, CHUNK):
                count = min(CHUNK, size - low)
                key_chunks.append((ref, low, count, at))
                at += count
        value_chunks = list(range(0, padded, CHUNK))

        def column(pair):
            return pl.multiple_of(pair * PAIR, PAIR)

        def head_queries(pair, half):
            turned = query_ref[:, pl.ds(column(pair), PAIR)].T
            row = lax.broadcasted_iota(jnp.int32, turned.shape, 0)
            own = (row < HEAD_DIM) if half == 0 else (row >= HEAD_DIM)
            return jnp.where(own, turned, jnp.zeros_like(turned))

        def score(pair, half, query_head, chunk, running):
            ref, low, count, at = chunk
            scores = jnp.dot(
                ref[low : low + count, pl.ds(column(pair), PAIR)],
                query_head,
                preferred_element_type=jnp.float32,
            )
            score_ref[half, at : at + count, :] = scores
            tallest = jnp.max(scores.reshape(count // 8, 8, tokens), axis=0)
            return tallest if running is None else jnp.maximum(running, tallest)

        def weigh(half, peak, weighted, low, gathered):
            high = min(low + CHUNK, keys)
            pieces = []
            for first, last, times in row_runs:
                first, last = max(first, low), min(last, high)
                if first < last:
                    offset = peak - math.log2(times)
                    pieces.append(jnp.exp2(score_ref[half, first:last, :] * scale - offset))
            if low + CHUNK > keys:
                pieces.append(jnp.zeros((low + CHUNK - keys, tokens), jnp.float32))
            probs = (pieces[0] if len(pieces) == 1 else jnp.concatenate(pieces, axis=0)).astype(
                jnp.bfloat16
            )
            product = jnp.dot(
                weighted[:, low : low + CHUNK], probs, preferred_element_type=jnp.float32
            )
            return product if gathered is None else gathered + product

        def finish(pair, half, gathered, peak, before):
            head = 2 * pair + half
            numer, total = gathered[:HEAD_DIM], gathered[HEAD_DIM : HEAD_DIM + 1]
            rows = pl.ds(pl.multiple_of(column(pair) + half * HEAD_DIM, HEAD_DIM), HEAD_DIM)
            if state is not None:
                factor = jnp.exp2(before - peak)
                numer = numer + factor * state_refs[0][rows, :]
                total = total + factor * state_refs[2][pl.ds(head, 1), :]
            if final:
                attended_ref[rows, :] = (numer / total).astype(jnp.bfloat16)
            else:
                numer_out[rows, :] = numer
                peak_out[pl.ds(head, 1), :] = peak
                total_out[pl.ds(head, 1), :] = total

        def overlap(pair, half, running, values_t, next_pair, next_half):
            peak = jnp.max(running, axis=0, keepdims=True) * scale
            before = None
            if state is not None:
                before = state_refs[1][pl.ds(2 * pair + half, 1), :]
                peak = jnp.maximum(peak, before)
            weighted = jnp.concatenate(
                [values_t[half * HEAD_DIM : (half + 1) * HEAD_DIM], ones], axis=0
            )
            query_head = head_queries(next_pair, next_half)
            next_running, gathered = None, None
            for step in range(max(len(key_chunks), len(value_chunks))):
                if step < len(key_chunks):
                    next_running = score(
                        next_pair, next_half, query_head, key_chunks[step], next_running
                    )
                if step < len(value_chunks):
                    gathered = weigh(half, peak, weighted, value_chunks[step], gathered)
            finish(pair, half, gathered, peak, before)
            return next_running

        def pair_step(pair, running):
            at = 0
            for ref, size in zip(set_refs, sizes):
                value_ref[at : at + size, :] = ref[:, pl.ds(column(pair) + width, PAIR)]
                at += size
            if padded > keys:
                value_ref[keys:, :] = jnp.zeros((padded - keys, PAIR), jnp.bfloat16)
            values_t = value_ref[...].T
            running = overlap(pair, 0, running, values_t, pair, 1)
            later = jnp.minimum(pair + 1, pairs - 1)
            return overlap(pair, 1, running, values_t, later, 0)

        first_head = head_queries(0, 0)
        running = None
        for chunk in key_chunks:
            running = score(0, 0, first_head, chunk, running)
        lax.fori_loop(0, pairs, pair_step, running)
        if final:
            out_ref[...] = lax.dot_general(
                attended_ref[...],
                weight_ref[...],
                (((0,), (0,)), ((), ())),
                preferred_element_type=jnp.float32,
            ).astype(jnp.bfloat16)

    if final:
        out_shape = jax.ShapeDtypeStruct((tokens, width), jnp.bfloat16)
    else:
        out_shape = [
            jax.ShapeDtypeStruct((width, tokens), jnp.float32),
            jax.ShapeDtypeStruct((heads, tokens), jnp.float32),
            jax.ShapeDtypeStruct((heads, tokens), jnp.float32),
        ]
    scratch = [
        pltpu.VMEM((2, padded, tokens), jnp.float32),
        pltpu.VMEM((padded, PAIR), jnp.bfloat16),
    ]
    if final:
        scratch.append(pltpu.VMEM((width, tokens), jnp.bfloat16))
    operands = [queries, *sets, *(state or []), *([out_weight] if final else [])]
    return pl.pallas_call(
        kernel,
        out_shape=out_shape,
        scratch_shapes=scratch,
        compiler_params=pltpu.CompilerParams(vmem_limit_bytes=VMEM_BYTES),
        cost_estimate=pl.CostEstimate(
            flops=16 * tokens * keys * width,
            bytes_accessed=4 * keys * width + 4 * tokens * width,
            transcendentals=tokens * keys * heads,
        ),
    )(*operands)


def local(queries, key_rows, values, out_weight):
    query_rows = queries[0]
    tokens = query_rows.shape[0]
    inner_bits = lax.axis_size("inner").bit_length() - 1
    outer_bits = lax.axis_size("outer").bit_length() - 1
    strides = [1 << (bit + 1) for bit in range(inner_bits + 1)] + [GSTEP]
    order, rank = nested_order(tokens, strides)
    select = np.zeros((tokens, tokens), np.float32)
    select[np.arange(tokens), order] = 1.0

    def prefix_counts(level, length):
        used = strides[level:]
        return sum((order[:length] % s == 0).astype(np.int64) for s in used)

    sends = [tokens >> (bit + 1) for bit in range(inner_bits + 1)]
    n_global = tokens // GSTEP
    prefixes = [(0, sends[1]), (sends[1], sends[0])]
    prefixes += [(0, count) for count in sends[1:]] + [(0, n_global)]
    ordered = order_rows(jnp.asarray(select, jnp.bfloat16), key_rows[0], values[0], prefixes)
    own, first_a, first_b = ordered[:3]
    own_sends, own_global = ordered[3:-1], ordered[-1]

    near_a = across(first_a, "inner", 0)
    direct = [across(own_sends[bit - 1], "inner", bit) for bit in range(1, inner_bits)]
    far = own_global
    far_parts = []
    for bit in range(1, outer_bits):
        came = across(far, "outer", bit)
        far = jnp.concatenate([far, came], axis=0)
    far = far[n_global:]
    near_b = across(first_b, "inner", 0)
    far = jnp.concatenate([far, across(far, "inner", 0)], axis=0)

    state = attend(query_rows, [own], 1 + rank[order])

    sets, counts = [near_a, near_b], [prefix_counts(0, sends[0])]
    held = [near_a]
    for bit in range(1, inner_bits):
        count = sends[bit]
        moved = jnp.concatenate([block[:count] for block in held] + [far], axis=0)
        came = across(moved, "inner", bit)
        sets += [direct[bit - 1], came]
        n_held = len(held) * count
        counts += [prefix_counts(bit, count)] * (1 + len(held))
        counts.append(np.ones(far.shape[0], np.int64))
        held = held + [direct[bit - 1]] + [
            came[at : at + count] for at in range(0, n_held, count)
        ]
        far = jnp.concatenate([far, came[n_held:]], axis=0)
    count = sends[inner_bits]
    moved = jnp.concatenate(
        [own_sends[inner_bits - 1]] + [block[:count] for block in held] + [far], axis=0
    )
    came = across(moved, "outer", 0)
    sets.append(came)
    counts += [prefix_counts(inner_bits, count)] * (1 + len(held))
    counts.append(np.ones(far.shape[0], np.int64))
    n_near = far.shape[0] >> (inner_bits - 1) if inner_bits > 1 else far.shape[0]
    sets.append(far[:n_near])
    counts.append(np.ones(n_near, np.int64))

    result = attend(query_rows, sets, np.concatenate(counts), state, out_weight)
    return result[None]


def solution(mesh):
    placed = (P("outer", "inner", None), P("outer", "inner", None), P("outer", "inner", None), P())
    return jax.shard_map(
        local, mesh=mesh, in_specs=placed, out_specs=P("outer", "inner", None), check_vma=False
    )
```

```python
import math

import jax
import jax.numpy as jnp
import numpy as np
from jax import lax
from jax.experimental import pallas as pl
from jax.experimental.pallas import tpu as pltpu
from jax.sharding import PartitionSpec as P

HEAD_DIM = 64
GSTEP = 64
PAIR = 2 * HEAD_DIM
CHUNK = 256
COST = 1
LANES = 128
LOG2E = math.log2(math.e)
VMEM_BYTES = 24 * 1024 * 1024


def across(block, axis, bit):
    count = lax.axis_size(axis)
    return lax.ppermute(block, axis, [(i, i ^ (1 << bit)) for i in range(count)])


def after(block, *others):
    return lax.optimization_barrier((block, *others))[0]


def runs(counts):
    found = []
    for at, value in enumerate(counts):
        if found and found[-1][2] == value:
            found[-1][1] = at + 1
        else:
            found.append([at, at + 1, int(value)])
    return [tuple(entry) for entry in found]


def order_rows(select, key_rows, values, prefixes):
    tokens, width = key_rows.shape

    def kernel(select_ref, key_ref, value_ref, *out_refs):
        for half, ref in enumerate((key_ref, value_ref)):
            moved = jnp.dot(
                select_ref[...], ref[...], preferred_element_type=jnp.float32
            ).astype(jnp.bfloat16)
            for (low, high), out_ref in zip(prefixes, out_refs):
                out_ref[:, half * width : (half + 1) * width] = moved[low:high]

    return pl.pallas_call(
        kernel,
        out_shape=[
            jax.ShapeDtypeStruct((high - low, 2 * width), jnp.bfloat16) for low, high in prefixes
        ],
        compiler_params=pltpu.CompilerParams(vmem_limit_bytes=VMEM_BYTES),
        cost_estimate=pl.CostEstimate(
            flops=4 * select.size * width, bytes_accessed=6 * tokens * width, transcendentals=0
        ),
    )(select, key_rows, values)


def attend(queries, sets, counts=None, row_strides=None, part=(0, 1), states=(), out_weight=None, cost=1):
    tokens = queries.shape[0]
    width = queries.shape[1] // part[1]
    heads, pairs = width // HEAD_DIM, width // PAIR
    joined = [not isinstance(block, tuple) for block in sets]
    sizes = [(block if whole else block[0]).shape[0] for block, whole in zip(sets, joined)]
    keys = sum(sizes)
    padded = -(-keys // CHUNK) * CHUNK
    row_runs = [(0, keys, 1)] if counts is None else runs(counts)
    scale = HEAD_DIM**-0.5 * LOG2E
    final = out_weight is not None
    groups = max(len(states), 1)

    def kernel(*refs):
        refs = list(refs)
        query_ref = refs.pop(0)
        set_refs = []
        for whole in joined:
            ref = refs.pop(0)
            set_refs.append((ref, 0, ref, width) if whole else (ref, 0, refs.pop(0), 0))
        state_refs = [[refs.pop(0) for _ in range(3)] for _ in states]
        if final:
            weight_ref, out_ref, attended_ref = refs.pop(0), refs.pop(0), refs.pop(-1)
        else:
            numer_out, peak_out, total_out = [refs.pop(0) for _ in range(3)]
        score_ref, value_ref = refs.pop(0), refs.pop(0)
        if row_strides is not None:
            offset_ref = refs.pop(0)
            row = lax.broadcasted_iota(jnp.int32, (keys, LANES), 0)
            rank = sum((row & (s - 1) == 0).astype(jnp.int32) for s in row_strides)
            offsets = jnp.zeros((keys, LANES), jnp.float32)
            for times in range(1, len(row_strides) + 1):
                offsets = jnp.where(rank == times, math.log2(1 + times), offsets)
            offset_ref[...] = offsets

        ones = jnp.ones((16, padded), jnp.bfloat16)
        key_chunks = []
        at = 0
        for entry, size in zip(set_refs, sizes):
            for low in range(0, size, CHUNK):
                count = min(CHUNK, size - low)
                key_chunks.append((entry[0], low, count, at))
                at += count
        value_chunks = list(range(0, padded, CHUNK))

        def column(pair):
            return pl.multiple_of(pair * PAIR, PAIR)

        def head_queries(pair, half):
            turned = query_ref[:, pl.ds(column(pair), PAIR)].T
            row = lax.broadcasted_iota(jnp.int32, turned.shape, 0)
            own = (row < HEAD_DIM) if half == 0 else (row >= HEAD_DIM)
            return jnp.where(own, turned, jnp.zeros_like(turned))

        def score(pair, half, query_head, chunk, running):
            ref, low, count, at = chunk
            scores = jnp.dot(
                ref[low : low + count, pl.ds(column(pair), PAIR)],
                query_head,
                preferred_element_type=jnp.float32,
            )
            score_ref[half, at : at + count, :] = scores
            tallest = jnp.max(scores.reshape(count // 8, 8, tokens), axis=0)
            return tallest if running is None else jnp.maximum(running, tallest)

        def weigh(half, peak, weighted, low, gathered):
            high = min(low + CHUNK, keys)
            pieces = []
            for first, last, times in row_runs:
                first, last = max(first, low), min(last, high)
                if first < last:
                    offset = peak - math.log2(times)
                    power = score_ref[half, first:last, :] * scale - offset
                    if row_strides is not None:
                        extra = offset_ref[first:last, :]
                        power = power + jnp.concatenate([extra] * (tokens // LANES), axis=1)
                    pieces.append(jnp.exp2(power))
            if low + CHUNK > keys:
                pieces.append(jnp.zeros((low + CHUNK - keys, tokens), jnp.float32))
            probs = (pieces[0] if len(pieces) == 1 else jnp.concatenate(pieces, axis=0)).astype(
                jnp.bfloat16
            )
            product = jnp.dot(
                weighted[:, low : low + CHUNK], probs, preferred_element_type=jnp.float32
            )
            return product if gathered is None else gathered + product

        def one_group(first_pair, last_pair, earlier):
            def local_rows(pair, half):
                start = (pair - first_pair) * PAIR + half * HEAD_DIM
                return pl.ds(pl.multiple_of(start, HEAD_DIM), HEAD_DIM)

            def local_head(pair, half):
                return pl.ds(2 * (pair - first_pair) + half, 1)

            def finish(pair, half, gathered, peak, before):
                numer, total = gathered[:HEAD_DIM], gathered[HEAD_DIM : HEAD_DIM + 1]
                if earlier is not None:
                    factor = jnp.exp2(before - peak)
                    numer = numer + factor * earlier[0][local_rows(pair, half), :]
                    total = total + factor * earlier[2][local_head(pair, half), :]
                start = pl.multiple_of(column(pair) + half * HEAD_DIM, HEAD_DIM)
                rows = pl.ds(start, HEAD_DIM)
                if final:
                    attended_ref[rows, :] = (numer / total).astype(jnp.bfloat16)
                else:
                    head = pl.ds(2 * pair + half, 1)
                    numer_out[rows, :] = numer
                    peak_out[head, :] = peak
                    total_out[head, :] = total

            def overlap(pair, half, running, values_t, next_pair, next_half):
                peak = jnp.max(running, axis=0, keepdims=True) * scale
                before = None
                if earlier is not None:
                    before = earlier[1][local_head(pair, half), :]
                    peak = jnp.maximum(peak, before)
                weighted = jnp.concatenate(
                    [values_t[half * HEAD_DIM : (half + 1) * HEAD_DIM], ones], axis=0
                )
                query_head = head_queries(next_pair, next_half)
                next_running, gathered = None, None
                for step in range(max(len(key_chunks), len(value_chunks))):
                    if step < len(key_chunks):
                        next_running = score(
                            next_pair, next_half, query_head, key_chunks[step], next_running
                        )
                    if step < len(value_chunks):
                        gathered = weigh(half, peak, weighted, value_chunks[step], gathered)
                finish(pair, half, gathered, peak, before)
                return next_running

            def pair_step(pair, running):
                at = 0
                for (_, _, ref, shift), size in zip(set_refs, sizes):
                    value_ref[at : at + size, :] = ref[:, pl.ds(column(pair) + shift, PAIR)]
                    at += size
                if padded > keys:
                    value_ref[keys:, :] = jnp.zeros((padded - keys, PAIR), jnp.bfloat16)
                values_t = value_ref[...].T
                running = overlap(pair, 0, running, values_t, pair, 1)
                later = jnp.minimum(pair + 1, last_pair - 1)
                return overlap(pair, 1, running, values_t, later, 0)

            first_head = head_queries(first_pair, 0)
            running = None
            for chunk in key_chunks:
                running = score(first_pair, 0, first_head, chunk, running)
            lax.fori_loop(first_pair, last_pair, pair_step, running)

        for group in range(groups):
            one_group(
                group * pairs // groups,
                (group + 1) * pairs // groups,
                state_refs[group] if states else None,
            )
        if final:
            out_ref[...] = lax.dot_general(
                attended_ref[...],
                weight_ref[...],
                (((0,), (0,)), ((), ())),
                preferred_element_type=jnp.float32,
            ).astype(jnp.bfloat16)

    if final:
        out_shape = jax.ShapeDtypeStruct((tokens, width), jnp.bfloat16)
    else:
        out_shape = [
            jax.ShapeDtypeStruct((width, tokens), jnp.float32),
            jax.ShapeDtypeStruct((heads, tokens), jnp.float32),
            jax.ShapeDtypeStruct((heads, tokens), jnp.float32),
        ]
    scratch = [
        pltpu.VMEM((2, padded, tokens), jnp.float32),
        pltpu.VMEM((padded, PAIR), jnp.bfloat16),
    ]
    if row_strides is not None:
        scratch.append(pltpu.VMEM((keys, LANES), jnp.float32))
    if final:
        scratch.append(pltpu.VMEM((width, tokens), jnp.bfloat16))
    whole_spec = pl.BlockSpec(memory_space=pltpu.VMEM)

    def part_spec(block):
        if part[1] == 1:
            return whole_spec
        return pl.BlockSpec((block.shape[0], block.shape[1] // part[1]), lambda step: (0, part[0]))

    operands, specs = [queries], [part_spec(queries)]
    for block, whole in zip(sets, joined):
        for array in (block,) if whole else block:
            operands.append(array)
            specs.append(part_spec(array))
    for array in [array for state in states for array in state] + ([out_weight] if final else []):
        operands.append(array)
        specs.append(whole_spec)
    return pl.pallas_call(
        kernel,
        out_shape=out_shape,
        grid=(1,) if part[1] > 1 else (),
        in_specs=specs,
        scratch_shapes=scratch,
        compiler_params=pltpu.CompilerParams(vmem_limit_bytes=VMEM_BYTES),
        cost_estimate=pl.CostEstimate(
            flops=16 * tokens * keys * width // cost,
            bytes_accessed=(4 * keys * width + 4 * tokens * width) // cost,
            transcendentals=tokens * keys * heads // cost,
        ),
    )(*operands)


def local(queries, key_rows, values, out_weight):
    query_rows, own_keys, own_values = queries[0], key_rows[0], values[0]
    tokens = query_rows.shape[0]
    inner_bits = lax.axis_size("inner").bit_length() - 1
    outer_bits = lax.axis_size("outer").bit_length() - 1
    strides = [1 << (bit + 1) for bit in range(inner_bits + 1)] + [GSTEP]
    sends = [tokens >> (bit + 1) for bit in range(inner_bits + 1)]
    n_global = tokens // GSTEP

    rows = np.arange(0, tokens, 2)
    rank = sum((rows % s == 0).astype(np.int64) for s in strides)
    order = rows[np.lexsort((rows, -rank))]
    select = np.zeros((sends[0], tokens), np.float32)
    select[np.arange(sends[0]), order] = 1.0

    def prefix_counts(level, length):
        return sum((order[:length] % s == 0).astype(np.int64) for s in strides[level:])

    first_a, first_b, own_global = order_rows(
        jnp.asarray(select, jnp.bfloat16),
        own_keys,
        own_values,
        [(0, sends[1]), (sends[1], sends[0]), (0, n_global)],
    )

    far = own_global
    came = across(far, "outer", 1) if outer_bits > 1 else None
    near_a = across(first_a, "inner", 0)
    direct = [across(first_a[: sends[bit]], "inner", bit) for bit in range(1, inner_bits)]
    near_b = across(first_b, "inner", 0)
    own_set = [(own_keys, own_values)]
    state_a = attend(query_rows, own_set, row_strides=strides, part=(0, 2), cost=COST)
    for bit in range(1, outer_bits):
        if bit > 1:
            came = across(far, "outer", bit)
        far = jnp.concatenate([far, came], axis=0)
    far = far[n_global:]
    state_b = attend(
        after(query_rows, near_a), own_set, row_strides=strides, part=(1, 2), cost=COST
    )
    far = after(far, state_a[1])
    far = jnp.concatenate([far, across(far, "inner", 0)], axis=0)

    sets, counts = [near_a, near_b], [prefix_counts(0, sends[0])]
    held = [near_a]
    early = None
    for bit in range(1, inner_bits):
        count = sends[bit]
        moved = [block[:count] for block in held]
        moved = moved[0] if len(moved) == 1 else jnp.concatenate(moved, axis=0)
        if bit == 1:
            moved = after(moved, state_a[1])
        came = across(moved, "inner", bit)
        far = after(far, state_b[1])
        far = jnp.concatenate([far, across(far, "inner", bit)], axis=0)
        if early is None:
            counts.append(prefix_counts(bit, count))
            early = attend(
                query_rows,
                sets + [direct[0]],
                np.concatenate(counts),
                states=[state_a, state_b],
                cost=COST,
            )
            sets, counts = [came], [prefix_counts(bit, count)] * len(held)
        else:
            sets += [direct[bit - 1], came]
            counts += [prefix_counts(bit, count)] * (1 + len(held))
        held = held + [direct[bit - 1]]
        held += [came[at : at + count] for at in range(0, came.shape[0], count)]
    count = sends[inner_bits]
    moved = jnp.concatenate([block[:count] for block in [first_a] + held] + [far], axis=0)
    if early is not None:
        moved = after(moved, early[1])
    came = across(moved, "outer", 0)
    sets += [came, far]
    counts += [prefix_counts(inner_bits, count)] * (1 + len(held))
    counts.append(np.ones(2 * far.shape[0], np.int64))
    states = [early] if early is not None else [state_a, state_b]
    result = attend(
        query_rows, sets, np.concatenate(counts), states=states, out_weight=out_weight
    )
    return result[None]


def solution(mesh):
    placed = (P("outer", "inner", None), P("outer", "inner", None), P("outer", "inner", None), P())
    return jax.shard_map(
        local, mesh=mesh, in_specs=placed, out_specs=P("outer", "inner", None), check_vma=False
    )
```

```python
import math

import jax
import jax.numpy as jnp
import numpy as np
from jax import lax
from jax.experimental import pallas as pl
from jax.experimental.pallas import tpu as pltpu
from jax.sharding import PartitionSpec as P

HEAD_DIM = 64
GSTEP = 64
PAIR = 2 * HEAD_DIM
CHUNK = 256
LANES = 128
LOG2E = math.log2(math.e)
VMEM_BYTES = 16 * 1024 * 1024
JOIN_VMEM_BYTES = 8 * 1024 * 1024
FETCH_VMEM_BYTES = 60 * 1024 * 1024


def across(block, axis, flip):
    return lax.ppermute(block, axis, [(i, i ^ flip) for i in range(lax.axis_size(axis))])


def after(block, *others):
    return lax.optimization_barrier((block, *others))[0]


def join_after(pieces, other):
    width = pieces[0][0].shape[1]
    total = sum(high - low for _, low, high in pieces)

    def kernel(*refs):
        out_ref, at = refs[-1], 0
        for ref, (_, low, high) in zip(refs, pieces):
            out_ref[at : at + high - low, :] = ref[low:high, :]
            at += high - low

    return pl.pallas_call(
        kernel,
        out_shape=jax.ShapeDtypeStruct((total, width), pieces[0][0].dtype),
        in_specs=[pl.BlockSpec(memory_space=pltpu.VMEM)] * len(pieces)
        + [pl.BlockSpec(memory_space=pl.ANY)],
        compiler_params=pltpu.CompilerParams(vmem_limit_bytes=JOIN_VMEM_BYTES),
        cost_estimate=pl.CostEstimate(
            flops=0, bytes_accessed=4 * total * width, transcendentals=0
        ),
    )(*[block for block, _, _ in pieces], other)


def runs(counts):
    found = []
    for at, value in enumerate(counts):
        if found and found[-1][2] == value:
            found[-1][1] = at + 1
        else:
            found.append([at, at + 1, int(value)])
    return [tuple(entry) for entry in found]


def order_rows(select, key_rows, values, prefixes):
    tokens, width = key_rows.shape

    def kernel(select_hbm, key_hbm, value_hbm, *refs):
        out_refs, (select_ref, row_ref, sems) = refs[: len(prefixes)], refs[len(prefixes) :]
        copies = [
            pltpu.make_async_copy(select_hbm, select_ref, sems.at[0]),
            pltpu.make_async_copy(key_hbm, row_ref.at[0], sems.at[1]),
            pltpu.make_async_copy(value_hbm, row_ref.at[1], sems.at[2]),
        ]
        for copy in copies:
            copy.start()
        copies[0].wait()
        for half in range(2):
            copies[1 + half].wait()
            moved = jnp.dot(
                select_ref[...], row_ref[half], preferred_element_type=jnp.float32
            ).astype(jnp.bfloat16)
            for (low, high), out_ref in zip(prefixes, out_refs):
                out_ref[:, half * width : (half + 1) * width] = moved[low:high]

    return pl.pallas_call(
        kernel,
        out_shape=[
            jax.ShapeDtypeStruct((high - low, 2 * width), jnp.bfloat16) for low, high in prefixes
        ],
        in_specs=[pl.BlockSpec(memory_space=pltpu.HBM)] * 3,
        scratch_shapes=[
            pltpu.VMEM(select.shape, jnp.bfloat16),
            pltpu.VMEM((2, tokens, width), jnp.bfloat16),
            pltpu.SemaphoreType.DMA((3,)),
        ],
        compiler_params=pltpu.CompilerParams(vmem_limit_bytes=FETCH_VMEM_BYTES),
        cost_estimate=pl.CostEstimate(
            flops=4 * select.size * width, bytes_accessed=6 * tokens * width, transcendentals=0
        ),
    )(select, key_rows, values)


def attend(queries, sets, counts=None, row_strides=None, part=(0, 1), states=(), out_weight=None, wait=None):
    tokens = queries.shape[0]
    width = queries.shape[1] // part[1]
    heads, pairs = width // HEAD_DIM, width // PAIR
    joined = [not isinstance(block, tuple) for block in sets]
    sizes = [(block if whole else block[0]).shape[0] for block, whole in zip(sets, joined)]
    keys = sum(sizes)
    padded = -(-keys // LANES) * LANES
    row_runs = [(0, keys, 1)] if counts is None else runs(counts)
    scale = HEAD_DIM**-0.5 * LOG2E
    final = out_weight is not None
    groups = max(len(states), 1)

    def kernel(*refs):
        refs = list(refs)
        query_ref = refs.pop(0)
        set_refs = []
        for whole in joined:
            ref = refs.pop(0)
            set_refs.append((ref, 0, ref, width) if whole else (ref, 0, refs.pop(0), 0))
        state_refs = [[refs.pop(0) for _ in range(3)] for _ in states]
        if wait is not None:
            refs.pop(1 if final else 0)
        if final:
            weight_ref, out_ref, attended_ref = refs.pop(0), refs.pop(0), refs.pop(-1)
        else:
            numer_out, peak_out, total_out = [refs.pop(0) for _ in range(3)]
        score_ref, value_ref = refs.pop(0), refs.pop(0)
        if row_strides is not None:
            offset_ref = refs.pop(0)
            row = lax.broadcasted_iota(jnp.int32, (keys, LANES), 0)
            rank = sum((row & (s - 1) == 0).astype(jnp.int32) for s in row_strides)
            offsets = jnp.zeros((keys, LANES), jnp.float32)
            for times in range(1, len(row_strides) + 1):
                offsets = jnp.where(rank == times, math.log2(1 + times), offsets)
            offset_ref[...] = offsets

        ones = jnp.ones((16, padded), jnp.bfloat16)
        key_chunks = []
        at = 0
        for entry, size in zip(set_refs, sizes):
            for low in range(0, size, CHUNK):
                count = min(CHUNK, size - low)
                key_chunks.append((entry[0], low, count, at))
                at += count
        value_chunks = [(low, min(CHUNK, padded - low)) for low in range(0, padded, CHUNK)]

        def column(pair):
            return pl.multiple_of(pair * PAIR, PAIR)

        def head_queries(pair, half):
            turned = query_ref[:, pl.ds(column(pair), PAIR)].T
            row = lax.broadcasted_iota(jnp.int32, turned.shape, 0)
            own = (row < HEAD_DIM) if half == 0 else (row >= HEAD_DIM)
            return jnp.where(own, turned, jnp.zeros_like(turned))

        def score(pair, half, query_head, chunk, running):
            ref, low, count, at = chunk
            scores = jnp.dot(
                ref[low : low + count, pl.ds(column(pair), PAIR)],
                query_head,
                preferred_element_type=jnp.float32,
            )
            score_ref[half, at : at + count, :] = scores
            tallest = jnp.max(scores.reshape(count // 8, 8, tokens), axis=0)
            return tallest if running is None else jnp.maximum(running, tallest)

        def weigh(half, peak, weighted, chunk, gathered):
            low, size = chunk
            high = min(low + size, keys)
            pieces = []
            for first, last, times in row_runs:
                first, last = max(first, low), min(last, high)
                if first < last:
                    offset = peak - math.log2(times)
                    power = score_ref[half, first:last, :] * scale - offset
                    if row_strides is not None:
                        extra = offset_ref[first:last, :]
                        power = power + jnp.concatenate([extra] * (tokens // LANES), axis=1)
                    pieces.append(jnp.exp2(power))
            if low + size > keys:
                pieces.append(jnp.zeros((low + size - keys, tokens), jnp.float32))
            probs = (pieces[0] if len(pieces) == 1 else jnp.concatenate(pieces, axis=0)).astype(
                jnp.bfloat16
            )
            product = jnp.dot(
                weighted[:, low : low + size], probs, preferred_element_type=jnp.float32
            )
            return product if gathered is None else gathered + product

        def one_group(first_pair, last_pair, earlier):
            def local_rows(pair, half):
                start = (pair - first_pair) * PAIR + half * HEAD_DIM
                return pl.ds(pl.multiple_of(start, HEAD_DIM), HEAD_DIM)

            def local_head(pair, half):
                return pl.ds(2 * (pair - first_pair) + half, 1)

            def finish(pair, half, gathered, peak, before):
                numer, total = gathered[:HEAD_DIM], gathered[HEAD_DIM : HEAD_DIM + 1]
                if earlier is not None:
                    factor = jnp.exp2(before - peak)
                    numer = numer + factor * earlier[0][local_rows(pair, half), :]
                    total = total + factor * earlier[2][local_head(pair, half), :]
                start = pl.multiple_of(column(pair) + half * HEAD_DIM, HEAD_DIM)
                rows = pl.ds(start, HEAD_DIM)
                if final:
                    attended_ref[rows, :] = (numer / total).astype(jnp.bfloat16)
                else:
                    head = pl.ds(2 * pair + half, 1)
                    numer_out[rows, :] = numer
                    peak_out[head, :] = peak
                    total_out[head, :] = total

            def overlap(pair, half, running, values_t, next_pair, next_half):
                peak = jnp.max(running, axis=0, keepdims=True) * scale
                before = None
                if earlier is not None:
                    before = earlier[1][local_head(pair, half), :]
                    peak = jnp.maximum(peak, before)
                weighted = jnp.concatenate(
                    [values_t[half * HEAD_DIM : (half + 1) * HEAD_DIM], ones], axis=0
                )
                query_head = head_queries(next_pair, next_half)
                next_running, gathered = None, None
                for step in range(max(len(key_chunks), len(value_chunks))):
                    if step < len(key_chunks):
                        next_running = score(
                            next_pair, next_half, query_head, key_chunks[step], next_running
                        )
                    if step < len(value_chunks):
                        gathered = weigh(half, peak, weighted, value_chunks[step], gathered)
                finish(pair, half, gathered, peak, before)
                return next_running

            def pair_step(pair, running):
                at = 0
                for (_, _, ref, shift), size in zip(set_refs, sizes):
                    value_ref[at : at + size, :] = ref[:, pl.ds(column(pair) + shift, PAIR)]
                    at += size
                if padded > keys:
                    value_ref[keys:, :] = jnp.zeros((padded - keys, PAIR), jnp.bfloat16)
                values_t = value_ref[...].T
                running = overlap(pair, 0, running, values_t, pair, 1)
                later = jnp.minimum(pair + 1, last_pair - 1)
                return overlap(pair, 1, running, values_t, later, 0)

            first_head = head_queries(first_pair, 0)
            running = None
            for chunk in key_chunks:
                running = score(first_pair, 0, first_head, chunk, running)
            lax.fori_loop(first_pair, last_pair, pair_step, running)

        for group in range(groups):
            one_group(
                group * pairs // groups,
                (group + 1) * pairs // groups,
                state_refs[group] if states else None,
            )
        if final:
            out_ref[...] = lax.dot_general(
                attended_ref[...],
                weight_ref[...],
                (((0,), (0,)), ((), ())),
                preferred_element_type=jnp.float32,
            ).astype(jnp.bfloat16)

    if final:
        out_shape = jax.ShapeDtypeStruct((tokens, width), jnp.bfloat16)
    else:
        out_shape = [
            jax.ShapeDtypeStruct((width, tokens), jnp.float32),
            jax.ShapeDtypeStruct((heads, tokens), jnp.float32),
            jax.ShapeDtypeStruct((heads, tokens), jnp.float32),
        ]
    scratch = [
        pltpu.VMEM((2, padded, tokens), jnp.float32),
        pltpu.VMEM((padded, PAIR), jnp.bfloat16),
    ]
    if row_strides is not None:
        scratch.append(pltpu.VMEM((keys, LANES), jnp.float32))
    if final:
        scratch.append(pltpu.VMEM((width, tokens), jnp.bfloat16))
    operands = [queries]
    for block, whole in zip(sets, joined):
        operands += [block] if whole else list(block)
    whole_spec = pl.BlockSpec(memory_space=pltpu.VMEM)
    specs = [whole_spec] * len(operands)
    if part[1] > 1:
        specs = [
            pl.BlockSpec((array.shape[0], array.shape[1] // part[1]), lambda step: (0, part[0]))
            for array in operands
        ]
    for array in [array for state in states for array in state] + ([out_weight] if final else []):
        operands.append(array)
        specs.append(whole_spec)
    if wait is not None:
        operands.append(wait)
        specs.append(pl.BlockSpec(memory_space=pl.ANY))
    return pl.pallas_call(
        kernel,
        out_shape=out_shape,
        grid=(1,) if part[1] > 1 else (),
        in_specs=specs,
        scratch_shapes=scratch,
        compiler_params=pltpu.CompilerParams(
            vmem_limit_bytes=VMEM_BYTES
        ),
        cost_estimate=pl.CostEstimate(
            flops=16 * tokens * keys * width,
            bytes_accessed=(4 * keys * width + 4 * tokens * width),
            transcendentals=tokens * keys * heads,
        ),
    )(*operands)


def local(queries, key_rows, values, out_weight):
    query_rows, own_keys, own_values = queries[0], key_rows[0], values[0]
    tokens = query_rows.shape[0]
    n_inner, n_outer = lax.axis_size("inner"), lax.axis_size("outer")
    inner_bits = n_inner.bit_length() - 1
    strides = [1 << (bit + 1) for bit in range(inner_bits + 1)]
    sends = [tokens >> (bit + 1) for bit in range(inner_bits + 1)]
    n_global = tokens // GSTEP

    rows = np.arange(0, tokens, 2)
    rank = sum((rows % s == 0).astype(np.int64) for s in strides + [GSTEP])
    order = rows[np.lexsort((rows, -rank))]
    select = np.zeros((sends[0], tokens), np.float32)
    select[np.arange(sends[0]), order] = 1.0

    def prefix_counts(level, low, high):
        return sum((order[low:high] % s == 0).astype(np.int64) for s in strides[level:])

    first_a, first_b, far = order_rows(
        jnp.asarray(select, jnp.bfloat16),
        own_keys,
        own_values,
        [(0, sends[1]), (sends[1], sends[0]), (0, n_global)],
    )

    held = {0: (first_a, 0)}
    for bit in range(1, inner_bits):
        held[1 << bit] = (across(first_a[: sends[bit]], "inner", 1 << bit), 0)
    held[1] = (across(first_a, "inner", 1), 0)
    flip = 2
    while flip < n_outer:
        far = jnp.concatenate([far, across(far, "outer", flip)], axis=0)
        flip *= 2
    n_far = far.shape[0]
    fars = {0: (far, 0)}

    def first_rows(where, count):
        return (where[0], where[1], where[1] + count)

    pieces = [first_rows((first_b, 0), sends[0] - sends[1]), first_rows(fars[0], n_far)]
    moved = join_after(pieces, far)
    near_b = across(moved, "inner", 1)
    fars[1] = (near_b, sends[0] - sends[1])
    own_set = [(own_keys, own_values)]
    state_a = attend(query_rows, own_set, row_strides=strides, part=(0, 2), wait=moved)
    own_done = state_a[1]

    known = [0] + [1 << bit for bit in range(inner_bits)]
    late = [d for d in range(n_inner) if d not in known]
    last = sends[inner_bits]
    late_sets = [near_b]
    late_counts = [prefix_counts(0, sends[1], sends[0]), np.ones(n_far, np.int64)]
    for bit in range(1, inner_bits):
        count = sends[bit]
        others = range(1, 1 << bit)
        pieces = [first_rows(held[d], count) for d in others] + [first_rows(fars[0], n_far)]
        own_done = join_after(pieces, own_done)
        came = across(own_done, "inner", 1 << bit)
        for at, d in enumerate(others):
            held[d | 1 << bit] = (came, at * count)
        fars[1 << bit] = (came, len(others) * count)
        late_sets.append(came)
        late_counts += [prefix_counts(bit, 0, count)] * len(others) + [np.ones(n_far, np.int64)]
    for d in late:
        fars[d] = (across(far, "inner", d), 0)
        late_sets.append(fars[d][0])
        late_counts.append(np.ones(n_far, np.int64))
    pieces = [first_rows(held[d], last) for d in known]
    moved = join_after(pieces, own_done)
    early_core = across(moved, "outer", 1)
    state_b = attend(query_rows, own_set, row_strides=strides, part=(1, 2), wait=moved)

    early_sets = [held[d][0] for d in known[1:]] + [early_core, far]
    early_counts = [prefix_counts(0, 0, sends[1])]
    early_counts += [prefix_counts(bit, 0, sends[bit]) for bit in range(1, inner_bits)]
    early_counts.append(np.ones(early_core.shape[0] + n_far, np.int64))
    state = attend(query_rows, early_sets, np.concatenate(early_counts), states=[state_a, state_b])

    pieces = [first_rows(held[d], last) for d in late]
    pieces += [first_rows(fars[d], n_far) for d in range(n_inner)]
    late_core = across(join_after(pieces, state[1]), "outer", 1)
    state = attend(query_rows, late_sets, np.concatenate(late_counts), states=[state])
    result = attend(query_rows, [late_core], states=[state], out_weight=out_weight)
    return result[None]


def solution(mesh):
    placed = (P("outer", "inner", None), P("outer", "inner", None), P("outer", "inner", None), P())
    return jax.shard_map(
        local, mesh=mesh, in_specs=placed, out_specs=P("outer", "inner", None), check_vma=False
    )
```

```python
import math

import jax
import jax.numpy as jnp
import numpy as np
from jax import lax
from jax.experimental import pallas as pl
from jax.experimental.pallas import tpu as pltpu
from jax.sharding import PartitionSpec as P

HEAD_DIM = 64
GSTEP = 64
PAIR = 2 * HEAD_DIM
CHUNK = 256
LANES = 128
LOG2E = math.log2(math.e)
VMEM_BYTES = 16 * 1024 * 1024
JOIN_VMEM_BYTES = 8 * 1024 * 1024
FETCH_VMEM_BYTES = 60 * 1024 * 1024


def across(block, axis, flip):
    return lax.ppermute(block, axis, [(i, i ^ flip) for i in range(lax.axis_size(axis))])


def after(block, *others):
    return lax.optimization_barrier((block, *others))[0]


def join_after(pieces, other):
    width = pieces[0][0].shape[1]
    total = sum(high - low for _, low, high in pieces)

    def kernel(*refs):
        out_ref, at = refs[-1], 0
        for ref, (_, low, high) in zip(refs, pieces):
            out_ref[at : at + high - low, :] = ref[low:high, :]
            at += high - low

    return pl.pallas_call(
        kernel,
        out_shape=jax.ShapeDtypeStruct((total, width), pieces[0][0].dtype),
        in_specs=[pl.BlockSpec(memory_space=pltpu.VMEM)] * len(pieces)
        + [pl.BlockSpec(memory_space=pl.ANY)],
        compiler_params=pltpu.CompilerParams(vmem_limit_bytes=JOIN_VMEM_BYTES),
        cost_estimate=pl.CostEstimate(
            flops=0, bytes_accessed=4 * total * width, transcendentals=0
        ),
    )(*[block for block, _, _ in pieces], other)


def runs(counts):
    found = []
    for at, value in enumerate(counts):
        if found and found[-1][2] == value:
            found[-1][1] = at + 1
        else:
            found.append([at, at + 1, int(value)])
    return [tuple(entry) for entry in found]


def order_rows(select, key_rows, values, prefixes):
    tokens, width = key_rows.shape

    pieces = [
        (half, low, min(CHUNK, width - low)) for half in range(2) for low in range(0, width, CHUNK)
    ]

    def kernel(select_hbm, key_hbm, value_hbm, *refs):
        out_refs, (select_ref, row_ref, sems) = refs[: len(prefixes)], refs[len(prefixes) :]
        copies = [pltpu.make_async_copy(select_hbm, select_ref, sems.at[0])]
        for at, (half, low, size) in enumerate(pieces):
            source = (key_hbm, value_hbm)[half].at[:, low : low + size]
            target = row_ref.at[half, :, low : low + size]
            copies.append(pltpu.make_async_copy(source, target, sems.at[1 + at]))
        for copy in copies:
            copy.start()
        copies[0].wait()
        for copy, (half, low, size) in zip(copies[1:], pieces):
            copy.wait()
            moved = jnp.dot(
                select_ref[...],
                row_ref[half, :, low : low + size],
                preferred_element_type=jnp.float32,
            ).astype(jnp.bfloat16)
            cols = slice(half * width + low, half * width + low + size)
            for (first, last), out_ref in zip(prefixes, out_refs):
                out_ref[:, cols] = moved[first:last]

    return pl.pallas_call(
        kernel,
        out_shape=[
            jax.ShapeDtypeStruct((high - low, 2 * width), jnp.bfloat16) for low, high in prefixes
        ],
        in_specs=[pl.BlockSpec(memory_space=pltpu.HBM)] * 3,
        scratch_shapes=[
            pltpu.VMEM(select.shape, jnp.bfloat16),
            pltpu.VMEM((2, tokens, width), jnp.bfloat16),
            pltpu.SemaphoreType.DMA((1 + len(pieces),)),
        ],
        compiler_params=pltpu.CompilerParams(vmem_limit_bytes=FETCH_VMEM_BYTES),
        cost_estimate=pl.CostEstimate(
            flops=4 * select.size * width, bytes_accessed=6 * tokens * width, transcendentals=0
        ),
    )(select, key_rows, values)


def attend(queries, sets, counts=None, row_strides=None, part=(0, 1), states=(), out_weight=None, wait=None):
    tokens = queries.shape[0]
    width = queries.shape[1] // part[1]
    heads, pairs = width // HEAD_DIM, width // PAIR
    joined = [not isinstance(block, tuple) for block in sets]
    sizes = [(block if whole else block[0]).shape[0] for block, whole in zip(sets, joined)]
    keys = sum(sizes)
    padded = -(-keys // LANES) * LANES
    row_runs = [(0, keys, 1)] if counts is None else runs(counts)
    scale = HEAD_DIM**-0.5 * LOG2E
    final = out_weight is not None
    groups = max(len(states), 1)

    def kernel(*refs):
        refs = list(refs)
        query_ref = refs.pop(0)
        set_refs = []
        for whole in joined:
            ref = refs.pop(0)
            set_refs.append((ref, 0, ref, width) if whole else (ref, 0, refs.pop(0), 0))
        state_refs = [[refs.pop(0) for _ in range(3)] for _ in states]
        if wait is not None:
            refs.pop(1 if final else 0)
        if final:
            weight_ref, out_ref, attended_ref = refs.pop(0), refs.pop(0), refs.pop(-1)
        else:
            numer_out, peak_out, total_out = [refs.pop(0) for _ in range(3)]
        score_ref, value_ref = refs.pop(0), refs.pop(0)
        if row_strides is not None:
            offset_ref = refs.pop(0)
            row = lax.broadcasted_iota(jnp.int32, (keys, LANES), 0)
            rank = sum((row & (s - 1) == 0).astype(jnp.int32) for s in row_strides)
            offsets = jnp.zeros((keys, LANES), jnp.float32)
            for times in range(1, len(row_strides) + 1):
                offsets = jnp.where(rank == times, math.log2(1 + times), offsets)
            offset_ref[...] = offsets

        ones = jnp.ones((16, padded), jnp.bfloat16)
        key_chunks = []
        at = 0
        for entry, size in zip(set_refs, sizes):
            for low in range(0, size, CHUNK):
                count = min(CHUNK, size - low)
                key_chunks.append((entry[0], low, count, at))
                at += count
        value_chunks = [(low, min(CHUNK, padded - low)) for low in range(0, padded, CHUNK)]

        def column(pair):
            return pl.multiple_of(pair * PAIR, PAIR)

        def head_queries(pair, half):
            turned = query_ref[:, pl.ds(column(pair), PAIR)].T
            row = lax.broadcasted_iota(jnp.int32, turned.shape, 0)
            own = (row < HEAD_DIM) if half == 0 else (row >= HEAD_DIM)
            return jnp.where(own, turned, jnp.zeros_like(turned))

        def score(pair, half, query_head, chunk, running):
            ref, low, count, at = chunk
            scores = jnp.dot(
                ref[low : low + count, pl.ds(column(pair), PAIR)],
                query_head,
                preferred_element_type=jnp.float32,
            )
            score_ref[half, at : at + count, :] = scores
            tallest = jnp.max(scores.reshape(count // 8, 8, tokens), axis=0)
            return tallest if running is None else jnp.maximum(running, tallest)

        def weigh(half, peak, weighted, chunk, gathered):
            low, size = chunk
            high = min(low + size, keys)
            pieces = []
            for first, last, times in row_runs:
                first, last = max(first, low), min(last, high)
                if first < last:
                    offset = peak - math.log2(times)
                    power = score_ref[half, first:last, :] * scale - offset
                    if row_strides is not None:
                        extra = offset_ref[first:last, :]
                        power = power + jnp.concatenate([extra] * (tokens // LANES), axis=1)
                    pieces.append(jnp.exp2(power))
            if low + size > keys:
                pieces.append(jnp.zeros((low + size - keys, tokens), jnp.float32))
            probs = (pieces[0] if len(pieces) == 1 else jnp.concatenate(pieces, axis=0)).astype(
                jnp.bfloat16
            )
            product = jnp.dot(
                weighted[:, low : low + size], probs, preferred_element_type=jnp.float32
            )
            return product if gathered is None else gathered + product

        def one_group(first_pair, last_pair, earlier):
            def local_rows(pair, half):
                start = (pair - first_pair) * PAIR + half * HEAD_DIM
                return pl.ds(pl.multiple_of(start, HEAD_DIM), HEAD_DIM)

            def local_head(pair, half):
                return pl.ds(2 * (pair - first_pair) + half, 1)

            def finish(pair, half, gathered, peak, before):
                numer, total = gathered[:HEAD_DIM], gathered[HEAD_DIM : HEAD_DIM + 1]
                if earlier is not None:
                    factor = jnp.exp2(before - peak)
                    numer = numer + factor * earlier[0][local_rows(pair, half), :]
                    total = total + factor * earlier[2][local_head(pair, half), :]
                start = pl.multiple_of(column(pair) + half * HEAD_DIM, HEAD_DIM)
                rows = pl.ds(start, HEAD_DIM)
                if final:
                    attended_ref[half] = (numer / total).astype(jnp.bfloat16)
                    if half == 1:
                        both = attended_ref[...].reshape(PAIR, tokens)
                        out_ref[:, pl.ds(column(pair), PAIR)] = both.T
                else:
                    head = pl.ds(2 * pair + half, 1)
                    numer_out[rows, :] = numer
                    peak_out[head, :] = peak
                    total_out[head, :] = total

            def overlap(pair, half, running, values_t, next_pair, next_half):
                peak = jnp.max(running, axis=0, keepdims=True) * scale
                before = None
                if earlier is not None:
                    before = earlier[1][local_head(pair, half), :]
                    peak = jnp.maximum(peak, before)
                weighted = jnp.concatenate(
                    [values_t[half * HEAD_DIM : (half + 1) * HEAD_DIM], ones], axis=0
                )
                query_head = head_queries(next_pair, next_half)
                next_running, gathered = None, None
                for step in range(max(len(key_chunks), len(value_chunks))):
                    if step < len(key_chunks):
                        next_running = score(
                            next_pair, next_half, query_head, key_chunks[step], next_running
                        )
                    if step < len(value_chunks):
                        gathered = weigh(half, peak, weighted, value_chunks[step], gathered)
                finish(pair, half, gathered, peak, before)
                return next_running

            def pair_step(pair, running):
                at = 0
                for (_, _, ref, shift), size in zip(set_refs, sizes):
                    value_ref[at : at + size, :] = ref[:, pl.ds(column(pair) + shift, PAIR)]
                    at += size
                if padded > keys:
                    value_ref[keys:, :] = jnp.zeros((padded - keys, PAIR), jnp.bfloat16)
                values_t = value_ref[...].T
                running = overlap(pair, 0, running, values_t, pair, 1)
                later = jnp.minimum(pair + 1, last_pair - 1)
                return overlap(pair, 1, running, values_t, later, 0)

            first_head = head_queries(first_pair, 0)
            running = None
            for chunk in key_chunks:
                running = score(first_pair, 0, first_head, chunk, running)
            lax.fori_loop(first_pair, last_pair, pair_step, running)

        for group in range(groups):
            one_group(
                group * pairs // groups,
                (group + 1) * pairs // groups,
                state_refs[group] if states else None,
            )
        if final:
            out_ref[...] = jnp.dot(
                out_ref[...], weight_ref[...], preferred_element_type=jnp.float32
            ).astype(jnp.bfloat16)

    if final:
        out_shape = jax.ShapeDtypeStruct((tokens, width), jnp.bfloat16)
    else:
        out_shape = [
            jax.ShapeDtypeStruct((width, tokens), jnp.float32),
            jax.ShapeDtypeStruct((heads, tokens), jnp.float32),
            jax.ShapeDtypeStruct((heads, tokens), jnp.float32),
        ]
    scratch = [
        pltpu.VMEM((2, padded, tokens), jnp.float32),
        pltpu.VMEM((padded, PAIR), jnp.bfloat16),
    ]
    if row_strides is not None:
        scratch.append(pltpu.VMEM((keys, LANES), jnp.float32))
    if final:
        scratch.append(pltpu.VMEM((2, HEAD_DIM, tokens), jnp.bfloat16))
    operands = [queries]
    for block, whole in zip(sets, joined):
        operands += [block] if whole else list(block)
    whole_spec = pl.BlockSpec(memory_space=pltpu.VMEM)
    specs = [whole_spec] * len(operands)
    if part[1] > 1:
        specs = [
            pl.BlockSpec((array.shape[0], array.shape[1] // part[1]), lambda step: (0, part[0]))
            for array in operands
        ]
    for array in [array for state in states for array in state] + ([out_weight] if final else []):
        operands.append(array)
        specs.append(whole_spec)
    if wait is not None:
        operands.append(wait)
        specs.append(pl.BlockSpec(memory_space=pl.ANY))
    return pl.pallas_call(
        kernel,
        out_shape=out_shape,
        grid=(1,) if part[1] > 1 else (),
        in_specs=specs,
        scratch_shapes=scratch,
        compiler_params=pltpu.CompilerParams(
            vmem_limit_bytes=VMEM_BYTES
        ),
        cost_estimate=pl.CostEstimate(
            flops=16 * tokens * keys * width,
            bytes_accessed=(4 * keys * width + 4 * tokens * width),
            transcendentals=tokens * keys * heads,
        ),
    )(*operands)


def local(queries, key_rows, values, out_weight):
    query_rows, own_keys, own_values = queries[0], key_rows[0], values[0]
    tokens = query_rows.shape[0]
    n_inner, n_outer = lax.axis_size("inner"), lax.axis_size("outer")
    inner_bits = n_inner.bit_length() - 1
    strides = [1 << (bit + 1) for bit in range(inner_bits + 1)]
    sends = [tokens >> (bit + 1) for bit in range(inner_bits + 1)]
    n_global = tokens // GSTEP

    rows = np.arange(0, tokens, 2)
    rank = sum((rows % s == 0).astype(np.int64) for s in strides + [GSTEP])
    order = rows[np.lexsort((rows, -rank))]
    select = np.zeros((sends[0], tokens), np.float32)
    select[np.arange(sends[0]), order] = 1.0

    def prefix_counts(level, low, high):
        return sum((order[low:high] % s == 0).astype(np.int64) for s in strides[level:])

    first_a, first_b, far = order_rows(
        jnp.asarray(select, jnp.bfloat16),
        own_keys,
        own_values,
        [(0, sends[1]), (sends[1], sends[0]), (0, n_global)],
    )

    held = {0: (first_a, 0)}
    for bit in range(1, inner_bits):
        held[1 << bit] = (across(first_a[: sends[bit]], "inner", 1 << bit), 0)
    held[1] = (across(first_a, "inner", 1), 0)
    own_set = [(own_keys, own_values)]
    own_states, moved, flip = [], far, 2
    while flip < n_outer or len(own_states) < 2:
        if flip < n_outer:
            came = across(moved, "outer", flip)
            flip *= 2
        if len(own_states) < 2:
            own_states.append(
                attend(
                    query_rows,
                    own_set,
                    row_strides=strides,
                    part=(len(own_states), 2),
                    wait=moved,
                )
            )
        moved = join_after([(moved, 0, moved.shape[0]), (came, 0, came.shape[0])], own_states[-1][1])
    far = moved
    n_far = far.shape[0]
    fars = {0: (far, 0)}

    def first_rows(where, count):
        return (where[0], where[1], where[1] + count)

    near_b = across(
        join_after([(first_b, 0, sends[0] - sends[1]), (far, 0, n_far)], far), "inner", 1
    )
    fars[1] = (near_b, sends[0] - sends[1])
    own_done = far

    known = [0] + [1 << bit for bit in range(inner_bits)]
    late = [d for d in range(n_inner) if d not in known]
    last = sends[inner_bits]
    late_sets = [near_b]
    late_counts = [prefix_counts(0, sends[1], sends[0]), np.ones(n_far, np.int64)]
    for bit in range(1, inner_bits):
        count = sends[bit]
        others = range(1, 1 << bit)
        pieces = [first_rows(held[d], count) for d in others] + [first_rows(fars[0], n_far)]
        own_done = join_after(pieces, own_done)
        came = across(own_done, "inner", 1 << bit)
        for at, d in enumerate(others):
            held[d | 1 << bit] = (came, at * count)
        fars[1 << bit] = (came, len(others) * count)
        late_sets.append(came)
        late_counts += [prefix_counts(bit, 0, count)] * len(others) + [np.ones(n_far, np.int64)]
    for d in late:
        fars[d] = (across(far, "inner", d), 0)
        late_sets.append(fars[d][0])
        late_counts.append(np.ones(n_far, np.int64))
    pieces = [first_rows(held[d], last) for d in known]
    moved = join_after(pieces, own_done)
    early_core = across(moved, "outer", 1)

    early_sets = [held[d][0] for d in known[1:]] + [early_core, far]
    early_counts = [prefix_counts(0, 0, sends[1])]
    early_counts += [prefix_counts(bit, 0, sends[bit]) for bit in range(1, inner_bits)]
    early_counts.append(np.ones(early_core.shape[0] + n_far, np.int64))
    state = attend(query_rows, early_sets, np.concatenate(early_counts), states=own_states)

    pieces = [first_rows(held[d], last) for d in late]
    pieces += [first_rows(fars[d], n_far) for d in range(n_inner)]
    late_core = across(join_after(pieces, state[1]), "outer", 1)
    state = attend(query_rows, late_sets, np.concatenate(late_counts), states=[state])
    result = attend(query_rows, [late_core], states=[state], out_weight=out_weight)
    return result[None]


def solution(mesh):
    placed = (P("outer", "inner", None), P("outer", "inner", None), P("outer", "inner", None), P())
    return jax.shard_map(
        local, mesh=mesh, in_specs=placed, out_specs=P("outer", "inner", None), check_vma=False
    )
```

```python
import math

import jax
import jax.numpy as jnp
import numpy as np
from jax import lax
from jax.experimental import pallas as pl
from jax.experimental.pallas import tpu as pltpu
from jax.sharding import PartitionSpec as P

HEAD_DIM = 64
GSTEP = 64
PAIR = 2 * HEAD_DIM
CHUNK = 256
KEY_CHUNK = 512
LANES = 128
LOG2E = math.log2(math.e)
VMEM_BYTES = 16 * 1024 * 1024
JOIN_VMEM_BYTES = 8 * 1024 * 1024
FETCH_VMEM_BYTES = 60 * 1024 * 1024


def across(block, axis, flip):
    return lax.ppermute(block, axis, [(i, i ^ flip) for i in range(lax.axis_size(axis))])


def after(block, *others):
    return lax.optimization_barrier((block, *others))[0]


def join_after(pieces, other):
    width = pieces[0][0].shape[1]
    total = sum(high - low for _, low, high in pieces)

    def kernel(*refs):
        out_ref, at = refs[-1], 0
        for ref, (_, low, high) in zip(refs, pieces):
            out_ref[at : at + high - low, :] = ref[low:high, :]
            at += high - low

    return pl.pallas_call(
        kernel,
        out_shape=jax.ShapeDtypeStruct((total, width), pieces[0][0].dtype),
        in_specs=[pl.BlockSpec(memory_space=pltpu.VMEM)] * len(pieces)
        + [pl.BlockSpec(memory_space=pl.ANY)],
        compiler_params=pltpu.CompilerParams(vmem_limit_bytes=JOIN_VMEM_BYTES),
        cost_estimate=pl.CostEstimate(
            flops=0, bytes_accessed=4 * total * width, transcendentals=0
        ),
    )(*[block for block, _, _ in pieces], other)


def runs(counts):
    found = []
    for at, value in enumerate(counts):
        if found and found[-1][2] == value:
            found[-1][1] = at + 1
        else:
            found.append([at, at + 1, int(value)])
    return [tuple(entry) for entry in found]


def order_rows(select, key_rows, values, prefixes):
    tokens, width = key_rows.shape

    def kernel(select_hbm, key_hbm, value_hbm, *refs):
        out_refs, (select_ref, row_ref, sems) = refs[: len(prefixes)], refs[len(prefixes) :]
        copies = [
            pltpu.make_async_copy(select_hbm, select_ref, sems.at[0]),
            pltpu.make_async_copy(key_hbm, row_ref.at[0], sems.at[1]),
            pltpu.make_async_copy(value_hbm, row_ref.at[1], sems.at[2]),
        ]
        for copy in copies:
            copy.start()
        copies[0].wait()
        for half in range(2):
            copies[1 + half].wait()
            moved = jnp.dot(
                select_ref[...], row_ref[half], preferred_element_type=jnp.float32
            ).astype(jnp.bfloat16)
            for (low, high), out_ref in zip(prefixes, out_refs):
                out_ref[:, half * width : (half + 1) * width] = moved[low:high]

    return pl.pallas_call(
        kernel,
        out_shape=[
            jax.ShapeDtypeStruct((high - low, 2 * width), jnp.bfloat16) for low, high in prefixes
        ],
        in_specs=[pl.BlockSpec(memory_space=pltpu.HBM)] * 3,
        scratch_shapes=[
            pltpu.VMEM(select.shape, jnp.bfloat16),
            pltpu.VMEM((2, tokens, width), jnp.bfloat16),
            pltpu.SemaphoreType.DMA((3,)),
        ],
        compiler_params=pltpu.CompilerParams(vmem_limit_bytes=FETCH_VMEM_BYTES),
        cost_estimate=pl.CostEstimate(
            flops=4 * select.size * width, bytes_accessed=6 * tokens * width, transcendentals=0
        ),
    )(select, key_rows, values)


def attend(queries, sets, counts=None, row_strides=None, part=(0, 1), states=(), out_weight=None, wait=None):
    tokens = queries.shape[0]
    width = queries.shape[1] // part[1]
    heads, pairs = width // HEAD_DIM, width // PAIR
    joined = [not isinstance(block, tuple) for block in sets]
    sizes = [(block if whole else block[0]).shape[0] for block, whole in zip(sets, joined)]
    keys = sum(sizes)
    padded = -(-keys // LANES) * LANES
    row_runs = [(0, keys, 1)] if counts is None else runs(counts)
    scale = HEAD_DIM**-0.5 * LOG2E
    final = out_weight is not None
    groups = max(len(states), 1)

    def kernel(*refs):
        refs = list(refs)
        query_ref = refs.pop(0)
        set_refs = []
        for whole in joined:
            ref = refs.pop(0)
            set_refs.append((ref, 0, ref, width) if whole else (ref, 0, refs.pop(0), 0))
        state_refs = [[refs.pop(0) for _ in range(3)] for _ in states]
        if wait is not None:
            refs.pop(1 if final else 0)
        if final:
            weight_ref, out_ref, attended_ref = refs.pop(0), refs.pop(0), refs.pop(-1)
        else:
            numer_out, peak_out, total_out = [refs.pop(0) for _ in range(3)]
        score_ref, value_ref, key_ref = refs.pop(0), refs.pop(0), refs.pop(0)
        if row_strides is not None:
            offset_ref = refs.pop(0)
            row = lax.broadcasted_iota(jnp.int32, (keys, LANES), 0)
            rank = sum((row & (s - 1) == 0).astype(jnp.int32) for s in row_strides)
            offsets = jnp.zeros((keys, LANES), jnp.float32)
            for times in range(1, len(row_strides) + 1):
                offsets = jnp.where(rank == times, math.log2(1 + times), offsets)
            offset_ref[...] = offsets

        ones = jnp.ones((16, padded), jnp.bfloat16)
        key_chunks = [(low, min(KEY_CHUNK, keys - low)) for low in range(0, keys, KEY_CHUNK)]
        value_chunks = [(low, min(CHUNK, padded - low)) for low in range(0, padded, CHUNK)]

        def column(pair):
            return pl.multiple_of(pair * PAIR, PAIR)

        def head_queries(pair, half):
            turned = query_ref[:, pl.ds(column(pair), PAIR)].T
            row = lax.broadcasted_iota(jnp.int32, turned.shape, 0)
            own = (row < HEAD_DIM) if half == 0 else (row >= HEAD_DIM)
            return jnp.where(own, turned, jnp.zeros_like(turned))

        def load_keys(pair):
            at = 0
            for (ref, _, _, _), size in zip(set_refs, sizes):
                key_ref[at : at + size, :] = ref[:, pl.ds(column(pair), PAIR)]
                at += size

        def score(half, query_head, chunk, running):
            low, count = chunk
            scores = jnp.dot(
                key_ref[low : low + count, :], query_head, preferred_element_type=jnp.float32
            )
            score_ref[half, low : low + count, :] = scores
            tallest = jnp.max(scores.reshape(count // 8, 8, tokens), axis=0)
            return tallest if running is None else jnp.maximum(running, tallest)

        def weigh(half, peak, weighted, chunk, gathered):
            low, size = chunk
            high = min(low + size, keys)
            pieces = []
            for first, last, times in row_runs:
                first, last = max(first, low), min(last, high)
                if first < last:
                    offset = peak - math.log2(times)
                    power = score_ref[half, first:last, :] * scale - offset
                    if row_strides is not None:
                        extra = offset_ref[first:last, :]
                        power = power + jnp.concatenate([extra] * (tokens // LANES), axis=1)
                    pieces.append(jnp.exp2(power))
            if low + size > keys:
                pieces.append(jnp.zeros((low + size - keys, tokens), jnp.float32))
            probs = (pieces[0] if len(pieces) == 1 else jnp.concatenate(pieces, axis=0)).astype(
                jnp.bfloat16
            )
            product = jnp.dot(
                weighted[:, low : low + size], probs, preferred_element_type=jnp.float32
            )
            return product if gathered is None else gathered + product

        def one_group(first_pair, last_pair, earlier):
            def local_rows(pair, half):
                start = (pair - first_pair) * PAIR + half * HEAD_DIM
                return pl.ds(pl.multiple_of(start, HEAD_DIM), HEAD_DIM)

            def local_head(pair, half):
                return pl.ds(2 * (pair - first_pair) + half, 1)

            def finish(pair, half, gathered, peak, before):
                numer, total = gathered[:HEAD_DIM], gathered[HEAD_DIM : HEAD_DIM + 1]
                if earlier is not None:
                    factor = jnp.exp2(before - peak)
                    numer = numer + factor * earlier[0][local_rows(pair, half), :]
                    total = total + factor * earlier[2][local_head(pair, half), :]
                start = pl.multiple_of(column(pair) + half * HEAD_DIM, HEAD_DIM)
                rows = pl.ds(start, HEAD_DIM)
                if final:
                    attended_ref[half] = (numer / total).astype(jnp.bfloat16)
                    if half == 1:
                        both = attended_ref[...].reshape(PAIR, tokens)
                        out_ref[:, pl.ds(column(pair), PAIR)] = both.T
                else:
                    head = pl.ds(2 * pair + half, 1)
                    numer_out[rows, :] = numer
                    peak_out[head, :] = peak
                    total_out[head, :] = total

            def overlap(pair, half, running, values_t, next_pair, next_half):
                peak = jnp.max(running, axis=0, keepdims=True) * scale
                before = None
                if earlier is not None:
                    before = earlier[1][local_head(pair, half), :]
                    peak = jnp.maximum(peak, before)
                weighted = jnp.concatenate(
                    [values_t[half * HEAD_DIM : (half + 1) * HEAD_DIM], ones], axis=0
                )
                if next_half == 0:
                    load_keys(next_pair)
                query_head = head_queries(next_pair, next_half)
                next_running, gathered = None, None
                for step in range(max(len(key_chunks), len(value_chunks))):
                    if step < len(key_chunks):
                        next_running = score(
                            next_half, query_head, key_chunks[step], next_running
                        )
                    if step < len(value_chunks):
                        gathered = weigh(half, peak, weighted, value_chunks[step], gathered)
                finish(pair, half, gathered, peak, before)
                return next_running

            def pair_step(pair, running):
                at = 0
                for (_, _, ref, shift), size in zip(set_refs, sizes):
                    value_ref[at : at + size, :] = ref[:, pl.ds(column(pair) + shift, PAIR)]
                    at += size
                if padded > keys:
                    value_ref[keys:, :] = jnp.zeros((padded - keys, PAIR), jnp.bfloat16)
                values_t = value_ref[...].T
                running = overlap(pair, 0, running, values_t, pair, 1)
                later = jnp.minimum(pair + 1, last_pair - 1)
                return overlap(pair, 1, running, values_t, later, 0)

            load_keys(first_pair)
            first_head = head_queries(first_pair, 0)
            running = None
            for chunk in key_chunks:
                running = score(0, first_head, chunk, running)
            lax.fori_loop(first_pair, last_pair, pair_step, running)

        for group in range(groups):
            one_group(
                group * pairs // groups,
                (group + 1) * pairs // groups,
                state_refs[group] if states else None,
            )
        if final:
            out_ref[...] = jnp.dot(
                out_ref[...], weight_ref[...], preferred_element_type=jnp.float32
            ).astype(jnp.bfloat16)

    if final:
        out_shape = jax.ShapeDtypeStruct((tokens, width), jnp.bfloat16)
    else:
        out_shape = [
            jax.ShapeDtypeStruct((width, tokens), jnp.float32),
            jax.ShapeDtypeStruct((heads, tokens), jnp.float32),
            jax.ShapeDtypeStruct((heads, tokens), jnp.float32),
        ]
    scratch = [
        pltpu.VMEM((2, padded, tokens), jnp.float32),
        pltpu.VMEM((padded, PAIR), jnp.bfloat16),
        pltpu.VMEM((padded, PAIR), jnp.bfloat16),
    ]
    if row_strides is not None:
        scratch.append(pltpu.VMEM((keys, LANES), jnp.float32))
    if final:
        scratch.append(pltpu.VMEM((2, HEAD_DIM, tokens), jnp.bfloat16))
    operands = [queries]
    for block, whole in zip(sets, joined):
        operands += [block] if whole else list(block)
    whole_spec = pl.BlockSpec(memory_space=pltpu.VMEM)
    specs = [whole_spec] * len(operands)
    if part[1] > 1:
        specs = [
            pl.BlockSpec((array.shape[0], array.shape[1] // part[1]), lambda step: (0, part[0]))
            for array in operands
        ]
    for array in [array for state in states for array in state] + ([out_weight] if final else []):
        operands.append(array)
        specs.append(whole_spec)
    if wait is not None:
        operands.append(wait)
        specs.append(pl.BlockSpec(memory_space=pl.ANY))
    return pl.pallas_call(
        kernel,
        out_shape=out_shape,
        grid=(1,) if part[1] > 1 else (),
        in_specs=specs,
        scratch_shapes=scratch,
        compiler_params=pltpu.CompilerParams(
            vmem_limit_bytes=VMEM_BYTES
        ),
        cost_estimate=pl.CostEstimate(
            flops=16 * tokens * keys * width,
            bytes_accessed=(4 * keys * width + 4 * tokens * width),
            transcendentals=tokens * keys * heads,
        ),
    )(*operands)


def local(queries, key_rows, values, out_weight):
    query_rows, own_keys, own_values = queries[0], key_rows[0], values[0]
    tokens = query_rows.shape[0]
    n_inner, n_outer = lax.axis_size("inner"), lax.axis_size("outer")
    inner_bits = n_inner.bit_length() - 1
    strides = [1 << (bit + 1) for bit in range(inner_bits + 1)]
    sends = [tokens >> (bit + 1) for bit in range(inner_bits + 1)]
    n_global = tokens // GSTEP

    rows = np.arange(0, tokens, 2)
    rank = sum((rows % s == 0).astype(np.int64) for s in strides + [GSTEP])
    order = rows[np.lexsort((rows, -rank))]
    select = np.zeros((sends[0], tokens), np.float32)
    select[np.arange(sends[0]), order] = 1.0

    def prefix_counts(level, low, high):
        return sum((order[low:high] % s == 0).astype(np.int64) for s in strides[level:])

    first_a, first_b, far = order_rows(
        jnp.asarray(select, jnp.bfloat16),
        own_keys,
        own_values,
        [(0, sends[1]), (sends[1], sends[0]), (0, n_global)],
    )

    held = {0: (first_a, 0)}
    for bit in range(1, inner_bits):
        held[1 << bit] = (across(first_a[: sends[bit]], "inner", 1 << bit), 0)
    held[1] = (across(first_a, "inner", 1), 0)
    own_set = [(own_keys, own_values)]
    own_states, moved, flip = [], far, 2
    while flip < n_outer or len(own_states) < 2:
        if flip < n_outer:
            came = across(moved, "outer", flip)
            flip *= 2
        if len(own_states) < 2:
            own_states.append(
                attend(
                    query_rows,
                    own_set,
                    row_strides=strides,
                    part=(len(own_states), 2),
                    wait=moved if own_states else None,
                )
            )
        moved = join_after([(moved, 0, moved.shape[0]), (came, 0, came.shape[0])], own_states[-1][1])
    far = moved
    n_far = far.shape[0]
    fars = {0: (far, 0)}

    def first_rows(where, count):
        return (where[0], where[1], where[1] + count)

    near_b = across(
        join_after([(first_b, 0, sends[0] - sends[1]), (far, 0, n_far)], far), "inner", 1
    )
    fars[1] = (near_b, sends[0] - sends[1])
    own_done = far

    known = [0] + [1 << bit for bit in range(inner_bits)]
    late = [d for d in range(n_inner) if d not in known]
    last = sends[inner_bits]
    late_sets = [near_b]
    late_counts = [prefix_counts(0, sends[1], sends[0]), np.ones(n_far, np.int64)]
    for bit in range(1, inner_bits):
        count = sends[bit]
        others = range(1, 1 << bit)
        pieces = [first_rows(held[d], count) for d in others] + [first_rows(fars[0], n_far)]
        own_done = join_after(pieces, own_done)
        came = across(own_done, "inner", 1 << bit)
        for at, d in enumerate(others):
            held[d | 1 << bit] = (came, at * count)
        fars[1 << bit] = (came, len(others) * count)
        late_sets.append(came)
        late_counts += [prefix_counts(bit, 0, count)] * len(others) + [np.ones(n_far, np.int64)]
    for d in late:
        fars[d] = (across(far, "inner", d), 0)
        late_sets.append(fars[d][0])
        late_counts.append(np.ones(n_far, np.int64))
    pieces = [first_rows(held[d], last) for d in known]
    moved = join_after(pieces, own_done)
    early_core = across(moved, "outer", 1)

    early_sets = [held[d][0] for d in known[1:]] + [early_core, far]
    early_counts = [prefix_counts(0, 0, sends[1])]
    early_counts += [prefix_counts(bit, 0, sends[bit]) for bit in range(1, inner_bits)]
    early_counts.append(np.ones(early_core.shape[0] + n_far, np.int64))
    state = attend(query_rows, early_sets, np.concatenate(early_counts), states=own_states)

    pieces = [first_rows(held[d], last) for d in late]
    pieces += [first_rows(fars[d], n_far) for d in range(n_inner)]
    late_core = across(join_after(pieces, state[1]), "outer", 1)
    state = attend(query_rows, late_sets, np.concatenate(late_counts), states=[state])
    result = attend(query_rows, [late_core], states=[state], out_weight=out_weight)
    return result[None]


def solution(mesh):
    placed = (P("outer", "inner", None), P("outer", "inner", None), P("outer", "inner", None), P())
    return jax.shard_map(
        local, mesh=mesh, in_specs=placed, out_specs=P("outer", "inner", None), check_vma=False
    )
```

```python
import math

import jax
import jax.numpy as jnp
import numpy as np
from jax import lax
from jax.experimental import pallas as pl
from jax.experimental.pallas import tpu as pltpu
from jax.sharding import PartitionSpec as P

HEAD_DIM = 64
GSTEP = 64
PAIR = 2 * HEAD_DIM
CHUNK = 256
KEY_CHUNK = 512
UNROLL = 3
LANES = 128
LOG2E = math.log2(math.e)
VMEM_BYTES = 16 * 1024 * 1024
JOIN_VMEM_BYTES = 8 * 1024 * 1024
FETCH_VMEM_BYTES = 60 * 1024 * 1024


def across(block, axis, flip):
    return lax.ppermute(block, axis, [(i, i ^ flip) for i in range(lax.axis_size(axis))])


def after(block, *others):
    return lax.optimization_barrier((block, *others))[0]


def join_after(pieces, other):
    width = pieces[0][0].shape[1]
    total = sum(high - low for _, low, high in pieces)

    def kernel(*refs):
        out_ref, at = refs[-1], 0
        for ref, (_, low, high) in zip(refs, pieces):
            out_ref[at : at + high - low, :] = ref[low:high, :]
            at += high - low

    return pl.pallas_call(
        kernel,
        out_shape=jax.ShapeDtypeStruct((total, width), pieces[0][0].dtype),
        in_specs=[pl.BlockSpec(memory_space=pltpu.VMEM)] * len(pieces)
        + [pl.BlockSpec(memory_space=pl.ANY)],
        compiler_params=pltpu.CompilerParams(vmem_limit_bytes=JOIN_VMEM_BYTES),
        cost_estimate=pl.CostEstimate(
            flops=0, bytes_accessed=4 * total * width, transcendentals=0
        ),
    )(*[block for block, _, _ in pieces], other)


def runs(counts):
    found = []
    for at, value in enumerate(counts):
        if found and found[-1][2] == value:
            found[-1][1] = at + 1
        else:
            found.append([at, at + 1, int(value)])
    return [tuple(entry) for entry in found]


def order_rows(select, key_rows, values, prefixes):
    tokens, width = key_rows.shape

    def kernel(select_hbm, key_hbm, value_hbm, *refs):
        out_refs, (select_ref, row_ref, sems) = refs[: len(prefixes)], refs[len(prefixes) :]
        copies = [
            pltpu.make_async_copy(select_hbm, select_ref, sems.at[0]),
            pltpu.make_async_copy(key_hbm, row_ref.at[0], sems.at[1]),
            pltpu.make_async_copy(value_hbm, row_ref.at[1], sems.at[2]),
        ]
        for copy in copies:
            copy.start()
        copies[0].wait()
        for half in range(2):
            copies[1 + half].wait()
            moved = jnp.dot(
                select_ref[...], row_ref[half], preferred_element_type=jnp.float32
            ).astype(jnp.bfloat16)
            for (low, high), out_ref in zip(prefixes, out_refs):
                out_ref[:, half * width : (half + 1) * width] = moved[low:high]

    return pl.pallas_call(
        kernel,
        out_shape=[
            jax.ShapeDtypeStruct((high - low, 2 * width), jnp.bfloat16) for low, high in prefixes
        ],
        in_specs=[pl.BlockSpec(memory_space=pltpu.HBM)] * 3,
        scratch_shapes=[
            pltpu.VMEM(select.shape, jnp.bfloat16),
            pltpu.VMEM((2, tokens, width), jnp.bfloat16),
            pltpu.SemaphoreType.DMA((3,)),
        ],
        compiler_params=pltpu.CompilerParams(vmem_limit_bytes=FETCH_VMEM_BYTES),
        cost_estimate=pl.CostEstimate(
            flops=4 * select.size * width, bytes_accessed=6 * tokens * width, transcendentals=0
        ),
    )(select, key_rows, values)


def attend(queries, sets, counts=None, row_strides=None, part=(0, 1), states=(), out_weight=None, wait=None):
    tokens = queries.shape[0]
    width = queries.shape[1] // part[1]
    heads, pairs = width // HEAD_DIM, width // PAIR
    joined = [not isinstance(block, tuple) for block in sets]
    sizes = [(block if whole else block[0]).shape[0] for block, whole in zip(sets, joined)]
    keys = sum(sizes)
    padded = -(-keys // LANES) * LANES
    row_runs = [(0, keys, 1)] if counts is None else runs(counts)
    scale = HEAD_DIM**-0.5 * LOG2E
    final = out_weight is not None
    groups = max(len(states), 1)

    def kernel(*refs):
        refs = list(refs)
        query_ref = refs.pop(0)
        set_refs = []
        for whole in joined:
            ref = refs.pop(0)
            set_refs.append((ref, 0, ref, width) if whole else (ref, 0, refs.pop(0), 0))
        state_refs = [[refs.pop(0) for _ in range(3)] for _ in states]
        if wait is not None:
            refs.pop(1 if final else 0)
        if final:
            weight_ref, out_ref, attended_ref = refs.pop(0), refs.pop(0), refs.pop(-1)
        else:
            numer_out, peak_out, total_out = [refs.pop(0) for _ in range(3)]
        score_ref, value_ref, key_ref, turned_ref = [refs.pop(0) for _ in range(4)]
        if row_strides is not None:
            offset_ref = refs.pop(0)
            row = lax.broadcasted_iota(jnp.int32, (keys, LANES), 0)
            rank = sum((row & (s - 1) == 0).astype(jnp.int32) for s in row_strides)
            offsets = jnp.zeros((keys, LANES), jnp.float32)
            for times in range(1, len(row_strides) + 1):
                offsets = jnp.where(rank == times, math.log2(1 + times), offsets)
            offset_ref[...] = offsets

        ones = jnp.ones((16, padded), jnp.bfloat16)
        key_chunks = [(low, min(KEY_CHUNK, keys - low)) for low in range(0, keys, KEY_CHUNK)]
        value_chunks = [(low, min(CHUNK, padded - low)) for low in range(0, padded, CHUNK)]

        def column(pair):
            return pl.multiple_of(pair * PAIR, PAIR)

        def head_queries(half):
            turned = turned_ref[...]
            row = lax.broadcasted_iota(jnp.int32, turned.shape, 0)
            own = (row < HEAD_DIM) if half == 0 else (row >= HEAD_DIM)
            return jnp.where(own, turned, jnp.zeros_like(turned))

        def load(pair):
            turned_ref[...] = query_ref[:, pl.ds(column(pair), PAIR)].T
            at = 0
            for (ref, _, _, _), size in zip(set_refs, sizes):
                key_ref[at : at + size, :] = ref[:, pl.ds(column(pair), PAIR)]
                at += size

        def score(half, query_head, chunk, running):
            low, count = chunk
            scores = jnp.dot(
                key_ref[low : low + count, :], query_head, preferred_element_type=jnp.float32
            )
            score_ref[half, low : low + count, :] = scores
            tallest = jnp.max(scores.reshape(count // 8, 8, tokens), axis=0)
            return tallest if running is None else jnp.maximum(running, tallest)

        def weigh(half, peak, weighted, chunk, gathered):
            low, size = chunk
            high = min(low + size, keys)
            pieces = []
            for first, last, times in row_runs:
                first, last = max(first, low), min(last, high)
                if first < last:
                    offset = peak - math.log2(times)
                    power = score_ref[half, first:last, :] * scale - offset
                    if row_strides is not None:
                        extra = offset_ref[first:last, :]
                        power = power + jnp.concatenate([extra] * (tokens // LANES), axis=1)
                    pieces.append(jnp.exp2(power))
            if low + size > keys:
                pieces.append(jnp.zeros((low + size - keys, tokens), jnp.float32))
            probs = (pieces[0] if len(pieces) == 1 else jnp.concatenate(pieces, axis=0)).astype(
                jnp.bfloat16
            )
            product = jnp.dot(
                weighted[:, low : low + size], probs, preferred_element_type=jnp.float32
            )
            return product if gathered is None else gathered + product

        def one_group(first_pair, last_pair, earlier):
            def local_rows(pair, half):
                start = (pair - first_pair) * PAIR + half * HEAD_DIM
                return pl.ds(pl.multiple_of(start, HEAD_DIM), HEAD_DIM)

            def local_head(pair, half):
                return pl.ds(2 * (pair - first_pair) + half, 1)

            def finish(pair, half, gathered, peak, before):
                numer, total = gathered[:HEAD_DIM], gathered[HEAD_DIM : HEAD_DIM + 1]
                if earlier is not None:
                    factor = jnp.exp2(before - peak)
                    numer = numer + factor * earlier[0][local_rows(pair, half), :]
                    total = total + factor * earlier[2][local_head(pair, half), :]
                start = pl.multiple_of(column(pair) + half * HEAD_DIM, HEAD_DIM)
                rows = pl.ds(start, HEAD_DIM)
                if final:
                    attended_ref[half] = (numer * (1.0 / total)).astype(jnp.bfloat16)
                    if half == 1:
                        both = attended_ref[...].reshape(PAIR, tokens)
                        out_ref[:, pl.ds(column(pair), PAIR)] = both.T
                else:
                    head = pl.ds(2 * pair + half, 1)
                    numer_out[rows, :] = numer
                    peak_out[head, :] = peak
                    total_out[head, :] = total

            def overlap(pair, half, running, values_t, next_pair, next_half):
                peak = jnp.max(running, axis=0, keepdims=True) * scale
                before = None
                if earlier is not None:
                    before = earlier[1][local_head(pair, half), :]
                    peak = jnp.maximum(peak, before)
                weighted = jnp.concatenate(
                    [values_t[half * HEAD_DIM : (half + 1) * HEAD_DIM], ones], axis=0
                )
                if next_half == 0:
                    load(next_pair)
                query_head = head_queries(next_half)
                next_running, gathered = None, None
                for step in range(max(len(key_chunks), len(value_chunks))):
                    if step < len(key_chunks):
                        next_running = score(
                            next_half, query_head, key_chunks[step], next_running
                        )
                    if step < len(value_chunks):
                        gathered = weigh(half, peak, weighted, value_chunks[step], gathered)
                finish(pair, half, gathered, peak, before)
                return next_running

            def pair_step(pair, running):
                at = 0
                for (_, _, ref, shift), size in zip(set_refs, sizes):
                    value_ref[at : at + size, :] = ref[:, pl.ds(column(pair) + shift, PAIR)]
                    at += size
                if padded > keys:
                    value_ref[keys:, :] = jnp.zeros((padded - keys, PAIR), jnp.bfloat16)
                values_t = value_ref[...].T
                running = overlap(pair, 0, running, values_t, pair, 1)
                later = jnp.minimum(pair + 1, last_pair - 1)
                return overlap(pair, 1, running, values_t, later, 0)

            load(first_pair)
            first_head = head_queries(0)
            running = None
            for chunk in key_chunks:
                running = score(0, first_head, chunk, running)
            lax.fori_loop(first_pair, last_pair, pair_step, running, unroll=UNROLL)

        for group in range(groups):
            one_group(
                group * pairs // groups,
                (group + 1) * pairs // groups,
                state_refs[group] if states else None,
            )
        if final:
            out_ref[...] = jnp.dot(
                out_ref[...], weight_ref[...], preferred_element_type=jnp.float32
            ).astype(jnp.bfloat16)

    if final:
        out_shape = jax.ShapeDtypeStruct((tokens, width), jnp.bfloat16)
    else:
        out_shape = [
            jax.ShapeDtypeStruct((width, tokens), jnp.float32),
            jax.ShapeDtypeStruct((heads, tokens), jnp.float32),
            jax.ShapeDtypeStruct((heads, tokens), jnp.float32),
        ]
    scratch = [
        pltpu.VMEM((2, padded, tokens), jnp.float32),
        pltpu.VMEM((padded, PAIR), jnp.bfloat16),
        pltpu.VMEM((padded, PAIR), jnp.bfloat16),
        pltpu.VMEM((PAIR, tokens), jnp.bfloat16),
    ]
    if row_strides is not None:
        scratch.append(pltpu.VMEM((keys, LANES), jnp.float32))
    if final:
        scratch.append(pltpu.VMEM((2, HEAD_DIM, tokens), jnp.bfloat16))
    operands = [queries]
    for block, whole in zip(sets, joined):
        operands += [block] if whole else list(block)
    whole_spec = pl.BlockSpec(memory_space=pltpu.VMEM)
    specs = [whole_spec] * len(operands)
    if part[1] > 1:
        specs = [
            pl.BlockSpec((array.shape[0], array.shape[1] // part[1]), lambda step: (0, part[0]))
            for array in operands
        ]
    for array in [array for state in states for array in state] + ([out_weight] if final else []):
        operands.append(array)
        specs.append(whole_spec)
    if wait is not None:
        operands.append(wait)
        specs.append(pl.BlockSpec(memory_space=pl.ANY))
    return pl.pallas_call(
        kernel,
        out_shape=out_shape,
        grid=(1,) if part[1] > 1 else (),
        in_specs=specs,
        scratch_shapes=scratch,
        compiler_params=pltpu.CompilerParams(
            vmem_limit_bytes=VMEM_BYTES
        ),
        cost_estimate=pl.CostEstimate(
            flops=16 * tokens * keys * width,
            bytes_accessed=(4 * keys * width + 4 * tokens * width),
            transcendentals=tokens * keys * heads,
        ),
    )(*operands)


def local(queries, key_rows, values, out_weight):
    query_rows, own_keys, own_values = queries[0], key_rows[0], values[0]
    tokens = query_rows.shape[0]
    n_inner, n_outer = lax.axis_size("inner"), lax.axis_size("outer")
    inner_bits = n_inner.bit_length() - 1
    strides = [1 << (bit + 1) for bit in range(inner_bits + 1)]
    sends = [tokens >> (bit + 1) for bit in range(inner_bits + 1)]
    n_global = tokens // GSTEP

    rows = np.arange(0, tokens, 2)
    rank = sum((rows % s == 0).astype(np.int64) for s in strides + [GSTEP])
    order = rows[np.lexsort((rows, -rank))]
    select = np.zeros((sends[0], tokens), np.float32)
    select[np.arange(sends[0]), order] = 1.0

    def prefix_counts(level, low, high):
        return sum((order[low:high] % s == 0).astype(np.int64) for s in strides[level:])

    first_a, first_b, far = order_rows(
        jnp.asarray(select, jnp.bfloat16),
        own_keys,
        own_values,
        [(0, sends[1]), (sends[1], sends[0]), (0, n_global)],
    )

    held = {0: (first_a, 0)}
    for bit in range(1, inner_bits):
        held[1 << bit] = (across(first_a[: sends[bit]], "inner", 1 << bit), 0)
    held[1] = (across(first_a, "inner", 1), 0)
    own_set = [(own_keys, own_values)]
    own_states, moved, flip = [], far, 2
    while flip < n_outer or len(own_states) < 2:
        if flip < n_outer:
            came = across(moved, "outer", flip)
            flip *= 2
        if len(own_states) < 2:
            own_states.append(
                attend(
                    query_rows,
                    own_set,
                    row_strides=strides,
                    part=(len(own_states), 2),
                    wait=moved if own_states else None,
                )
            )
        moved = join_after([(moved, 0, moved.shape[0]), (came, 0, came.shape[0])], own_states[-1][1])
    far = moved
    n_far = far.shape[0]
    fars = {0: (far, 0)}

    def first_rows(where, count):
        return (where[0], where[1], where[1] + count)

    near_b = across(first_b, "inner", 1)
    fars[1] = (across(far, "inner", 1), 0)
    own_done = far

    known = [0] + [1 << bit for bit in range(inner_bits)]
    late = [d for d in range(n_inner) if d not in known]
    last = sends[inner_bits]
    late_sets, late_counts = [], []
    for bit in range(1, inner_bits):
        count = sends[bit]
        others = range(1, 1 << bit)
        pieces = [first_rows(held[d], count) for d in others] + [first_rows(fars[0], n_far)]
        own_done = join_after(pieces, own_done)
        came = across(own_done, "inner", 1 << bit)
        for at, d in enumerate(others):
            held[d | 1 << bit] = (came, at * count)
        fars[1 << bit] = (came, len(others) * count)
        late_sets.append(came)
        late_counts += [prefix_counts(bit, 0, count)] * len(others) + [np.ones(n_far, np.int64)]
    for d in late:
        fars[d] = (across(far, "inner", d), 0)
    late_sets += [fars[d][0] for d in [0, 1] + late]
    late_counts.append(np.ones(n_far * (2 + len(late)), np.int64))

    early_sets = [held[1][0], near_b] + [held[d][0] for d in known[2:]]
    early_counts = [prefix_counts(0, 0, sends[0])]
    early_counts += [prefix_counts(bit, 0, sends[bit]) for bit in range(1, inner_bits)]
    state = attend(query_rows, early_sets, np.concatenate(early_counts), states=own_states)

    pieces = [first_rows(held[d], last) for d in range(n_inner)]
    pieces += [first_rows(fars[d], n_far) for d in range(n_inner)]
    core = across(join_after(pieces, state[1]), "outer", 1)
    state = attend(query_rows, late_sets, np.concatenate(late_counts), states=[state])
    result = attend(query_rows, [core], states=[state], out_weight=out_weight)
    return result[None]


def solution(mesh):
    placed = (P("outer", "inner", None), P("outer", "inner", None), P("outer", "inner", None), P())
    return jax.shard_map(
        local, mesh=mesh, in_specs=placed, out_specs=P("outer", "inner", None), check_vma=False
    )
```

```python
import math

import jax
import jax.numpy as jnp
import numpy as np
from jax import lax
from jax.experimental import pallas as pl
from jax.experimental.pallas import tpu as pltpu
from jax.sharding import PartitionSpec as P

HEAD_DIM = 64
GSTEP = 64
PAIR = 2 * HEAD_DIM
CHUNK = 256
KEY_CHUNK = 512
UNROLL = 3
LANES = 128
LOG2E = math.log2(math.e)
VMEM_BYTES = 16 * 1024 * 1024
JOIN_VMEM_BYTES = 8 * 1024 * 1024
FETCH_VMEM_BYTES = 56 * 1024 * 1024


def across(block, axis, flip):
    return lax.ppermute(block, axis, [(i, i ^ flip) for i in range(lax.axis_size(axis))])


def after(block, *others):
    return lax.optimization_barrier((block, *others))[0]


def join_after(pieces, other):
    width = pieces[0][0].shape[1]
    total = sum(high - low for _, low, high in pieces)

    def kernel(*refs):
        out_ref, at = refs[-1], 0
        for ref, (_, low, high) in zip(refs, pieces):
            out_ref[at : at + high - low, :] = ref[low:high, :]
            at += high - low

    return pl.pallas_call(
        kernel,
        out_shape=jax.ShapeDtypeStruct((total, width), pieces[0][0].dtype),
        in_specs=[pl.BlockSpec(memory_space=pltpu.VMEM)] * len(pieces)
        + [pl.BlockSpec(memory_space=pl.ANY)],
        compiler_params=pltpu.CompilerParams(vmem_limit_bytes=JOIN_VMEM_BYTES),
        cost_estimate=pl.CostEstimate(
            flops=0, bytes_accessed=4 * total * width, transcendentals=0
        ),
    )(*[block for block, _, _ in pieces], other)


def runs(counts):
    found = []
    for at, value in enumerate(counts):
        if found and found[-1][2] == value:
            found[-1][1] = at + 1
        else:
            found.append([at, at + 1, int(value)])
    return [tuple(entry) for entry in found]


def order_rows(select, key_rows, values, prefixes):
    tokens, width = key_rows.shape

    def kernel(select_hbm, key_hbm, value_hbm, *refs):
        out_refs, (select_ref, row_ref, moved_ref, sems) = (
            refs[: len(prefixes)],
            refs[len(prefixes) :],
        )
        copies = [
            pltpu.make_async_copy(select_hbm, select_ref, sems.at[0]),
            pltpu.make_async_copy(key_hbm, row_ref.at[0], sems.at[1]),
            pltpu.make_async_copy(value_hbm, row_ref.at[1], sems.at[2]),
        ]
        for copy in copies:
            copy.start()
        copies[0].wait()
        stores = []
        for half in range(2):
            copies[1 + half].wait()
            moved_ref[half] = jnp.dot(
                select_ref[...], row_ref[half], preferred_element_type=jnp.float32
            ).astype(jnp.bfloat16)
            cols = slice(half * width, (half + 1) * width)
            for (low, high), out_ref in zip(prefixes[:-1], out_refs):
                stores.append(
                    pltpu.make_async_copy(
                        moved_ref.at[half, low:high], out_ref.at[:, cols], sems.at[3 + len(stores)]
                    )
                )
                stores[-1].start()
            low, high = prefixes[-1]
            out_refs[-1][:, cols] = moved_ref[half, low : 2 * high, :][: high - low]
        for store in stores:
            store.wait()

    return pl.pallas_call(
        kernel,
        out_shape=[
            jax.ShapeDtypeStruct((high - low, 2 * width), jnp.bfloat16) for low, high in prefixes
        ],
        in_specs=[pl.BlockSpec(memory_space=pltpu.HBM)] * 3,
        out_specs=[pl.BlockSpec(memory_space=pl.ANY)] * (len(prefixes) - 1)
        + [pl.BlockSpec(memory_space=pltpu.VMEM)],
        scratch_shapes=[
            pltpu.VMEM(select.shape, jnp.bfloat16),
            pltpu.VMEM((2, tokens, width), jnp.bfloat16),
            pltpu.VMEM((2, select.shape[0], width), jnp.bfloat16),
            pltpu.SemaphoreType.DMA((3 + 2 * (len(prefixes) - 1),)),
        ],
        compiler_params=pltpu.CompilerParams(vmem_limit_bytes=FETCH_VMEM_BYTES),
        cost_estimate=pl.CostEstimate(
            flops=4 * select.size * width, bytes_accessed=6 * tokens * width, transcendentals=0
        ),
    )(select, key_rows, values)


def attend(queries, sets, counts=None, row_strides=None, part=(0, 1), states=(), out_weight=None, wait=None):
    tokens = queries.shape[0]
    full = queries.shape[1]
    width = full // part[1]
    base = part[0] * width
    heads, pairs = width // HEAD_DIM, width // PAIR
    joined = [not isinstance(block, tuple) for block in sets]
    sizes = [(block if whole else block[0]).shape[0] for block, whole in zip(sets, joined)]
    keys = sum(sizes)
    padded = -(-keys // LANES) * LANES
    row_runs = [(0, keys, 1)] if counts is None else runs(counts)
    scale = HEAD_DIM**-0.5 * LOG2E
    final = out_weight is not None
    groups = max(len(states), 1)

    def kernel(*refs):
        refs = list(refs)
        query_ref = refs.pop(0)
        set_refs = []
        for whole in joined:
            ref = refs.pop(0)
            set_refs.append((ref, ref, full) if whole else (ref, refs.pop(0), 0))
        state_refs = [[refs.pop(0) for _ in range(3)] for _ in states]
        if wait is not None:
            refs.pop(1 if final else 0)
        if final:
            weight_ref, out_hbm = refs.pop(0), refs.pop(0)
            attended_ref, out_ref, result_ref, sems = refs[-4:]
        else:
            numer_out, peak_out, total_out = [refs.pop(0) for _ in range(3)]
        score_ref, value_ref, key_ref, turned_ref = [refs.pop(0) for _ in range(4)]
        if row_strides is not None:
            offset_ref = refs.pop(0)
            row = lax.broadcasted_iota(jnp.int32, (keys, LANES), 0)
            rank = sum((row & (s - 1) == 0).astype(jnp.int32) for s in row_strides)
            offsets = jnp.zeros((keys, LANES), jnp.float32)
            for times in range(1, len(row_strides) + 1):
                offsets = jnp.where(rank == times, math.log2(1 + times), offsets)
            offset_ref[...] = offsets

        ones = jnp.ones((16, padded), jnp.bfloat16)
        key_chunks = [(low, min(KEY_CHUNK, keys - low)) for low in range(0, keys, KEY_CHUNK)]
        value_chunks = [(low, min(CHUNK, padded - low)) for low in range(0, padded, CHUNK)]

        def column(pair):
            return pl.multiple_of(pair * PAIR, PAIR)

        def columns(pair, shift=0):
            return pl.ds(pl.multiple_of(base + shift + pair * PAIR, PAIR), PAIR)

        def head_queries(half):
            turned = turned_ref[...]
            row = lax.broadcasted_iota(jnp.int32, turned.shape, 0)
            own = (row < HEAD_DIM) if half == 0 else (row >= HEAD_DIM)
            return jnp.where(own, turned, jnp.zeros_like(turned))

        def load(pair):
            turned_ref[...] = query_ref[:, columns(pair)].T
            at = 0
            for (ref, _, _), size in zip(set_refs, sizes):
                key_ref[at : at + size, :] = ref[:, columns(pair)]
                at += size

        def score(half, query_head, chunk, running):
            low, count = chunk
            scores = jnp.dot(
                key_ref[low : low + count, :], query_head, preferred_element_type=jnp.float32
            )
            score_ref[half, low : low + count, :] = scores
            tallest = jnp.max(scores.reshape(count // 8, 8, tokens), axis=0)
            return tallest if running is None else jnp.maximum(running, tallest)

        def weigh(half, peak, weighted, chunk, gathered):
            low, size = chunk
            high = min(low + size, keys)
            pieces = []
            for first, last, times in row_runs:
                first, last = max(first, low), min(last, high)
                if first < last:
                    offset = peak - math.log2(times)
                    power = score_ref[half, first:last, :] * scale - offset
                    if row_strides is not None:
                        extra = offset_ref[first:last, :]
                        power = power + jnp.concatenate([extra] * (tokens // LANES), axis=1)
                    pieces.append(jnp.exp2(power))
            if low + size > keys:
                pieces.append(jnp.zeros((low + size - keys, tokens), jnp.float32))
            probs = (pieces[0] if len(pieces) == 1 else jnp.concatenate(pieces, axis=0)).astype(
                jnp.bfloat16
            )
            product = jnp.dot(
                weighted[:, low : low + size], probs, preferred_element_type=jnp.float32
            )
            return product if gathered is None else gathered + product

        def one_group(first_pair, last_pair, earlier):
            def local_rows(pair, half):
                start = (pair - first_pair) * PAIR + half * HEAD_DIM
                return pl.ds(pl.multiple_of(start, HEAD_DIM), HEAD_DIM)

            def local_head(pair, half):
                return pl.ds(2 * (pair - first_pair) + half, 1)

            def finish(pair, half, gathered, peak, before):
                numer, total = gathered[:HEAD_DIM], gathered[HEAD_DIM : HEAD_DIM + 1]
                if earlier is not None:
                    factor = jnp.exp2(before - peak)
                    numer = numer + factor * earlier[0][local_rows(pair, half), :]
                    total = total + factor * earlier[2][local_head(pair, half), :]
                start = pl.multiple_of(column(pair) + half * HEAD_DIM, HEAD_DIM)
                rows = pl.ds(start, HEAD_DIM)
                if final:
                    attended_ref[half] = (numer * (1.0 / total)).astype(jnp.bfloat16)
                    if half == 1:
                        both = attended_ref[...].reshape(PAIR, tokens)
                        out_ref[:, pl.ds(column(pair), PAIR)] = both.T
                else:
                    head = pl.ds(2 * pair + half, 1)
                    numer_out[rows, :] = numer
                    peak_out[head, :] = peak
                    total_out[head, :] = total

            def overlap(pair, half, running, values_t, next_pair, next_half):
                peak = jnp.max(running, axis=0, keepdims=True) * scale
                before = None
                if earlier is not None:
                    before = earlier[1][local_head(pair, half), :]
                    peak = jnp.maximum(peak, before)
                weighted = jnp.concatenate(
                    [values_t[half * HEAD_DIM : (half + 1) * HEAD_DIM], ones], axis=0
                )
                if next_half == 0:
                    load(next_pair)
                query_head = head_queries(next_half)
                next_running, gathered = None, None
                for step in range(max(len(key_chunks), len(value_chunks))):
                    if step < len(key_chunks):
                        next_running = score(
                            next_half, query_head, key_chunks[step], next_running
                        )
                    if step < len(value_chunks):
                        gathered = weigh(half, peak, weighted, value_chunks[step], gathered)
                finish(pair, half, gathered, peak, before)
                return next_running

            def pair_step(pair, running):
                at = 0
                for (_, ref, shift), size in zip(set_refs, sizes):
                    value_ref[at : at + size, :] = ref[:, columns(pair, shift)]
                    at += size
                if padded > keys:
                    value_ref[keys:, :] = jnp.zeros((padded - keys, PAIR), jnp.bfloat16)
                values_t = value_ref[...].T
                running = overlap(pair, 0, running, values_t, pair, 1)
                later = jnp.minimum(pair + 1, last_pair - 1)
                return overlap(pair, 1, running, values_t, later, 0)

            load(first_pair)
            first_head = head_queries(0)
            running = None
            for chunk in key_chunks:
                running = score(0, first_head, chunk, running)
            lax.fori_loop(first_pair, last_pair, pair_step, running, unroll=UNROLL)

        for group in range(groups):
            one_group(
                group * pairs // groups,
                (group + 1) * pairs // groups,
                state_refs[group] if states else None,
            )
        if final:
            copies = []
            for at, low in enumerate(range(0, tokens, LANES)):
                rows = slice(low, low + LANES)
                result_ref[rows, :] = jnp.dot(
                    out_ref[rows, :], weight_ref[...], preferred_element_type=jnp.float32
                ).astype(jnp.bfloat16)
                copies.append(
                    pltpu.make_async_copy(result_ref.at[rows], out_hbm.at[rows], sems.at[at])
                )
                copies[-1].start()
            for copy in copies:
                copy.wait()

    if final:
        out_shape = jax.ShapeDtypeStruct((tokens, width), jnp.bfloat16)
    else:
        out_shape = [
            jax.ShapeDtypeStruct((width, tokens), jnp.float32),
            jax.ShapeDtypeStruct((heads, tokens), jnp.float32),
            jax.ShapeDtypeStruct((heads, tokens), jnp.float32),
        ]
    scratch = [
        pltpu.VMEM((2, padded, tokens), jnp.float32),
        pltpu.VMEM((padded, PAIR), jnp.bfloat16),
        pltpu.VMEM((padded, PAIR), jnp.bfloat16),
        pltpu.VMEM((PAIR, tokens), jnp.bfloat16),
    ]
    if row_strides is not None:
        scratch.append(pltpu.VMEM((keys, LANES), jnp.float32))
    if final:
        scratch.append(pltpu.VMEM((2, HEAD_DIM, tokens), jnp.bfloat16))
        scratch += [pltpu.VMEM((tokens, width), jnp.bfloat16)] * 2
        scratch.append(pltpu.SemaphoreType.DMA((tokens // LANES,)))
    operands = [queries]
    for block, whole in zip(sets, joined):
        operands += [block] if whole else list(block)
    whole_spec = pl.BlockSpec(memory_space=pltpu.VMEM)
    specs = [whole_spec] * len(operands)
    for array in [array for state in states for array in state] + ([out_weight] if final else []):
        operands.append(array)
        specs.append(whole_spec)
    if wait is not None:
        operands.append(wait)
        specs.append(pl.BlockSpec(memory_space=pl.ANY))
    return pl.pallas_call(
        kernel,
        out_shape=out_shape,
        in_specs=specs,
        **({"out_specs": pl.BlockSpec(memory_space=pl.ANY)} if final else {}),
        scratch_shapes=scratch,
        compiler_params=pltpu.CompilerParams(
            vmem_limit_bytes=VMEM_BYTES
        ),
        cost_estimate=pl.CostEstimate(
            flops=16 * tokens * keys * width,
            bytes_accessed=(4 * keys * width + 4 * tokens * width),
            transcendentals=tokens * keys * heads,
        ),
    )(*operands)


def local(queries, key_rows, values, out_weight):
    query_rows, own_keys, own_values = queries[0], key_rows[0], values[0]
    tokens = query_rows.shape[0]
    n_inner, n_outer = lax.axis_size("inner"), lax.axis_size("outer")
    inner_bits = n_inner.bit_length() - 1
    strides = [1 << (bit + 1) for bit in range(inner_bits + 1)]
    sends = [tokens >> (bit + 1) for bit in range(inner_bits + 1)]
    n_global = tokens // GSTEP

    rows = np.arange(0, tokens, 2)
    rank = sum((rows % s == 0).astype(np.int64) for s in strides + [GSTEP])
    order = rows[np.lexsort((rows, -rank))]
    select = np.zeros((sends[0], tokens), np.float32)
    select[np.arange(sends[0]), order] = 1.0

    def prefix_counts(level, low, high):
        return sum((order[low:high] % s == 0).astype(np.int64) for s in strides[level:])

    first_a, first_b, far = order_rows(
        jnp.asarray(select, jnp.bfloat16),
        own_keys,
        own_values,
        [(0, sends[1]), (sends[1], sends[0]), (0, n_global)],
    )

    held = {0: (first_a, 0)}
    for bit in range(1, inner_bits):
        held[1 << bit] = (across(first_a[: sends[bit]], "inner", 1 << bit), 0)
    held[1] = (across(first_a, "inner", 1), 0)
    own_set = [(own_keys, own_values)]
    own_states, moved, flip = [], far, 2
    while flip < n_outer or len(own_states) < 2:
        if flip < n_outer:
            came = across(moved, "outer", flip)
            flip *= 2
        if len(own_states) < 2:
            own_states.append(
                attend(
                    query_rows,
                    own_set,
                    row_strides=strides,
                    part=(len(own_states), 2),
                    wait=moved if own_states else None,
                )
            )
        moved = join_after([(moved, 0, moved.shape[0]), (came, 0, came.shape[0])], own_states[-1][1])
    far = moved
    n_far = far.shape[0]
    fars = {0: (far, 0)}

    def first_rows(where, count):
        return (where[0], where[1], where[1] + count)

    near_b = across(first_b, "inner", 1)
    fars[1] = (across(far, "inner", 1), 0)
    own_done = far

    known = [0] + [1 << bit for bit in range(inner_bits)]
    late = [d for d in range(n_inner) if d not in known]
    last = sends[inner_bits]
    late_sets, late_counts = [], []
    for bit in range(1, inner_bits):
        count = sends[bit]
        others = range(1, 1 << bit)
        pieces = [first_rows(held[d], count) for d in others] + [first_rows(fars[0], n_far)]
        own_done = join_after(pieces, own_done)
        came = across(own_done, "inner", 1 << bit)
        for at, d in enumerate(others):
            held[d | 1 << bit] = (came, at * count)
        fars[1 << bit] = (came, len(others) * count)
        late_sets.append(came)
        late_counts += [prefix_counts(bit, 0, count)] * len(others) + [np.ones(n_far, np.int64)]
    for d in late:
        fars[d] = (across(far, "inner", d), 0)
    late_sets += [fars[d][0] for d in [0, 1] + late]
    late_counts.append(np.ones(n_far * (2 + len(late)), np.int64))

    early_sets = [held[1][0], near_b] + [held[d][0] for d in known[2:]]
    early_counts = [prefix_counts(0, 0, sends[0])]
    early_counts += [prefix_counts(bit, 0, sends[bit]) for bit in range(1, inner_bits)]
    state = attend(query_rows, early_sets, np.concatenate(early_counts), states=own_states)

    pieces = [first_rows(held[d], last) for d in range(n_inner)]
    pieces += [first_rows(fars[d], n_far) for d in range(n_inner)]
    core = across(join_after(pieces, state[1]), "outer", 1)
    state = attend(query_rows, late_sets, np.concatenate(late_counts), states=[state])
    result = attend(query_rows, [core], states=[state], out_weight=out_weight)
    return result[None]


def solution(mesh):
    placed = (P("outer", "inner", None), P("outer", "inner", None), P("outer", "inner", None), P())
    return jax.shard_map(
        local, mesh=mesh, in_specs=placed, out_specs=P("outer", "inner", None), check_vma=False
    )
```

```python
import math

import jax
import jax.numpy as jnp
import numpy as np
from jax import lax
from jax.experimental import pallas as pl
from jax.experimental.pallas import tpu as pltpu
from jax.sharding import PartitionSpec as P

HEAD_DIM = 64
GSTEP = 64
PAIR = 2 * HEAD_DIM
CHUNK = 256
KEY_CHUNK = 512
UNROLL = 3
LANES = 128
LOG2E = math.log2(math.e)
VMEM_BYTES = 16 * 1024 * 1024
JOIN_VMEM_BYTES = 8 * 1024 * 1024
FETCH_VMEM_BYTES = 60 * 1024 * 1024


def across(block, axis, flip):
    return lax.ppermute(block, axis, [(i, i ^ flip) for i in range(lax.axis_size(axis))])


def after(block, *others):
    return lax.optimization_barrier((block, *others))[0]


def join_after(pieces, other):
    width = pieces[0][0].shape[1]
    total = sum(high - low for _, low, high in pieces)

    def kernel(*refs):
        out_ref, at = refs[-1], 0
        for ref, (_, low, high) in zip(refs, pieces):
            out_ref[at : at + high - low, :] = ref[low:high, :]
            at += high - low

    return pl.pallas_call(
        kernel,
        out_shape=jax.ShapeDtypeStruct((total, width), pieces[0][0].dtype),
        in_specs=[pl.BlockSpec(memory_space=pltpu.VMEM)] * len(pieces)
        + [pl.BlockSpec(memory_space=pl.ANY)],
        compiler_params=pltpu.CompilerParams(vmem_limit_bytes=JOIN_VMEM_BYTES),
        cost_estimate=pl.CostEstimate(
            flops=0, bytes_accessed=4 * total * width, transcendentals=0
        ),
    )(*[block for block, _, _ in pieces], other)


def runs(counts):
    found = []
    for at, value in enumerate(counts):
        if found and found[-1][2] == value:
            found[-1][1] = at + 1
        else:
            found.append([at, at + 1, int(value)])
    return [tuple(entry) for entry in found]


def order_rows(select, key_rows, values, prefixes):
    tokens, width = key_rows.shape

    def kernel(select_hbm, key_hbm, value_hbm, *refs):
        out_refs, (select_ref, row_ref, sems) = refs[: len(prefixes)], refs[len(prefixes) :]
        copies = [
            pltpu.make_async_copy(select_hbm, select_ref, sems.at[0]),
            pltpu.make_async_copy(key_hbm, row_ref.at[0], sems.at[1]),
            pltpu.make_async_copy(value_hbm, row_ref.at[1], sems.at[2]),
        ]
        for copy in copies:
            copy.start()
        copies[0].wait()
        for half in range(2):
            copies[1 + half].wait()
            moved = jnp.dot(
                select_ref[...], row_ref[half], preferred_element_type=jnp.float32
            ).astype(jnp.bfloat16)
            for (low, high), out_ref in zip(prefixes, out_refs):
                out_ref[:, half * width : (half + 1) * width] = moved[low:high]

    return pl.pallas_call(
        kernel,
        out_shape=[
            jax.ShapeDtypeStruct((high - low, 2 * width), jnp.bfloat16) for low, high in prefixes
        ],
        in_specs=[pl.BlockSpec(memory_space=pltpu.HBM)] * 3,
        scratch_shapes=[
            pltpu.VMEM(select.shape, jnp.bfloat16),
            pltpu.VMEM((2, tokens, width), jnp.bfloat16),
            pltpu.SemaphoreType.DMA((3,)),
        ],
        compiler_params=pltpu.CompilerParams(vmem_limit_bytes=FETCH_VMEM_BYTES),
        cost_estimate=pl.CostEstimate(
            flops=4 * select.size * width, bytes_accessed=6 * tokens * width, transcendentals=0
        ),
    )(select, key_rows, values)


def attend(queries, sets, counts=None, row_strides=None, part=(0, 1), states=(), out_weight=None, wait=None):
    tokens = queries.shape[0]
    full = queries.shape[1]
    width = full // part[1]
    base = part[0] * width
    heads, pairs = width // HEAD_DIM, width // PAIR
    joined = [not isinstance(block, tuple) for block in sets]
    sizes = [(block if whole else block[0]).shape[0] for block, whole in zip(sets, joined)]
    keys = sum(sizes)
    padded = -(-keys // LANES) * LANES
    row_runs = [(0, keys, 1)] if counts is None else runs(counts)
    scale = HEAD_DIM**-0.5 * LOG2E
    final = out_weight is not None
    groups = 2 if final else max(len(states), 1)

    def kernel(*refs):
        refs = list(refs)
        query_ref = refs.pop(0)
        set_refs = []
        for whole in joined:
            ref = refs.pop(0)
            set_refs.append((ref, ref, full) if whole else (ref, refs.pop(0), 0))
        state_refs = [[refs.pop(0) for _ in range(3)] for _ in states]
        if wait is not None:
            refs.pop(1 if final else 0)
        if final:
            weight_ref, out_hbm = refs.pop(0), refs.pop(0)
            attended_ref, out_ref, result_ref, sum_ref, sems = refs[-5:]
        else:
            numer_out, peak_out, total_out = [refs.pop(0) for _ in range(3)]
        score_ref, value_ref, key_ref, turned_ref = [refs.pop(0) for _ in range(4)]
        ones = jnp.ones((16, padded), jnp.bfloat16)
        if row_strides is not None:
            row = lax.broadcasted_iota(jnp.int32, (16, padded), 1)
            times = sum((row & (s - 1) == 0).astype(jnp.int32) for s in [1] + row_strides)
            ones = times.astype(jnp.float32).astype(jnp.bfloat16)
        key_chunks = [(low, min(KEY_CHUNK, keys - low)) for low in range(0, keys, KEY_CHUNK)]
        value_chunks = [(low, min(CHUNK, padded - low)) for low in range(0, padded, CHUNK)]

        def column(pair):
            return pl.multiple_of(pair * PAIR, PAIR)

        def columns(pair, shift=0):
            return pl.ds(pl.multiple_of(base + shift + pair * PAIR, PAIR), PAIR)

        def head_queries(half):
            turned = turned_ref[...]
            row = lax.broadcasted_iota(jnp.int32, turned.shape, 0)
            own = (row < HEAD_DIM) if half == 0 else (row >= HEAD_DIM)
            return jnp.where(own, turned, jnp.zeros_like(turned))

        def load(pair):
            turned_ref[...] = query_ref[:, columns(pair)].T
            at = 0
            for (ref, _, _), size in zip(set_refs, sizes):
                key_ref[at : at + size, :] = ref[:, columns(pair)]
                at += size

        def score(half, query_head, chunk, running):
            low, count = chunk
            scores = jnp.dot(
                key_ref[low : low + count, :], query_head, preferred_element_type=jnp.float32
            )
            score_ref[half, low : low + count, :] = scores
            tallest = jnp.max(scores.reshape(count // 8, 8, tokens), axis=0)
            return tallest if running is None else jnp.maximum(running, tallest)

        def weigh(half, peak, weighted, chunk, gathered):
            low, size = chunk
            high = min(low + size, keys)
            pieces = []
            for first, last, times in row_runs:
                first, last = max(first, low), min(last, high)
                if first < last:
                    offset = peak - math.log2(times)
                    pieces.append(jnp.exp2(score_ref[half, first:last, :] * scale - offset))
            if low + size > keys:
                pieces.append(jnp.zeros((low + size - keys, tokens), jnp.float32))
            probs = (pieces[0] if len(pieces) == 1 else jnp.concatenate(pieces, axis=0)).astype(
                jnp.bfloat16
            )
            product = jnp.dot(
                weighted[:, low : low + size], probs, preferred_element_type=jnp.float32
            )
            return product if gathered is None else gathered + product

        def one_group(first_pair, last_pair, earlier, first_state):
            def local_rows(pair, half):
                start = (pair - first_state) * PAIR + half * HEAD_DIM
                return pl.ds(pl.multiple_of(start, HEAD_DIM), HEAD_DIM)

            def local_head(pair, half):
                return pl.ds(2 * (pair - first_state) + half, 1)

            def finish(pair, half, gathered, peak, before):
                numer, total = gathered[:HEAD_DIM], gathered[HEAD_DIM : HEAD_DIM + 1]
                if earlier is not None:
                    factor = jnp.exp2(before - peak)
                    numer = numer + factor * earlier[0][local_rows(pair, half), :]
                    total = total + factor * earlier[2][local_head(pair, half), :]
                start = pl.multiple_of(column(pair) + half * HEAD_DIM, HEAD_DIM)
                rows = pl.ds(start, HEAD_DIM)
                if final:
                    attended_ref[half] = (numer * (1.0 / total)).astype(jnp.bfloat16)
                    if half == 1:
                        both = attended_ref[...].reshape(PAIR, tokens)
                        out_ref[:, pl.ds(column(pair), PAIR)] = both.T
                else:
                    head = pl.ds(2 * pair + half, 1)
                    numer_out[rows, :] = numer
                    peak_out[head, :] = peak
                    total_out[head, :] = total

            def overlap(pair, half, running, values_t, next_pair, next_half):
                peak = jnp.max(running, axis=0, keepdims=True) * scale
                before = None
                if earlier is not None:
                    before = earlier[1][local_head(pair, half), :]
                    peak = jnp.maximum(peak, before)
                weighted = jnp.concatenate(
                    [values_t[half * HEAD_DIM : (half + 1) * HEAD_DIM], ones], axis=0
                )
                if next_half == 0:
                    load(next_pair)
                query_head = head_queries(next_half)
                next_running, gathered = None, None
                for step in range(max(len(key_chunks), len(value_chunks))):
                    if step < len(key_chunks):
                        next_running = score(
                            next_half, query_head, key_chunks[step], next_running
                        )
                    if step < len(value_chunks):
                        gathered = weigh(half, peak, weighted, value_chunks[step], gathered)
                finish(pair, half, gathered, peak, before)
                return next_running

            def pair_step(pair, running):
                at = 0
                for (_, ref, shift), size in zip(set_refs, sizes):
                    value_ref[at : at + size, :] = ref[:, columns(pair, shift)]
                    at += size
                if padded > keys:
                    value_ref[keys:, :] = jnp.zeros((padded - keys, PAIR), jnp.bfloat16)
                values_t = value_ref[...].T
                if row_strides is not None:
                    values_t = values_t * ones[:1]
                running = overlap(pair, 0, running, values_t, pair, 1)
                later = jnp.minimum(pair + 1, last_pair - 1)
                return overlap(pair, 1, running, values_t, later, 0)

            load(first_pair)
            first_head = head_queries(0)
            running = None
            for chunk in key_chunks:
                running = score(0, first_head, chunk, running)
            lax.fori_loop(first_pair, last_pair, pair_step, running, unroll=UNROLL)

        for group in range(groups):
            low, high = group * pairs // groups, (group + 1) * pairs // groups
            shared = len(states) == 1
            one_group(
                low, high, state_refs[0 if shared else group] if states else None, 0 if shared else low
            )
            if final and group == 0:
                sum_ref[...] = jnp.dot(
                    out_ref[:, : high * PAIR],
                    weight_ref[: high * PAIR, :],
                    preferred_element_type=jnp.float32,
                )
        if final:
            copies, split = [], pairs // groups * PAIR
            for at, low in enumerate(range(0, tokens, LANES)):
                rows = slice(low, low + LANES)
                result_ref[rows, :] = (
                    sum_ref[rows, :]
                    + jnp.dot(
                        out_ref[rows, split:],
                        weight_ref[split:, :],
                        preferred_element_type=jnp.float32,
                    )
                ).astype(jnp.bfloat16)
                copies.append(
                    pltpu.make_async_copy(result_ref.at[rows], out_hbm.at[rows], sems.at[at])
                )
                copies[-1].start()
            for copy in copies:
                copy.wait()

    if final:
        out_shape = jax.ShapeDtypeStruct((tokens, width), jnp.bfloat16)
    else:
        out_shape = [
            jax.ShapeDtypeStruct((width, tokens), jnp.float32),
            jax.ShapeDtypeStruct((heads, tokens), jnp.float32),
            jax.ShapeDtypeStruct((heads, tokens), jnp.float32),
        ]
    scratch = [
        pltpu.VMEM((2, padded, tokens), jnp.float32),
        pltpu.VMEM((padded, PAIR), jnp.bfloat16),
        pltpu.VMEM((padded, PAIR), jnp.bfloat16),
        pltpu.VMEM((PAIR, tokens), jnp.bfloat16),
    ]
    if final:
        scratch.append(pltpu.VMEM((2, HEAD_DIM, tokens), jnp.bfloat16))
        scratch += [pltpu.VMEM((tokens, width), jnp.bfloat16)] * 2
        scratch.append(pltpu.VMEM((tokens, width), jnp.float32))
        scratch.append(pltpu.SemaphoreType.DMA((tokens // LANES,)))
    operands = [queries]
    for block, whole in zip(sets, joined):
        operands += [block] if whole else list(block)
    whole_spec = pl.BlockSpec(memory_space=pltpu.VMEM)
    specs = [whole_spec] * len(operands)
    for array in [array for state in states for array in state] + ([out_weight] if final else []):
        operands.append(array)
        specs.append(whole_spec)
    if wait is not None:
        operands.append(wait)
        specs.append(pl.BlockSpec(memory_space=pl.ANY))
    return pl.pallas_call(
        kernel,
        out_shape=out_shape,
        in_specs=specs,
        **({"out_specs": pl.BlockSpec(memory_space=pl.ANY)} if final else {}),
        scratch_shapes=scratch,
        compiler_params=pltpu.CompilerParams(
            vmem_limit_bytes=VMEM_BYTES
        ),
        cost_estimate=pl.CostEstimate(
            flops=16 * tokens * keys * width,
            bytes_accessed=(4 * keys * width + 4 * tokens * width),
            transcendentals=tokens * keys * heads,
        ),
    )(*operands)


def local(queries, key_rows, values, out_weight):
    query_rows, own_keys, own_values = queries[0], key_rows[0], values[0]
    tokens = query_rows.shape[0]
    n_inner, n_outer = lax.axis_size("inner"), lax.axis_size("outer")
    inner_bits = n_inner.bit_length() - 1
    strides = [1 << (bit + 1) for bit in range(inner_bits + 1)]
    sends = [tokens >> (bit + 1) for bit in range(inner_bits + 1)]
    n_global = tokens // GSTEP

    rows = np.arange(0, tokens, 2)
    rank = sum((rows % s == 0).astype(np.int64) for s in strides + [GSTEP])
    order = rows[np.lexsort((rows, -rank))]
    select = np.zeros((sends[0], tokens), np.float32)
    select[np.arange(sends[0]), order] = 1.0

    def prefix_counts(level, low, high):
        return sum((order[low:high] % s == 0).astype(np.int64) for s in strides[level:])

    first_a, first_b, far = order_rows(
        jnp.asarray(select, jnp.bfloat16),
        own_keys,
        own_values,
        [(0, sends[1]), (sends[1], sends[0]), (0, n_global)],
    )

    held = {0: (first_a, 0)}
    for bit in range(1, inner_bits):
        held[1 << bit] = (across(first_a[: sends[bit]], "inner", 1 << bit), 0)
    held[1] = (across(first_a, "inner", 1), 0)
    own_set = [(own_keys, own_values)]
    own_states, moved, flip = [], far, 2
    while flip < n_outer or len(own_states) < 2:
        if flip < n_outer:
            came = across(moved, "outer", flip)
            flip *= 2
        if len(own_states) < 2:
            own_states.append(
                attend(
                    query_rows,
                    own_set,
                    row_strides=strides,
                    part=(len(own_states), 2),
                    wait=moved if own_states else None,
                )
            )
        moved = join_after([(moved, 0, moved.shape[0]), (came, 0, came.shape[0])], own_states[-1][1])
    far = moved
    n_far = far.shape[0]
    fars = {0: (far, 0)}

    def first_rows(where, count):
        return (where[0], where[1], where[1] + count)

    near_b = across(first_b, "inner", 1)
    fars[1] = (across(far, "inner", 1), 0)
    own_done = far

    known = [0] + [1 << bit for bit in range(inner_bits)]
    late = [d for d in range(n_inner) if d not in known]
    last = sends[inner_bits]
    late_sets, late_counts = [], []
    for bit in range(1, inner_bits):
        count = sends[bit]
        others = range(1, 1 << bit)
        pieces = [first_rows(held[d], count) for d in others] + [first_rows(fars[0], n_far)]
        own_done = join_after(pieces, own_done)
        came = across(own_done, "inner", 1 << bit)
        for at, d in enumerate(others):
            held[d | 1 << bit] = (came, at * count)
        fars[1 << bit] = (came, len(others) * count)
        late_sets.append(came)
        late_counts += [prefix_counts(bit, 0, count)] * len(others) + [np.ones(n_far, np.int64)]
    for d in late:
        fars[d] = (across(far, "inner", d), 0)
    late_sets += [fars[d][0] for d in [0, 1] + late]
    late_counts.append(np.ones(n_far * (2 + len(late)), np.int64))

    early_sets = [held[1][0], near_b] + [held[d][0] for d in known[2:]]
    early_counts = [prefix_counts(0, 0, sends[0])]
    early_counts += [prefix_counts(bit, 0, sends[bit]) for bit in range(1, inner_bits)]
    state = attend(query_rows, early_sets, np.concatenate(early_counts), states=own_states)

    pieces = [first_rows(held[d], last) for d in range(n_inner)]
    pieces += [first_rows(fars[d], n_far) for d in range(n_inner)]
    core = across(join_after(pieces, state[1]), "outer", 1)
    state = attend(query_rows, late_sets, np.concatenate(late_counts), states=[state])
    result = attend(query_rows, [core], states=[state], out_weight=out_weight)
    return result[None]


def solution(mesh):
    placed = (P("outer", "inner", None), P("outer", "inner", None), P("outer", "inner", None), P())
    return jax.shard_map(
        local, mesh=mesh, in_specs=placed, out_specs=P("outer", "inner", None), check_vma=False
    )
```

```python
import math

import jax
import jax.numpy as jnp
import numpy as np
from jax import lax
from jax.experimental import pallas as pl
from jax.experimental.pallas import tpu as pltpu
from jax.sharding import PartitionSpec as P

HEAD_DIM = 64
GSTEP = 64
PAIR = 2 * HEAD_DIM
CHUNK = 256
KEY_CHUNK = 512
UNROLL = 3
OWN_PARTS = 3
PIECES = 4
LANES = 128
LOG2E = math.log2(math.e)
VMEM_BYTES = 16 * 1024 * 1024
JOIN_VMEM_BYTES = 8 * 1024 * 1024
FETCH_VMEM_BYTES = 60 * 1024 * 1024


def across(block, axis, flip):
    return lax.ppermute(block, axis, [(i, i ^ flip) for i in range(lax.axis_size(axis))])


def after(block, *others):
    return lax.optimization_barrier((block, *others))[0]


def join_after(pieces, other):
    width = pieces[0][0].shape[1]
    total = sum(high - low for _, low, high in pieces)

    def kernel(*refs):
        out_ref, at = refs[-1], 0
        for ref, (_, low, high) in zip(refs, pieces):
            out_ref[at : at + high - low, :] = ref[low:high, :]
            at += high - low

    return pl.pallas_call(
        kernel,
        out_shape=jax.ShapeDtypeStruct((total, width), pieces[0][0].dtype),
        in_specs=[pl.BlockSpec(memory_space=pltpu.VMEM)] * len(pieces)
        + [pl.BlockSpec(memory_space=pl.ANY)],
        compiler_params=pltpu.CompilerParams(vmem_limit_bytes=JOIN_VMEM_BYTES),
        cost_estimate=pl.CostEstimate(
            flops=0, bytes_accessed=4 * total * width, transcendentals=0
        ),
    )(*[block for block, _, _ in pieces], other)


def runs(counts):
    found = []
    for at, value in enumerate(counts):
        if found and found[-1][2] == value:
            found[-1][1] = at + 1
        else:
            found.append([at, at + 1, int(value)])
    return [tuple(entry) for entry in found]


def row_copies(source, target, sems):
    count = source.shape[0] // PIECES
    copies = []
    for at in range(PIECES):
        rows = pl.ds(at * count, count)
        copies.append(pltpu.make_async_copy(source.at[rows], target.at[rows], sems.at[at]))
        copies[-1].start()
    return copies


def fetch_rows(source, target, sems):
    for copy in row_copies(source, target, sems):
        copy.wait()


def order_rows(select, key_rows, values, prefixes):
    tokens, width = key_rows.shape

    def kernel(select_hbm, key_hbm, value_hbm, *refs):
        out_refs, (select_ref, row_ref, sems) = refs[: len(prefixes)], refs[len(prefixes) :]
        sources = (select_hbm, key_hbm, value_hbm)
        targets = (select_ref, row_ref.at[0], row_ref.at[1])
        copies = [
            row_copies(source, target, sems.at[at])
            for at, (source, target) in enumerate(zip(sources, targets))
        ]
        for copy in copies[0]:
            copy.wait()
        for half in range(2):
            for copy in copies[1 + half]:
                copy.wait()
            moved = jnp.dot(
                select_ref[...], row_ref[half], preferred_element_type=jnp.float32
            ).astype(jnp.bfloat16)
            for (low, high), out_ref in zip(prefixes, out_refs):
                out_ref[:, half * width : (half + 1) * width] = moved[low:high]

    return pl.pallas_call(
        kernel,
        out_shape=[
            jax.ShapeDtypeStruct((high - low, 2 * width), jnp.bfloat16) for low, high in prefixes
        ],
        in_specs=[pl.BlockSpec(memory_space=pltpu.HBM)] * 3,
        scratch_shapes=[
            pltpu.VMEM(select.shape, jnp.bfloat16),
            pltpu.VMEM((2, tokens, width), jnp.bfloat16),
            pltpu.SemaphoreType.DMA((3, PIECES)),
        ],
        compiler_params=pltpu.CompilerParams(vmem_limit_bytes=FETCH_VMEM_BYTES),
        cost_estimate=pl.CostEstimate(
            flops=4 * select.size * width, bytes_accessed=6 * tokens * width, transcendentals=0
        ),
    )(select, key_rows, values)


def attend(queries, sets, counts=None, row_strides=None, part=(0, 1), states=(), out_weight=None, wait=None):
    tokens = queries.shape[0]
    full = queries.shape[1]
    width = full // part[1]
    base = part[0] * width
    heads, pairs = width // HEAD_DIM, width // PAIR
    joined = [not isinstance(block, tuple) for block in sets]
    sizes = [(block if whole else block[0]).shape[0] for block, whole in zip(sets, joined)]
    keys = sum(sizes)
    padded = -(-keys // LANES) * LANES
    row_runs = [(0, keys, 1)] if counts is None else runs(counts)
    scale = HEAD_DIM**-0.5 * LOG2E
    final = out_weight is not None
    groups = max(len(states), 1)

    def kernel(*refs):
        refs = list(refs)
        query_ref = refs.pop(0)
        set_refs = []
        for whole in joined:
            ref = refs.pop(0)
            set_refs.append((ref, ref, full) if whole else (ref, refs.pop(0), 0))
        state_refs = [[refs.pop(0) for _ in range(3)] for _ in states]
        if wait is not None:
            refs.pop(1 if final else 0)
        if final:
            weight_ref, out_hbm = refs.pop(0), refs.pop(0)
            attended_ref, out_ref, result_ref, sems = refs[-4:]
        else:
            numer_out, peak_out, total_out = [refs.pop(0) for _ in range(3)]
        score_ref, value_ref, key_ref, turned_ref = [refs.pop(0) for _ in range(4)]
        ones = jnp.ones((16, padded), jnp.bfloat16)
        if row_strides is not None:
            row = lax.broadcasted_iota(jnp.int32, (16, padded), 1)
            times = sum((row & (s - 1) == 0).astype(jnp.int32) for s in [1] + row_strides)
            ones = times.astype(jnp.float32).astype(jnp.bfloat16)
        key_chunks = [(low, min(KEY_CHUNK, keys - low)) for low in range(0, keys, KEY_CHUNK)]
        value_chunks = [(low, min(CHUNK, padded - low)) for low in range(0, padded, CHUNK)]

        def column(pair):
            return pl.multiple_of(pair * PAIR, PAIR)

        def columns(pair, shift=0):
            return pl.ds(pl.multiple_of(base + shift + pair * PAIR, PAIR), PAIR)

        def head_queries(half):
            turned = turned_ref[...]
            row = lax.broadcasted_iota(jnp.int32, turned.shape, 0)
            own = (row < HEAD_DIM) if half == 0 else (row >= HEAD_DIM)
            return jnp.where(own, turned, jnp.zeros_like(turned))

        def load(pair):
            turned_ref[...] = query_ref[:, columns(pair)].T
            at = 0
            for (ref, _, _), size in zip(set_refs, sizes):
                key_ref[at : at + size, :] = ref[:, columns(pair)]
                at += size

        def score(half, query_head, chunk, running):
            low, count = chunk
            scores = jnp.dot(
                key_ref[low : low + count, :], query_head, preferred_element_type=jnp.float32
            )
            score_ref[half, low : low + count, :] = scores
            tallest = jnp.max(scores.reshape(count // 8, 8, tokens), axis=0)
            return tallest if running is None else jnp.maximum(running, tallest)

        def weigh(half, peak, weighted, chunk, gathered):
            low, size = chunk
            high = min(low + size, keys)
            pieces = []
            for first, last, times in row_runs:
                first, last = max(first, low), min(last, high)
                if first < last:
                    offset = peak - math.log2(times)
                    pieces.append(jnp.exp2(score_ref[half, first:last, :] * scale - offset))
            if low + size > keys:
                pieces.append(jnp.zeros((low + size - keys, tokens), jnp.float32))
            probs = (pieces[0] if len(pieces) == 1 else jnp.concatenate(pieces, axis=0)).astype(
                jnp.bfloat16
            )
            product = jnp.dot(
                weighted[:, low : low + size], probs, preferred_element_type=jnp.float32
            )
            return product if gathered is None else gathered + product

        def one_group(first_pair, last_pair, earlier, first_state):
            def local_rows(pair, half):
                start = (pair - first_state) * PAIR + half * HEAD_DIM
                return pl.ds(pl.multiple_of(start, HEAD_DIM), HEAD_DIM)

            def local_head(pair, half):
                return pl.ds(2 * (pair - first_state) + half, 1)

            def finish(pair, half, gathered, peak, before):
                numer, total = gathered[:HEAD_DIM], gathered[HEAD_DIM : HEAD_DIM + 1]
                if earlier is not None:
                    factor = jnp.exp2(before - peak)
                    numer = numer + factor * earlier[0][local_rows(pair, half), :]
                    total = total + factor * earlier[2][local_head(pair, half), :]
                start = pl.multiple_of(column(pair) + half * HEAD_DIM, HEAD_DIM)
                rows = pl.ds(start, HEAD_DIM)
                if final:
                    attended_ref[half] = (numer * (1.0 / total)).astype(jnp.bfloat16)
                    if half == 1:
                        both = attended_ref[...].reshape(PAIR, tokens)
                        out_ref[:, pl.ds(column(pair), PAIR)] = both.T
                else:
                    head = pl.ds(2 * pair + half, 1)
                    numer_out[rows, :] = numer
                    peak_out[head, :] = peak
                    total_out[head, :] = total

            def overlap(pair, half, running, values_t, next_pair, next_half):
                peak = jnp.max(running, axis=0, keepdims=True) * scale
                before = None
                if earlier is not None:
                    before = earlier[1][local_head(pair, half), :]
                    peak = jnp.maximum(peak, before)
                weighted = jnp.concatenate(
                    [values_t[half * HEAD_DIM : (half + 1) * HEAD_DIM], ones], axis=0
                )
                if next_half == 0:
                    load(next_pair)
                query_head = head_queries(next_half)
                next_running, gathered = None, None
                for step in range(max(len(key_chunks), len(value_chunks))):
                    if step < len(key_chunks):
                        next_running = score(
                            next_half, query_head, key_chunks[step], next_running
                        )
                    if step < len(value_chunks):
                        gathered = weigh(half, peak, weighted, value_chunks[step], gathered)
                finish(pair, half, gathered, peak, before)
                return next_running

            def pair_step(pair, running):
                at = 0
                for (_, ref, shift), size in zip(set_refs, sizes):
                    value_ref[at : at + size, :] = ref[:, columns(pair, shift)]
                    at += size
                if padded > keys:
                    value_ref[keys:, :] = jnp.zeros((padded - keys, PAIR), jnp.bfloat16)
                values_t = value_ref[...].T
                if row_strides is not None:
                    values_t = values_t * ones[:1]
                running = overlap(pair, 0, running, values_t, pair, 1)
                later = jnp.minimum(pair + 1, last_pair - 1)
                return overlap(pair, 1, running, values_t, later, 0)

            load(first_pair)
            first_head = head_queries(0)
            running = None
            for chunk in key_chunks:
                running = score(0, first_head, chunk, running)
            lax.fori_loop(first_pair, last_pair, pair_step, running, unroll=min(UNROLL, last_pair - first_pair))

        for group in range(groups):
            low, high = group * pairs // groups, (group + 1) * pairs // groups
            shared = len(states) == 1
            one_group(
                low, high, state_refs[0 if shared else group] if states else None, 0 if shared else low
            )
        if final:
            copies = []
            for at, low in enumerate(range(0, tokens, LANES)):
                rows = slice(low, low + LANES)
                result_ref[rows, :] = jnp.dot(
                    out_ref[rows, :], weight_ref[...], preferred_element_type=jnp.float32
                ).astype(jnp.bfloat16)
                copies.append(
                    pltpu.make_async_copy(result_ref.at[rows], out_hbm.at[rows], sems.at[at])
                )
                copies[-1].start()
            for copy in copies:
                copy.wait()

    if final:
        out_shape = jax.ShapeDtypeStruct((tokens, width), jnp.bfloat16)
    else:
        out_shape = [
            jax.ShapeDtypeStruct((width, tokens), jnp.float32),
            jax.ShapeDtypeStruct((heads, tokens), jnp.float32),
            jax.ShapeDtypeStruct((heads, tokens), jnp.float32),
        ]
    scratch = [
        pltpu.VMEM((2, padded, tokens), jnp.float32),
        pltpu.VMEM((padded, PAIR), jnp.bfloat16),
        pltpu.VMEM((padded, PAIR), jnp.bfloat16),
        pltpu.VMEM((PAIR, tokens), jnp.bfloat16),
    ]
    if final:
        scratch.append(pltpu.VMEM((2, HEAD_DIM, tokens), jnp.bfloat16))
        scratch += [pltpu.VMEM((tokens, width), jnp.bfloat16)] * 2
        scratch.append(pltpu.SemaphoreType.DMA((tokens // LANES,)))
    operands = [queries]
    for block, whole in zip(sets, joined):
        operands += [block] if whole else list(block)
    whole_spec = pl.BlockSpec(memory_space=pltpu.VMEM)
    specs = [whole_spec] * len(operands)
    for array in [array for state in states for array in state] + ([out_weight] if final else []):
        operands.append(array)
        specs.append(whole_spec)
    if wait is not None:
        operands.append(wait)
        specs.append(pl.BlockSpec(memory_space=pl.ANY))
    return pl.pallas_call(
        kernel,
        out_shape=out_shape,
        in_specs=specs,
        **({"out_specs": pl.BlockSpec(memory_space=pl.ANY)} if final else {}),
        scratch_shapes=scratch,
        compiler_params=pltpu.CompilerParams(
            vmem_limit_bytes=VMEM_BYTES
        ),
        cost_estimate=pl.CostEstimate(
            flops=16 * tokens * keys * width,
            bytes_accessed=(4 * keys * width + 4 * tokens * width),
            transcendentals=tokens * keys * heads,
        ),
    )(*operands)


def local(queries, key_rows, values, out_weight):
    query_rows, own_keys, own_values = queries[0], key_rows[0], values[0]
    tokens = query_rows.shape[0]
    n_inner, n_outer = lax.axis_size("inner"), lax.axis_size("outer")
    inner_bits = n_inner.bit_length() - 1
    strides = [1 << (bit + 1) for bit in range(inner_bits + 1)]
    sends = [tokens >> (bit + 1) for bit in range(inner_bits + 1)]
    n_global = tokens // GSTEP

    rows = np.arange(0, tokens, 2)
    rank = sum((rows % s == 0).astype(np.int64) for s in strides + [GSTEP])
    order = rows[np.lexsort((rows, -rank))]
    select = np.zeros((sends[0], tokens), np.float32)
    select[np.arange(sends[0]), order] = 1.0

    def prefix_counts(level, low, high):
        return sum((order[low:high] % s == 0).astype(np.int64) for s in strides[level:])

    first_a, first_b, far = order_rows(
        jnp.asarray(select, jnp.bfloat16),
        own_keys,
        own_values,
        [(0, sends[1]), (sends[1], sends[0]), (0, n_global)],
    )

    held = {0: (first_a, 0)}
    for bit in range(1, inner_bits):
        held[1 << bit] = (across(first_a[: sends[bit]], "inner", 1 << bit), 0)
    held[1] = (across(first_a, "inner", 1), 0)
    own_set = [(own_keys, own_values)]
    own_states, moved, flip = [], far, 2

    def own_part(wait):
        part = (len(own_states), OWN_PARTS)
        own_states.append(
            attend(query_rows, own_set, row_strides=strides, part=part, wait=wait)
        )

    while flip < n_outer:
        came = across(moved, "outer", flip)
        if len(own_states) < OWN_PARTS - 1:
            own_part(moved if own_states else None)
        moved = join_after([(moved, 0, moved.shape[0]), (came, 0, came.shape[0])], own_states[-1][1])
        flip *= 2
    far = moved
    n_far = far.shape[0]
    fars = {0: (far, 0)}

    def first_rows(where, count):
        return (where[0], where[1], where[1] + count)

    pieces = [first_rows((first_b, 0), sends[0] - sends[1]), first_rows(fars[0], n_far)]
    near_b = across(join_after(pieces, far), "inner", 1)
    fars[1] = (near_b, sends[0] - sends[1])
    own_done = far

    known = [0] + [1 << bit for bit in range(inner_bits)]
    late = [d for d in range(n_inner) if d not in known]
    last = sends[inner_bits]
    late_sets = [near_b]
    late_counts = [prefix_counts(0, sends[1], sends[0]), np.ones(n_far, np.int64)]
    for bit in range(1, inner_bits):
        count = sends[bit]
        others = range(1, 1 << bit)
        pieces = [first_rows(held[d], count) for d in others] + [first_rows(fars[0], n_far)]
        own_done = join_after(pieces, own_done)
        came = across(own_done, "inner", 1 << bit)
        for at, d in enumerate(others):
            held[d | 1 << bit] = (came, at * count)
        fars[1 << bit] = (came, len(others) * count)
        late_sets.append(came)
        late_counts += [prefix_counts(bit, 0, count)] * len(others) + [np.ones(n_far, np.int64)]
    for d in late:
        fars[d] = (across(far, "inner", d), 0)
    late_sets += [fars[d][0] for d in late]
    late_counts.append(np.ones(n_far * len(late), np.int64))

    moved = join_after([first_rows(held[d], last) for d in known], own_done)
    early_core = across(moved, "outer", 1)
    while len(own_states) < OWN_PARTS:
        own_part(moved)

    early_sets = [held[d][0] for d in known[1:]] + [early_core, far]
    early_counts = [prefix_counts(0, 0, sends[1])]
    early_counts += [prefix_counts(bit, 0, sends[bit]) for bit in range(1, inner_bits)]
    early_counts.append(np.ones(early_core.shape[0] + n_far, np.int64))
    state = attend(query_rows, early_sets, np.concatenate(early_counts), states=own_states)

    pieces = [first_rows(held[d], last) for d in late]
    pieces += [first_rows(fars[d], n_far) for d in range(n_inner)]
    core = across(join_after(pieces, state[1]), "outer", 1)
    state = attend(query_rows, late_sets, np.concatenate(late_counts), states=[state])
    result = attend(query_rows, [core], states=[state], out_weight=out_weight)
    return result[None]


def solution(mesh):
    placed = (P("outer", "inner", None), P("outer", "inner", None), P("outer", "inner", None), P())
    return jax.shard_map(
        local, mesh=mesh, in_specs=placed, out_specs=P("outer", "inner", None), check_vma=False
    )
```

```python
import math

import jax
import jax.numpy as jnp
import numpy as np
from jax import lax
from jax.experimental import pallas as pl
from jax.experimental.pallas import tpu as pltpu
from jax.sharding import PartitionSpec as P

HEAD_DIM = 64
GSTEP = 64
PAIR = 2 * HEAD_DIM
CHUNK = 256
KEY_CHUNK = 512
LANES = 128
LOG2E = math.log2(math.e)
VMEM_BYTES = 16 * 1024 * 1024
JOIN_VMEM_BYTES = 8 * 1024 * 1024
FETCH_VMEM_BYTES = 60 * 1024 * 1024


def across(block, axis, flip):
    return lax.ppermute(block, axis, [(i, i ^ flip) for i in range(lax.axis_size(axis))])


def after(block, *others):
    return lax.optimization_barrier((block, *others))[0]


def join_after(pieces, other):
    width = pieces[0][0].shape[1]
    total = sum(high - low for _, low, high in pieces)

    def kernel(*refs):
        out_ref, at = refs[-1], 0
        for ref, (_, low, high) in zip(refs, pieces):
            out_ref[at : at + high - low, :] = ref[low:high, :]
            at += high - low

    return pl.pallas_call(
        kernel,
        out_shape=jax.ShapeDtypeStruct((total, width), pieces[0][0].dtype),
        in_specs=[pl.BlockSpec(memory_space=pltpu.VMEM)] * len(pieces)
        + [pl.BlockSpec(memory_space=pl.ANY)],
        compiler_params=pltpu.CompilerParams(vmem_limit_bytes=JOIN_VMEM_BYTES),
        cost_estimate=pl.CostEstimate(
            flops=0, bytes_accessed=4 * total * width, transcendentals=0
        ),
    )(*[block for block, _, _ in pieces], other)


def runs(counts):
    found = []
    for at, value in enumerate(counts):
        if found and found[-1][2] == value:
            found[-1][1] = at + 1
        else:
            found.append([at, at + 1, int(value)])
    return [tuple(entry) for entry in found]


def order_rows(select, key_rows, values, prefixes):
    tokens, width = key_rows.shape

    def kernel(select_hbm, key_hbm, value_hbm, *refs):
        out_refs, (select_ref, row_ref, sems) = refs[: len(prefixes)], refs[len(prefixes) :]
        copies = [
            pltpu.make_async_copy(select_hbm, select_ref, sems.at[0]),
            pltpu.make_async_copy(key_hbm, row_ref.at[0], sems.at[1]),
            pltpu.make_async_copy(value_hbm, row_ref.at[1], sems.at[2]),
        ]
        for copy in copies:
            copy.start()
        copies[0].wait()
        for half in range(2):
            copies[1 + half].wait()
            moved = jnp.dot(
                select_ref[...], row_ref[half], preferred_element_type=jnp.float32
            ).astype(jnp.bfloat16)
            for (low, high), out_ref in zip(prefixes, out_refs):
                out_ref[:, half * width : (half + 1) * width] = moved[low:high]

    return pl.pallas_call(
        kernel,
        out_shape=[
            jax.ShapeDtypeStruct((high - low, 2 * width), jnp.bfloat16) for low, high in prefixes
        ],
        in_specs=[pl.BlockSpec(memory_space=pltpu.HBM)] * 3,
        scratch_shapes=[
            pltpu.VMEM(select.shape, jnp.bfloat16),
            pltpu.VMEM((2, tokens, width), jnp.bfloat16),
            pltpu.SemaphoreType.DMA((3,)),
        ],
        compiler_params=pltpu.CompilerParams(vmem_limit_bytes=FETCH_VMEM_BYTES),
        cost_estimate=pl.CostEstimate(
            flops=4 * select.size * width, bytes_accessed=6 * tokens * width, transcendentals=0
        ),
    )(select, key_rows, values)


def attend(queries, sets, counts=None, row_strides=None, part=(0, 1), states=(), out_weight=None, wait=None):
    tokens = queries.shape[0]
    full = queries.shape[1]
    width = full // part[1]
    base = part[0] * width
    heads, pairs = width // HEAD_DIM, width // PAIR
    joined = [not isinstance(block, tuple) for block in sets]
    sizes = [(block if whole else block[0]).shape[0] for block, whole in zip(sets, joined)]
    keys = sum(sizes)
    padded = -(-keys // LANES) * LANES
    row_runs = [(0, keys, 1)] if counts is None else runs(counts)
    scale = HEAD_DIM**-0.5 * LOG2E
    final = out_weight is not None
    groups = max(len(states), 1)

    def kernel(*refs):
        refs = list(refs)
        query_ref = refs.pop(0)
        set_refs = []
        for whole in joined:
            ref = refs.pop(0)
            set_refs.append((ref, ref, full) if whole else (ref, refs.pop(0), 0))
        state_refs = [[refs.pop(0) for _ in range(3)] for _ in states]
        if wait is not None:
            refs.pop(1 if final else 0)
        if final:
            weight_ref, out_hbm = refs.pop(0), refs.pop(0)
            attended_ref, out_ref, result_ref, sems = refs[-4:]
        else:
            numer_out, peak_out, total_out = [refs.pop(0) for _ in range(3)]
        score_ref, value_ref, key_ref, turned_ref = [refs.pop(0) for _ in range(4)]
        ones = jnp.ones((16, padded), jnp.bfloat16)
        if row_strides is not None:
            row = lax.broadcasted_iota(jnp.int32, (16, padded), 1)
            times = sum((row & (s - 1) == 0).astype(jnp.int32) for s in [1] + row_strides)
            ones = times.astype(jnp.float32).astype(jnp.bfloat16)
        key_chunks = [(low, min(KEY_CHUNK, keys - low)) for low in range(0, keys, KEY_CHUNK)]
        value_chunks = [(low, min(CHUNK, padded - low)) for low in range(0, padded, CHUNK)]

        def columns(pair, shift=0):
            return pl.ds(base + shift + pair * PAIR, PAIR)

        def head_queries(half):
            turned = turned_ref[...]
            row = lax.broadcasted_iota(jnp.int32, turned.shape, 0)
            own = (row < HEAD_DIM) if half == 0 else (row >= HEAD_DIM)
            return jnp.where(own, turned, jnp.zeros_like(turned))

        def load(pair):
            turned_ref[...] = query_ref[:, columns(pair)].T
            at = 0
            for (ref, _, _), size in zip(set_refs, sizes):
                key_ref[at : at + size, :] = ref[:, columns(pair)]
                at += size

        def score(half, query_head, chunk, running):
            low, count = chunk
            scores = jnp.dot(
                key_ref[low : low + count, :], query_head, preferred_element_type=jnp.float32
            )
            score_ref[half, low : low + count, :] = scores
            tallest = jnp.max(scores.reshape(count // 8, 8, tokens), axis=0)
            return tallest if running is None else jnp.maximum(running, tallest)

        def weigh(half, peak, weighted, chunk, gathered):
            low, size = chunk
            high = min(low + size, keys)
            pieces = []
            for first, last, times in row_runs:
                first, last = max(first, low), min(last, high)
                if first < last:
                    offset = peak - math.log2(times)
                    pieces.append(jnp.exp2(score_ref[half, first:last, :] * scale - offset))
            if low + size > keys:
                pieces.append(jnp.zeros((low + size - keys, tokens), jnp.float32))
            probs = (pieces[0] if len(pieces) == 1 else jnp.concatenate(pieces, axis=0)).astype(
                jnp.bfloat16
            )
            product = jnp.dot(
                weighted[:, low : low + size], probs, preferred_element_type=jnp.float32
            )
            return product if gathered is None else gathered + product

        def one_group(first_pair, last_pair, earlier, first_state):
            def local_rows(pair, half):
                start = (pair - first_state) * PAIR + half * HEAD_DIM
                return pl.ds(start, HEAD_DIM)

            def local_head(pair, half):
                return pl.ds(2 * (pair - first_state) + half, 1)

            def finish(pair, half, gathered, peak, before):
                numer, total = gathered[:HEAD_DIM], gathered[HEAD_DIM : HEAD_DIM + 1]
                if earlier is not None:
                    factor = jnp.exp2(before - peak)
                    numer = numer + factor * earlier[0][local_rows(pair, half), :]
                    total = total + factor * earlier[2][local_head(pair, half), :]
                rows = pl.ds(pair * PAIR + half * HEAD_DIM, HEAD_DIM)
                if final:
                    attended_ref[half] = (numer * (1.0 / total)).astype(jnp.bfloat16)
                    if half == 1:
                        both = attended_ref[...].reshape(PAIR, tokens)
                        out_ref[:, pl.ds(pair * PAIR, PAIR)] = both.T
                else:
                    head = pl.ds(2 * pair + half, 1)
                    numer_out[rows, :] = numer
                    peak_out[head, :] = peak
                    total_out[head, :] = total

            def overlap(pair, half, running, values_t, next_pair, next_half):
                peak = jnp.max(running, axis=0, keepdims=True) * scale
                before = None
                if earlier is not None:
                    before = earlier[1][local_head(pair, half), :]
                    peak = jnp.maximum(peak, before)
                weighted = jnp.concatenate(
                    [values_t[half * HEAD_DIM : (half + 1) * HEAD_DIM], ones], axis=0
                )
                ahead = next_pair < last_pair
                if ahead and next_half == 0:
                    load(next_pair)
                query_head = head_queries(next_half) if ahead else None
                next_running, gathered = None, None
                for step in range(max(len(key_chunks), len(value_chunks))):
                    if ahead and step < len(key_chunks):
                        next_running = score(
                            next_half, query_head, key_chunks[step], next_running
                        )
                    if step < len(value_chunks):
                        gathered = weigh(half, peak, weighted, value_chunks[step], gathered)
                finish(pair, half, gathered, peak, before)
                return next_running

            def pair_step(pair, running):
                at = 0
                for (_, ref, shift), size in zip(set_refs, sizes):
                    value_ref[at : at + size, :] = ref[:, columns(pair, shift)]
                    at += size
                if padded > keys:
                    value_ref[keys:, :] = jnp.zeros((padded - keys, PAIR), jnp.bfloat16)
                values_t = value_ref[...].T
                if row_strides is not None:
                    values_t = values_t * ones[:1]
                running = overlap(pair, 0, running, values_t, pair, 1)
                return overlap(pair, 1, running, values_t, pair + 1, 0)

            load(first_pair)
            first_head = head_queries(0)
            running = None
            for chunk in key_chunks:
                running = score(0, first_head, chunk, running)
            for pair in range(first_pair, last_pair):
                running = pair_step(pair, running)

        for group in range(groups):
            low, high = group * pairs // groups, (group + 1) * pairs // groups
            shared = len(states) == 1
            one_group(
                low, high, state_refs[0 if shared else group] if states else None, 0 if shared else low
            )
        if final:
            copies = []
            for at, low in enumerate(range(0, tokens, LANES)):
                rows = slice(low, low + LANES)
                result_ref[rows, :] = jnp.dot(
                    out_ref[rows, :], weight_ref[...], preferred_element_type=jnp.float32
                ).astype(jnp.bfloat16)
                copies.append(
                    pltpu.make_async_copy(result_ref.at[rows], out_hbm.at[rows], sems.at[at])
                )
                copies[-1].start()
            for copy in copies:
                copy.wait()

    if final:
        out_shape = jax.ShapeDtypeStruct((tokens, width), jnp.bfloat16)
    else:
        out_shape = [
            jax.ShapeDtypeStruct((width, tokens), jnp.float32),
            jax.ShapeDtypeStruct((heads, tokens), jnp.float32),
            jax.ShapeDtypeStruct((heads, tokens), jnp.float32),
        ]
    scratch = [
        pltpu.VMEM((2, padded, tokens), jnp.float32),
        pltpu.VMEM((padded, PAIR), jnp.bfloat16),
        pltpu.VMEM((padded, PAIR), jnp.bfloat16),
        pltpu.VMEM((PAIR, tokens), jnp.bfloat16),
    ]
    if final:
        scratch.append(pltpu.VMEM((2, HEAD_DIM, tokens), jnp.bfloat16))
        scratch += [pltpu.VMEM((tokens, width), jnp.bfloat16)] * 2
        scratch.append(pltpu.SemaphoreType.DMA((tokens // LANES,)))
    operands = [queries]
    for block, whole in zip(sets, joined):
        operands += [block] if whole else list(block)
    whole_spec = pl.BlockSpec(memory_space=pltpu.VMEM)
    specs = [whole_spec] * len(operands)
    for array in [array for state in states for array in state] + ([out_weight] if final else []):
        operands.append(array)
        specs.append(whole_spec)
    if wait is not None:
        operands.append(wait)
        specs.append(pl.BlockSpec(memory_space=pl.ANY))
    return pl.pallas_call(
        kernel,
        out_shape=out_shape,
        in_specs=specs,
        **({"out_specs": pl.BlockSpec(memory_space=pl.ANY)} if final else {}),
        scratch_shapes=scratch,
        compiler_params=pltpu.CompilerParams(
            vmem_limit_bytes=VMEM_BYTES
        ),
        cost_estimate=pl.CostEstimate(
            flops=16 * tokens * keys * width,
            bytes_accessed=(4 * keys * width + 4 * tokens * width),
            transcendentals=tokens * keys * heads,
        ),
    )(*operands)


def local(queries, key_rows, values, out_weight):
    query_rows, own_keys, own_values = queries[0], key_rows[0], values[0]
    tokens = query_rows.shape[0]
    n_inner, n_outer = lax.axis_size("inner"), lax.axis_size("outer")
    inner_bits = n_inner.bit_length() - 1
    strides = [1 << (bit + 1) for bit in range(inner_bits + 1)]
    sends = [tokens >> (bit + 1) for bit in range(inner_bits + 1)]
    n_global = tokens // GSTEP

    rows = np.arange(0, tokens, 2)
    rank = sum((rows % s == 0).astype(np.int64) for s in strides + [GSTEP])
    order = rows[np.lexsort((rows, -rank))]
    select = np.zeros((sends[0], tokens), np.float32)
    select[np.arange(sends[0]), order] = 1.0

    def prefix_counts(level, low, high):
        return sum((order[low:high] % s == 0).astype(np.int64) for s in strides[level:])

    first_a, first_b, far = order_rows(
        jnp.asarray(select, jnp.bfloat16),
        own_keys,
        own_values,
        [(0, sends[1]), (sends[1], sends[0]), (0, n_global)],
    )

    held = {0: (first_a, 0)}
    for bit in range(1, inner_bits):
        held[1 << bit] = (across(first_a[: sends[bit]], "inner", 1 << bit), 0)
    held[1] = (across(first_a, "inner", 1), 0)
    own_set = [(own_keys, own_values)]
    own_states, moved, flip = [], far, 2
    while flip < n_outer or len(own_states) < 2:
        if flip < n_outer:
            came = across(moved, "outer", flip)
            flip *= 2
        if len(own_states) < 2:
            own_states.append(
                attend(
                    query_rows,
                    own_set,
                    row_strides=strides,
                    part=(len(own_states), 2),
                    wait=moved if own_states else None,
                )
            )
        moved = join_after([(moved, 0, moved.shape[0]), (came, 0, came.shape[0])], own_states[-1][1])
    far = moved
    n_far = far.shape[0]
    fars = {0: (far, 0)}

    def first_rows(where, count):
        return (where[0], where[1], where[1] + count)

    near_b = across(first_b, "inner", 1)
    fars[1] = (across(far, "inner", 1), 0)
    own_done = far

    known = [0] + [1 << bit for bit in range(inner_bits)]
    late = [d for d in range(n_inner) if d not in known]
    last = sends[inner_bits]
    late_sets, late_counts = [], []
    for bit in range(1, inner_bits):
        count = sends[bit]
        others = range(1, 1 << bit)
        pieces = [first_rows(held[d], count) for d in others] + [first_rows(fars[0], n_far)]
        own_done = join_after(pieces, own_done)
        came = across(own_done, "inner", 1 << bit)
        for at, d in enumerate(others):
            held[d | 1 << bit] = (came, at * count)
        fars[1 << bit] = (came, len(others) * count)
        late_sets.append(came)
        late_counts += [prefix_counts(bit, 0, count)] * len(others) + [np.ones(n_far, np.int64)]
    for d in late:
        fars[d] = (across(far, "inner", d), 0)
    late_sets += [fars[d][0] for d in [0, 1] + late]
    late_counts.append(np.ones(n_far * (2 + len(late)), np.int64))

    early_sets = [held[1][0], near_b] + [held[d][0] for d in known[2:]]
    early_counts = [prefix_counts(0, 0, sends[0])]
    early_counts += [prefix_counts(bit, 0, sends[bit]) for bit in range(1, inner_bits)]
    state = attend(query_rows, early_sets, np.concatenate(early_counts), states=own_states)

    pieces = [first_rows(held[d], last) for d in range(n_inner)]
    pieces += [first_rows(fars[d], n_far) for d in range(n_inner)]
    core = across(join_after(pieces, state[1]), "outer", 1)
    state = attend(query_rows, late_sets, np.concatenate(late_counts), states=[state])
    result = attend(query_rows, [core], states=[state], out_weight=out_weight)
    return result[None]


def solution(mesh):
    placed = (P("outer", "inner", None), P("outer", "inner", None), P("outer", "inner", None), P())
    return jax.shard_map(
        local, mesh=mesh, in_specs=placed, out_specs=P("outer", "inner", None), check_vma=False
    )
```

```python
import math

import jax
import jax.numpy as jnp
import numpy as np
from jax import lax
from jax.experimental import pallas as pl
from jax.experimental.pallas import tpu as pltpu
from jax.sharding import PartitionSpec as P

HEAD_DIM = 64
GSTEP = 64
PAIR = 2 * HEAD_DIM
CHUNK = 256
KEY_CHUNK = 512
LANES = 128
LOG2E = math.log2(math.e)
VMEM_BYTES = 16 * 1024 * 1024
JOIN_VMEM_BYTES = 8 * 1024 * 1024
FETCH_VMEM_BYTES = 60 * 1024 * 1024


def across(block, axis, flip):
    return lax.ppermute(block, axis, [(i, i ^ flip) for i in range(lax.axis_size(axis))])


def after(block, *others):
    return lax.optimization_barrier((block, *others))[0]


def join_after(pieces, other):
    width = pieces[0][0].shape[1]
    total = sum(high - low for _, low, high in pieces)

    def kernel(*refs):
        out_ref, at = refs[-1], 0
        for ref, (_, low, high) in zip(refs, pieces):
            out_ref[at : at + high - low, :] = ref[low:high, :]
            at += high - low

    return pl.pallas_call(
        kernel,
        out_shape=jax.ShapeDtypeStruct((total, width), pieces[0][0].dtype),
        in_specs=[pl.BlockSpec(memory_space=pltpu.VMEM)] * len(pieces)
        + [pl.BlockSpec(memory_space=pl.ANY)],
        compiler_params=pltpu.CompilerParams(vmem_limit_bytes=JOIN_VMEM_BYTES),
        cost_estimate=pl.CostEstimate(
            flops=0, bytes_accessed=4 * total * width, transcendentals=0
        ),
    )(*[block for block, _, _ in pieces], other)


def runs(counts):
    found = []
    for at, value in enumerate(counts):
        if found and found[-1][2] == value:
            found[-1][1] = at + 1
        else:
            found.append([at, at + 1, int(value)])
    return [tuple(entry) for entry in found]


def order_rows(select, key_rows, values, prefixes):
    tokens, width = key_rows.shape

    def kernel(select_hbm, key_hbm, value_hbm, *refs):
        out_refs, (select_ref, row_ref, sems) = refs[: len(prefixes)], refs[len(prefixes) :]
        copies = [
            pltpu.make_async_copy(select_hbm, select_ref, sems.at[0]),
            pltpu.make_async_copy(key_hbm, row_ref.at[0], sems.at[1]),
            pltpu.make_async_copy(value_hbm, row_ref.at[1], sems.at[2]),
        ]
        for copy in copies:
            copy.start()
        copies[0].wait()
        for half in range(2):
            copies[1 + half].wait()
            moved = jnp.dot(
                select_ref[...], row_ref[half], preferred_element_type=jnp.float32
            ).astype(jnp.bfloat16)
            for (low, high), out_ref in zip(prefixes, out_refs):
                out_ref[:, half * width : (half + 1) * width] = moved[low:high]

    return pl.pallas_call(
        kernel,
        out_shape=[
            jax.ShapeDtypeStruct((high - low, 2 * width), jnp.bfloat16) for low, high in prefixes
        ],
        in_specs=[pl.BlockSpec(memory_space=pltpu.HBM)] * 3,
        scratch_shapes=[
            pltpu.VMEM(select.shape, jnp.bfloat16),
            pltpu.VMEM((2, tokens, width), jnp.bfloat16),
            pltpu.SemaphoreType.DMA((3,)),
        ],
        compiler_params=pltpu.CompilerParams(vmem_limit_bytes=FETCH_VMEM_BYTES),
        cost_estimate=pl.CostEstimate(
            flops=4 * select.size * width, bytes_accessed=6 * tokens * width, transcendentals=0
        ),
    )(select, key_rows, values)


def attend(queries, sets, counts=None, row_strides=None, part=(0, 1), states=(), out_weight=None, wait=None):
    tokens = queries.shape[0]
    full = queries.shape[1]
    width = full // part[1]
    base = part[0] * width
    heads, pairs = width // HEAD_DIM, width // PAIR
    joined = [not isinstance(block, tuple) for block in sets]
    sizes = [(block if whole else block[0]).shape[0] for block, whole in zip(sets, joined)]
    keys = sum(sizes)
    padded = -(-keys // LANES) * LANES
    row_runs = [(0, keys, 1)] if counts is None else runs(counts)
    scale = HEAD_DIM**-0.5 * LOG2E
    final = out_weight is not None
    groups = max(len(states), 1)

    def kernel(*refs):
        refs = list(refs)
        query_ref = refs.pop(0)
        set_refs = []
        for whole in joined:
            ref = refs.pop(0)
            set_refs.append((ref, ref, full) if whole else (ref, refs.pop(0), 0))
        state_refs = [[refs.pop(0) for _ in range(3)] for _ in states]
        if wait is not None:
            refs.pop(1 if final else 0)
        if final:
            weight_ref, out_ref = refs.pop(0), refs.pop(0)
            attended_ref, row_ref = refs[-2:]
        else:
            numer_out, peak_out, total_out = [refs.pop(0) for _ in range(3)]
        score_ref, value_ref, key_ref, turned_ref = [refs.pop(0) for _ in range(4)]
        ones = jnp.ones((16, padded), jnp.bfloat16)
        if row_strides is not None:
            row = lax.broadcasted_iota(jnp.int32, (16, padded), 1)
            times = sum((row & (s - 1) == 0).astype(jnp.int32) for s in [1] + row_strides)
            ones = times.astype(jnp.float32).astype(jnp.bfloat16)
        key_chunks = [(low, min(KEY_CHUNK, keys - low)) for low in range(0, keys, KEY_CHUNK)]
        value_chunks = [(low, min(CHUNK, padded - low)) for low in range(0, padded, CHUNK)]

        def columns(pair, shift=0):
            return pl.ds(base + shift + pair * PAIR, PAIR)

        def head_queries(half):
            turned = turned_ref[...]
            row = lax.broadcasted_iota(jnp.int32, turned.shape, 0)
            own = (row < HEAD_DIM) if half == 0 else (row >= HEAD_DIM)
            return jnp.where(own, turned, jnp.zeros_like(turned))

        def load(pair):
            turned_ref[...] = query_ref[:, columns(pair)].T
            at = 0
            for (ref, _, _), size in zip(set_refs, sizes):
                key_ref[at : at + size, :] = ref[:, columns(pair)]
                at += size

        def score(half, query_head, chunk, running):
            low, count = chunk
            scores = jnp.dot(
                key_ref[low : low + count, :], query_head, preferred_element_type=jnp.float32
            )
            score_ref[half, low : low + count, :] = scores
            tallest = jnp.max(scores.reshape(count // 8, 8, tokens), axis=0)
            return tallest if running is None else jnp.maximum(running, tallest)

        def weigh(half, peak, weighted, chunk, gathered):
            low, size = chunk
            high = min(low + size, keys)
            pieces = []
            for first, last, times in row_runs:
                first, last = max(first, low), min(last, high)
                if first < last:
                    offset = peak - math.log2(times)
                    pieces.append(jnp.exp2(score_ref[half, first:last, :] * scale - offset))
            if low + size > keys:
                pieces.append(jnp.zeros((low + size - keys, tokens), jnp.float32))
            probs = (pieces[0] if len(pieces) == 1 else jnp.concatenate(pieces, axis=0)).astype(
                jnp.bfloat16
            )
            product = jnp.dot(
                weighted[:, low : low + size], probs, preferred_element_type=jnp.float32
            )
            return product if gathered is None else gathered + product

        def one_group(first_pair, last_pair, earlier, first_state):
            def local_rows(pair, half):
                start = (pair - first_state) * PAIR + half * HEAD_DIM
                return pl.ds(start, HEAD_DIM)

            def local_head(pair, half):
                return pl.ds(2 * (pair - first_state) + half, 1)

            def finish(pair, half, gathered, peak, before):
                numer, total = gathered[:HEAD_DIM], gathered[HEAD_DIM : HEAD_DIM + 1]
                if earlier is not None:
                    factor = jnp.exp2(before - peak)
                    numer = numer + factor * earlier[0][local_rows(pair, half), :]
                    total = total + factor * earlier[2][local_head(pair, half), :]
                rows = pl.ds(pair * PAIR + half * HEAD_DIM, HEAD_DIM)
                if final:
                    attended_ref[half] = (numer * (1.0 / total)).astype(jnp.bfloat16)
                    if half == 1:
                        both = attended_ref[...].reshape(PAIR, tokens)
                        row_ref[:, pl.ds(pair * PAIR, PAIR)] = both.T
                else:
                    head = pl.ds(2 * pair + half, 1)
                    numer_out[rows, :] = numer
                    peak_out[head, :] = peak
                    total_out[head, :] = total

            def overlap(pair, half, running, values_t, next_pair, next_half):
                peak = jnp.max(running, axis=0, keepdims=True) * scale
                before = None
                if earlier is not None:
                    before = earlier[1][local_head(pair, half), :]
                    peak = jnp.maximum(peak, before)
                weighted = jnp.concatenate(
                    [values_t[half * HEAD_DIM : (half + 1) * HEAD_DIM], ones], axis=0
                )
                ahead = next_pair < last_pair
                if ahead and next_half == 0:
                    load(next_pair)
                query_head = head_queries(next_half) if ahead else None
                next_running, gathered = None, None
                for step in range(max(len(key_chunks), len(value_chunks))):
                    if ahead and step < len(key_chunks):
                        next_running = score(
                            next_half, query_head, key_chunks[step], next_running
                        )
                    if step < len(value_chunks):
                        gathered = weigh(half, peak, weighted, value_chunks[step], gathered)
                finish(pair, half, gathered, peak, before)
                return next_running

            def pair_step(pair, running):
                at = 0
                for (_, ref, shift), size in zip(set_refs, sizes):
                    value_ref[at : at + size, :] = ref[:, columns(pair, shift)]
                    at += size
                if padded > keys:
                    value_ref[keys:, :] = jnp.zeros((padded - keys, PAIR), jnp.bfloat16)
                values_t = value_ref[...].T
                if row_strides is not None:
                    values_t = values_t * ones[:1]
                running = overlap(pair, 0, running, values_t, pair, 1)
                return overlap(pair, 1, running, values_t, pair + 1, 0)

            load(first_pair)
            first_head = head_queries(0)
            running = None
            for chunk in key_chunks:
                running = score(0, first_head, chunk, running)
            for pair in range(first_pair, last_pair):
                running = pair_step(pair, running)

        for group in range(groups):
            low, high = group * pairs // groups, (group + 1) * pairs // groups
            shared = len(states) == 1
            one_group(
                low, high, state_refs[0 if shared else group] if states else None, 0 if shared else low
            )
        if final:
            out_ref[...] = jnp.dot(
                row_ref[...], weight_ref[...], preferred_element_type=jnp.float32
            ).astype(jnp.bfloat16)

    if final:
        out_shape = jax.ShapeDtypeStruct((tokens, width), jnp.bfloat16)
    else:
        out_shape = [
            jax.ShapeDtypeStruct((width, tokens), jnp.float32),
            jax.ShapeDtypeStruct((heads, tokens), jnp.float32),
            jax.ShapeDtypeStruct((heads, tokens), jnp.float32),
        ]
    scratch = [
        pltpu.VMEM((2, padded, tokens), jnp.float32),
        pltpu.VMEM((padded, PAIR), jnp.bfloat16),
        pltpu.VMEM((padded, PAIR), jnp.bfloat16),
        pltpu.VMEM((PAIR, tokens), jnp.bfloat16),
    ]
    if final:
        scratch.append(pltpu.VMEM((2, HEAD_DIM, tokens), jnp.bfloat16))
        scratch.append(pltpu.VMEM((tokens, width), jnp.bfloat16))
    operands = [queries]
    for block, whole in zip(sets, joined):
        operands += [block] if whole else list(block)
    whole_spec = pl.BlockSpec(memory_space=pltpu.VMEM)
    specs = [whole_spec] * len(operands)
    for array in [array for state in states for array in state] + ([out_weight] if final else []):
        operands.append(array)
        specs.append(whole_spec)
    if wait is not None:
        operands.append(wait)
        specs.append(pl.BlockSpec(memory_space=pl.ANY))
    return pl.pallas_call(
        kernel,
        out_shape=out_shape,
        in_specs=specs,
        scratch_shapes=scratch,
        compiler_params=pltpu.CompilerParams(
            vmem_limit_bytes=VMEM_BYTES
        ),
        cost_estimate=pl.CostEstimate(
            flops=16 * tokens * keys * width,
            bytes_accessed=(4 * keys * width + 4 * tokens * width),
            transcendentals=tokens * keys * heads,
        ),
    )(*operands)


def local(queries, key_rows, values, out_weight):
    query_rows, own_keys, own_values = queries[0], key_rows[0], values[0]
    tokens = query_rows.shape[0]
    n_inner, n_outer = lax.axis_size("inner"), lax.axis_size("outer")
    inner_bits = n_inner.bit_length() - 1
    strides = [1 << (bit + 1) for bit in range(inner_bits + 1)]
    sends = [tokens >> (bit + 1) for bit in range(inner_bits + 1)]
    n_global = tokens // GSTEP

    rows = np.arange(0, tokens, 2)
    rank = sum((rows % s == 0).astype(np.int64) for s in strides + [GSTEP])
    order = rows[np.lexsort((rows, -rank))]
    select = np.zeros((sends[0], tokens), np.float32)
    select[np.arange(sends[0]), order] = 1.0

    def prefix_counts(level, low, high):
        return sum((order[low:high] % s == 0).astype(np.int64) for s in strides[level:])

    first_a, first_b, far = order_rows(
        jnp.asarray(select, jnp.bfloat16),
        own_keys,
        own_values,
        [(0, sends[1]), (sends[1], sends[0]), (0, n_global)],
    )

    held = {0: (first_a, 0)}
    for bit in range(1, inner_bits):
        held[1 << bit] = (across(first_a[: sends[bit]], "inner", 1 << bit), 0)
    held[1] = (across(first_a, "inner", 1), 0)
    own_set = [(own_keys, own_values)]
    own_states, moved, flip = [], far, 2
    while flip < n_outer or len(own_states) < 2:
        if flip < n_outer:
            came = across(moved, "outer", flip)
            flip *= 2
        if len(own_states) < 2:
            own_states.append(
                attend(
                    query_rows,
                    own_set,
                    row_strides=strides,
                    part=(len(own_states), 2),
                    wait=moved if own_states else None,
                )
            )
        moved = join_after([(moved, 0, moved.shape[0]), (came, 0, came.shape[0])], own_states[-1][1])
    far = moved
    n_far = far.shape[0]
    fars = {0: (far, 0)}

    def first_rows(where, count):
        return (where[0], where[1], where[1] + count)

    near_b = across(first_b, "inner", 1)
    fars[1] = (across(far, "inner", 1), 0)
    own_done = far

    known = [0] + [1 << bit for bit in range(inner_bits)]
    late = [d for d in range(n_inner) if d not in known]
    last = sends[inner_bits]
    late_sets, late_counts = [], []
    for bit in range(1, inner_bits):
        count = sends[bit]
        others = range(1, 1 << bit)
        pieces = [first_rows(held[d], count) for d in others] + [first_rows(fars[0], n_far)]
        own_done = join_after(pieces, own_done)
        came = across(own_done, "inner", 1 << bit)
        for at, d in enumerate(others):
            held[d | 1 << bit] = (came, at * count)
        fars[1 << bit] = (came, len(others) * count)
        late_sets.append(came)
        late_counts += [prefix_counts(bit, 0, count)] * len(others) + [np.ones(n_far, np.int64)]
    for d in late:
        fars[d] = (across(far, "inner", d), 0)
    late_sets += [fars[d][0] for d in [0, 1] + late]
    late_counts.append(np.ones(n_far * (2 + len(late)), np.int64))

    early_sets = [held[1][0], near_b] + [held[d][0] for d in known[2:]]
    early_counts = [prefix_counts(0, 0, sends[0])]
    early_counts += [prefix_counts(bit, 0, sends[bit]) for bit in range(1, inner_bits)]
    state = attend(query_rows, early_sets, np.concatenate(early_counts), states=own_states)

    pieces = [first_rows(held[d], last) for d in range(n_inner)]
    pieces += [first_rows(fars[d], n_far) for d in range(n_inner)]
    core = across(join_after(pieces, state[1]), "outer", 1)
    state = attend(query_rows, late_sets, np.concatenate(late_counts), states=[state])
    result = attend(query_rows, [core], states=[state], out_weight=out_weight)
    return result[None]


def solution(mesh):
    placed = (P("outer", "inner", None), P("outer", "inner", None), P("outer", "inner", None), P())
    return jax.shard_map(
        local, mesh=mesh, in_specs=placed, out_specs=P("outer", "inner", None), check_vma=False
    )
```

```python
import math

import jax
import jax.numpy as jnp
import numpy as np
from jax import lax
from jax.experimental import pallas as pl
from jax.experimental.pallas import tpu as pltpu
from jax.sharding import PartitionSpec as P

HEAD_DIM = 64
GSTEP = 64
PAIR = 2 * HEAD_DIM
CHUNK = 256
KEY_CHUNK = 512
LANES = 128
LOG2E = math.log2(math.e)
VMEM_BYTES = 16 * 1024 * 1024
JOIN_VMEM_BYTES = 8 * 1024 * 1024
FETCH_VMEM_BYTES = 60 * 1024 * 1024


def across(block, axis, flip):
    return lax.ppermute(block, axis, [(i, i ^ flip) for i in range(lax.axis_size(axis))])


def after(block, *others):
    return lax.optimization_barrier((block, *others))[0]


def join_after(pieces, other):
    width = pieces[0][0].shape[1]
    total = sum(high - low for _, low, high in pieces)

    def kernel(*refs):
        out_ref, at = refs[-1], 0
        for ref, (_, low, high) in zip(refs, pieces):
            out_ref[at : at + high - low, :] = ref[low:high, :]
            at += high - low

    return pl.pallas_call(
        kernel,
        out_shape=jax.ShapeDtypeStruct((total, width), pieces[0][0].dtype),
        in_specs=[pl.BlockSpec(memory_space=pltpu.VMEM)] * len(pieces)
        + [pl.BlockSpec(memory_space=pl.ANY)],
        compiler_params=pltpu.CompilerParams(vmem_limit_bytes=JOIN_VMEM_BYTES),
        cost_estimate=pl.CostEstimate(
            flops=0, bytes_accessed=4 * total * width, transcendentals=0
        ),
    )(*[block for block, _, _ in pieces], other)


def runs(counts):
    found = []
    for at, value in enumerate(counts):
        if found and found[-1][2] == value:
            found[-1][1] = at + 1
        else:
            found.append([at, at + 1, int(value)])
    return [tuple(entry) for entry in found]


def order_rows(select, key_rows, values, prefixes):
    tokens, width = key_rows.shape

    def kernel(select_hbm, key_hbm, value_hbm, *refs):
        out_refs, (select_ref, row_ref, sems) = refs[: len(prefixes)], refs[len(prefixes) :]
        copies = [
            pltpu.make_async_copy(select_hbm, select_ref, sems.at[0]),
            pltpu.make_async_copy(key_hbm, row_ref.at[0], sems.at[1]),
            pltpu.make_async_copy(value_hbm, row_ref.at[1], sems.at[2]),
        ]
        for copy in copies:
            copy.start()
        copies[0].wait()
        for half in range(2):
            copies[1 + half].wait()
            moved = jnp.dot(
                select_ref[...], row_ref[half], preferred_element_type=jnp.float32
            ).astype(jnp.bfloat16)
            for (low, high), out_ref in zip(prefixes, out_refs):
                out_ref[:, half * width : (half + 1) * width] = moved[low:high]

    return pl.pallas_call(
        kernel,
        out_shape=[
            jax.ShapeDtypeStruct((high - low, 2 * width), jnp.bfloat16) for low, high in prefixes
        ],
        in_specs=[pl.BlockSpec(memory_space=pltpu.HBM)] * 3,
        scratch_shapes=[
            pltpu.VMEM(select.shape, jnp.bfloat16),
            pltpu.VMEM((2, tokens, width), jnp.bfloat16),
            pltpu.SemaphoreType.DMA((3,)),
        ],
        compiler_params=pltpu.CompilerParams(vmem_limit_bytes=FETCH_VMEM_BYTES),
        cost_estimate=pl.CostEstimate(
            flops=4 * select.size * width, bytes_accessed=6 * tokens * width, transcendentals=0
        ),
    )(select, key_rows, values)


def attend(queries, sets, counts=None, row_strides=None, part=(0, 1), states=(), out_weight=None, wait=None):
    tokens = queries.shape[0]
    full = queries.shape[1]
    width = full // part[1]
    base = part[0] * width
    heads, pairs = width // HEAD_DIM, width // PAIR
    joined = [not isinstance(block, tuple) for block in sets]
    sizes = [(block if whole else block[0]).shape[0] for block, whole in zip(sets, joined)]
    keys = sum(sizes)
    padded = -(-keys // LANES) * LANES
    row_runs = [(0, keys, 1)] if counts is None else runs(counts)
    scale = HEAD_DIM**-0.5 * LOG2E
    final = out_weight is not None
    groups = max(len(states), 1)

    def kernel(*refs):
        refs = list(refs)
        query_ref = refs.pop(0)
        set_refs = []
        for whole in joined:
            ref = refs.pop(0)
            set_refs.append((ref, ref, full) if whole else (ref, refs.pop(0), 0))
        state_refs = [[refs.pop(0) for _ in range(3)] for _ in states]
        if wait is not None:
            refs.pop(1 if final else 0)
        if final:
            weight_ref, out_hbm = refs.pop(0), refs.pop(0)
            attended_ref, out_ref, result_ref, sems = refs[-4:]
        else:
            numer_out, peak_out, total_out = [refs.pop(0) for _ in range(3)]
        score_ref, value_ref, key_ref, turned_ref = [refs.pop(0) for _ in range(4)]
        ones = jnp.ones((16, padded), jnp.bfloat16)
        if row_strides is not None:
            row = lax.broadcasted_iota(jnp.int32, (16, padded), 1)
            times = sum((row & (s - 1) == 0).astype(jnp.int32) for s in [1] + row_strides)
            ones = times.astype(jnp.float32).astype(jnp.bfloat16)
        key_chunks = [(low, min(KEY_CHUNK, keys - low)) for low in range(0, keys, KEY_CHUNK)]
        value_chunks = [(low, min(CHUNK, padded - low)) for low in range(0, padded, CHUNK)]

        def columns(pair, shift=0):
            return pl.ds(base + shift + pair * PAIR, PAIR)

        def head_queries(half):
            turned = turned_ref[...]
            row = lax.broadcasted_iota(jnp.int32, turned.shape, 0)
            own = (row < HEAD_DIM) if half == 0 else (row >= HEAD_DIM)
            return jnp.where(own, turned, jnp.zeros_like(turned))

        def load(pair):
            turned_ref[...] = query_ref[:, columns(pair)].T
            at = 0
            for (ref, _, _), size in zip(set_refs, sizes):
                key_ref[at : at + size, :] = ref[:, columns(pair)]
                at += size

        def score(half, query_head, chunk, running):
            low, count = chunk
            scores = jnp.dot(
                key_ref[low : low + count, :], query_head, preferred_element_type=jnp.float32
            )
            score_ref[half, low : low + count, :] = scores
            tallest = jnp.max(scores.reshape(count // 8, 8, tokens), axis=0)
            return tallest if running is None else jnp.maximum(running, tallest)

        def weigh(half, peak, weighted, chunk, gathered):
            low, size = chunk
            high = min(low + size, keys)
            pieces = []
            for first, last, times in row_runs:
                first, last = max(first, low), min(last, high)
                if first < last:
                    offset = peak - math.log2(times)
                    pieces.append(jnp.exp2(score_ref[half, first:last, :] * scale - offset))
            if low + size > keys:
                pieces.append(jnp.zeros((low + size - keys, tokens), jnp.float32))
            probs = (pieces[0] if len(pieces) == 1 else jnp.concatenate(pieces, axis=0)).astype(
                jnp.bfloat16
            )
            product = jnp.dot(
                weighted[:, low : low + size], probs, preferred_element_type=jnp.float32
            )
            return product if gathered is None else gathered + product

        def one_group(first_pair, last_pair, earlier, first_state):
            def local_rows(pair, half):
                start = (pair - first_state) * PAIR + half * HEAD_DIM
                return pl.ds(start, HEAD_DIM)

            def local_head(pair, half):
                return pl.ds(2 * (pair - first_state) + half, 1)

            def finish(pair, half, gathered, peak, before):
                numer, total = gathered[:HEAD_DIM], gathered[HEAD_DIM : HEAD_DIM + 1]
                if earlier is not None:
                    factor = jnp.exp2(before - peak)
                    numer = numer + factor * earlier[0][local_rows(pair, half), :]
                    total = total + factor * earlier[2][local_head(pair, half), :]
                rows = pl.ds(pair * PAIR + half * HEAD_DIM, HEAD_DIM)
                if final:
                    attended_ref[half] = (numer * (1.0 / total)).astype(jnp.bfloat16)
                    if half == 1:
                        both = attended_ref[...].reshape(PAIR, tokens)
                        out_ref[:, pl.ds(pair * PAIR, PAIR)] = both.T
                else:
                    head = pl.ds(2 * pair + half, 1)
                    numer_out[rows, :] = numer
                    peak_out[head, :] = peak
                    total_out[head, :] = total

            def overlap(pair, half, running, values_t, next_pair, next_half):
                peak = jnp.max(running, axis=0, keepdims=True) * scale
                before = None
                if earlier is not None:
                    before = earlier[1][local_head(pair, half), :]
                    peak = jnp.maximum(peak, before)
                weighted = jnp.concatenate(
                    [values_t[half * HEAD_DIM : (half + 1) * HEAD_DIM], ones], axis=0
                )
                ahead = next_pair < last_pair
                if ahead and next_half == 0:
                    load(next_pair)
                query_head = head_queries(next_half) if ahead else None
                next_running, gathered = None, None
                for step in range(max(len(key_chunks), len(value_chunks))):
                    if ahead and step < len(key_chunks):
                        next_running = score(
                            next_half, query_head, key_chunks[step], next_running
                        )
                    if step < len(value_chunks):
                        gathered = weigh(half, peak, weighted, value_chunks[step], gathered)
                finish(pair, half, gathered, peak, before)
                return next_running

            def pair_step(pair, running):
                at = 0
                for (_, ref, shift), size in zip(set_refs, sizes):
                    value_ref[at : at + size, :] = ref[:, columns(pair, shift)]
                    at += size
                if padded > keys:
                    value_ref[keys:, :] = jnp.zeros((padded - keys, PAIR), jnp.bfloat16)
                values_t = value_ref[...].T
                if row_strides is not None:
                    values_t = values_t * ones[:1]
                running = overlap(pair, 0, running, values_t, pair, 1)
                return overlap(pair, 1, running, values_t, pair + 1, 0)

            load(first_pair)
            first_head = head_queries(0)
            running = None
            for chunk in key_chunks:
                running = score(0, first_head, chunk, running)
            for pair in range(first_pair, last_pair):
                running = pair_step(pair, running)

        for group in range(groups):
            low, high = group * pairs // groups, (group + 1) * pairs // groups
            shared = len(states) == 1
            one_group(
                low, high, state_refs[0 if shared else group] if states else None, 0 if shared else low
            )
        if final:
            copies, step = [], tokens // 2
            for low in range(0, tokens, step):
                result_ref[low : low + step, :] = jnp.dot(
                    out_ref[low : low + step, :],
                    weight_ref[...],
                    preferred_element_type=jnp.float32,
                ).astype(jnp.bfloat16)
                for first in range(low, low + step, LANES):
                    rows = slice(first, first + LANES)
                    copies.append(
                        pltpu.make_async_copy(
                            result_ref.at[rows], out_hbm.at[rows], sems.at[len(copies)]
                        )
                    )
                    copies[-1].start()
            for copy in copies:
                copy.wait()

    if final:
        out_shape = jax.ShapeDtypeStruct((tokens, width), jnp.bfloat16)
    else:
        out_shape = [
            jax.ShapeDtypeStruct((width, tokens), jnp.float32),
            jax.ShapeDtypeStruct((heads, tokens), jnp.float32),
            jax.ShapeDtypeStruct((heads, tokens), jnp.float32),
        ]
    scratch = [
        pltpu.VMEM((2, padded, tokens), jnp.float32),
        pltpu.VMEM((padded, PAIR), jnp.bfloat16),
        pltpu.VMEM((padded, PAIR), jnp.bfloat16),
        pltpu.VMEM((PAIR, tokens), jnp.bfloat16),
    ]
    if final:
        scratch.append(pltpu.VMEM((2, HEAD_DIM, tokens), jnp.bfloat16))
        scratch += [pltpu.VMEM((tokens, width), jnp.bfloat16)] * 2
        scratch.append(pltpu.SemaphoreType.DMA((tokens // LANES,)))
    operands = [queries]
    for block, whole in zip(sets, joined):
        operands += [block] if whole else list(block)
    whole_spec = pl.BlockSpec(memory_space=pltpu.VMEM)
    specs = [whole_spec] * len(operands)
    for array in [array for state in states for array in state] + ([out_weight] if final else []):
        operands.append(array)
        specs.append(whole_spec)
    if wait is not None:
        operands.append(wait)
        specs.append(pl.BlockSpec(memory_space=pl.ANY))
    return pl.pallas_call(
        kernel,
        out_shape=out_shape,
        in_specs=specs,
        **({"out_specs": pl.BlockSpec(memory_space=pl.ANY)} if final else {}),
        scratch_shapes=scratch,
        compiler_params=pltpu.CompilerParams(
            vmem_limit_bytes=VMEM_BYTES
        ),
        cost_estimate=pl.CostEstimate(
            flops=16 * tokens * keys * width,
            bytes_accessed=(4 * keys * width + 4 * tokens * width),
            transcendentals=tokens * keys * heads,
        ),
    )(*operands)


def local(queries, key_rows, values, out_weight):
    query_rows, own_keys, own_values = queries[0], key_rows[0], values[0]
    tokens = query_rows.shape[0]
    n_inner, n_outer = lax.axis_size("inner"), lax.axis_size("outer")
    inner_bits = n_inner.bit_length() - 1
    strides = [1 << (bit + 1) for bit in range(inner_bits + 1)]
    sends = [tokens >> (bit + 1) for bit in range(inner_bits + 1)]
    n_global = tokens // GSTEP

    rows = np.arange(0, tokens, 2)
    rank = sum((rows % s == 0).astype(np.int64) for s in strides + [GSTEP])
    order = rows[np.lexsort((rows, -rank))]
    select = np.zeros((sends[0], tokens), np.float32)
    select[np.arange(sends[0]), order] = 1.0

    def prefix_counts(level, low, high):
        return sum((order[low:high] % s == 0).astype(np.int64) for s in strides[level:])

    first_a, first_b, far = order_rows(
        jnp.asarray(select, jnp.bfloat16),
        own_keys,
        own_values,
        [(0, sends[1]), (sends[1], sends[0]), (0, n_global)],
    )

    held = {0: (first_a, 0)}
    for bit in range(1, inner_bits):
        held[1 << bit] = (across(first_a[: sends[bit]], "inner", 1 << bit), 0)
    held[1] = (across(first_a, "inner", 1), 0)
    own_set = [(own_keys, own_values)]
    own_states, moved, flip = [], far, 2
    while flip < n_outer or len(own_states) < 2:
        if flip < n_outer:
            came = across(moved, "outer", flip)
            flip *= 2
        if len(own_states) < 2:
            own_states.append(
                attend(
                    query_rows,
                    own_set,
                    row_strides=strides,
                    part=(len(own_states), 2),
                    wait=moved if own_states else None,
                )
            )
        moved = join_after([(moved, 0, moved.shape[0]), (came, 0, came.shape[0])], own_states[-1][1])
    far = moved
    n_far = far.shape[0]
    fars = {0: (far, 0)}

    def first_rows(where, count):
        return (where[0], where[1], where[1] + count)

    near_b = across(first_b, "inner", 1)
    fars[1] = (across(far, "inner", 1), 0)
    own_done = far

    known = [0] + [1 << bit for bit in range(inner_bits)]
    late = [d for d in range(n_inner) if d not in known]
    last = sends[inner_bits]
    late_sets, late_counts = [], []
    for bit in range(1, inner_bits):
        count = sends[bit]
        others = range(1, 1 << bit)
        pieces = [first_rows(held[d], count) for d in others] + [first_rows(fars[0], n_far)]
        own_done = join_after(pieces, own_done)
        came = across(own_done, "inner", 1 << bit)
        for at, d in enumerate(others):
            held[d | 1 << bit] = (came, at * count)
        fars[1 << bit] = (came, len(others) * count)
        late_sets.append(came)
        late_counts += [prefix_counts(bit, 0, count)] * len(others) + [np.ones(n_far, np.int64)]
    for d in late:
        fars[d] = (across(far, "inner", d), 0)
    late_sets += [fars[d][0] for d in [0, 1] + late]
    late_counts.append(np.ones(n_far * (2 + len(late)), np.int64))

    early_sets = [held[1][0], near_b] + [held[d][0] for d in known[2:]]
    early_counts = [prefix_counts(0, 0, sends[0])]
    early_counts += [prefix_counts(bit, 0, sends[bit]) for bit in range(1, inner_bits)]
    state = attend(query_rows, early_sets, np.concatenate(early_counts), states=own_states)

    pieces = [first_rows(held[d], last) for d in range(n_inner)]
    pieces += [first_rows(fars[d], n_far) for d in range(n_inner)]
    core = across(join_after(pieces, state[1]), "outer", 1)
    state = attend(query_rows, late_sets, np.concatenate(late_counts), states=[state])
    result = attend(query_rows, [core], states=[state], out_weight=out_weight)
    return result[None]


def solution(mesh):
    placed = (P("outer", "inner", None), P("outer", "inner", None), P("outer", "inner", None), P())
    return jax.shard_map(
        local, mesh=mesh, in_specs=placed, out_specs=P("outer", "inner", None), check_vma=False
    )
```

```python
import math

import jax
import jax.numpy as jnp
import numpy as np
from jax import lax
from jax.experimental import pallas as pl
from jax.experimental.pallas import tpu as pltpu
from jax.sharding import PartitionSpec as P

HEAD_DIM = 64
GSTEP = 64
PAIR = 2 * HEAD_DIM
CHUNK = 512
KEY_CHUNK = 512
LANES = 128
LOG2E = math.log2(math.e)
VMEM_BYTES = 16 * 1024 * 1024
JOIN_VMEM_BYTES = 8 * 1024 * 1024
FETCH_VMEM_BYTES = 60 * 1024 * 1024


def across(block, axis, flip):
    return lax.ppermute(block, axis, [(i, i ^ flip) for i in range(lax.axis_size(axis))])


def after(block, *others):
    return lax.optimization_barrier((block, *others))[0]


def join_after(pieces, other):
    width = pieces[0][0].shape[1]
    total = sum(high - low for _, low, high in pieces)

    def kernel(*refs):
        out_ref, at = refs[-1], 0
        for ref, (_, low, high) in zip(refs, pieces):
            out_ref[at : at + high - low, :] = ref[low:high, :]
            at += high - low

    return pl.pallas_call(
        kernel,
        out_shape=jax.ShapeDtypeStruct((total, width), pieces[0][0].dtype),
        in_specs=[pl.BlockSpec(memory_space=pltpu.VMEM)] * len(pieces)
        + [pl.BlockSpec(memory_space=pl.ANY)],
        compiler_params=pltpu.CompilerParams(vmem_limit_bytes=JOIN_VMEM_BYTES),
        cost_estimate=pl.CostEstimate(
            flops=0, bytes_accessed=4 * total * width, transcendentals=0
        ),
    )(*[block for block, _, _ in pieces], other)


def runs(counts):
    found = []
    for at, value in enumerate(counts):
        if found and found[-1][2] == value:
            found[-1][1] = at + 1
        else:
            found.append([at, at + 1, int(value)])
    return [tuple(entry) for entry in found]


def order_rows(select, key_rows, values, prefixes):
    tokens, width = key_rows.shape

    def kernel(select_hbm, key_hbm, value_hbm, *refs):
        out_refs, (select_ref, row_ref, sems) = refs[: len(prefixes)], refs[len(prefixes) :]
        copies = [
            pltpu.make_async_copy(select_hbm, select_ref, sems.at[0]),
            pltpu.make_async_copy(key_hbm, row_ref.at[0], sems.at[1]),
            pltpu.make_async_copy(value_hbm, row_ref.at[1], sems.at[2]),
        ]
        for copy in copies:
            copy.start()
        copies[0].wait()
        for half in range(2):
            copies[1 + half].wait()
            moved = jnp.dot(
                select_ref[...], row_ref[half], preferred_element_type=jnp.float32
            ).astype(jnp.bfloat16)
            for (low, high), out_ref in zip(prefixes, out_refs):
                out_ref[:, half * width : (half + 1) * width] = moved[low:high]

    return pl.pallas_call(
        kernel,
        out_shape=[
            jax.ShapeDtypeStruct((high - low, 2 * width), jnp.bfloat16) for low, high in prefixes
        ],
        in_specs=[pl.BlockSpec(memory_space=pltpu.HBM)] * 3,
        scratch_shapes=[
            pltpu.VMEM(select.shape, jnp.bfloat16),
            pltpu.VMEM((2, tokens, width), jnp.bfloat16),
            pltpu.SemaphoreType.DMA((3,)),
        ],
        compiler_params=pltpu.CompilerParams(vmem_limit_bytes=FETCH_VMEM_BYTES),
        cost_estimate=pl.CostEstimate(
            flops=4 * select.size * width, bytes_accessed=6 * tokens * width, transcendentals=0
        ),
    )(select, key_rows, values)


def attend(queries, sets, counts=None, row_strides=None, part=(0, 1), states=(), out_weight=None, wait=None):
    tokens = queries.shape[0]
    full = queries.shape[1]
    width = full // part[1]
    base = part[0] * width
    heads, pairs = width // HEAD_DIM, width // PAIR
    joined = [not isinstance(block, tuple) for block in sets]
    sizes = [(block if whole else block[0]).shape[0] for block, whole in zip(sets, joined)]
    keys = sum(sizes)
    padded = -(-keys // LANES) * LANES
    row_runs = [(0, keys, 1)] if counts is None else runs(counts)
    scale = HEAD_DIM**-0.5 * LOG2E
    final = out_weight is not None
    groups = max(len(states), 1)

    def kernel(*refs):
        refs = list(refs)
        query_ref = refs.pop(0)
        set_refs = []
        for whole in joined:
            ref = refs.pop(0)
            set_refs.append((ref, ref, full) if whole else (ref, refs.pop(0), 0))
        state_refs = [[refs.pop(0) for _ in range(3)] for _ in states]
        if wait is not None:
            refs.pop(1 if final else 0)
        if final:
            weight_ref, out_hbm = refs.pop(0), refs.pop(0)
            attended_ref, out_ref, result_ref, sems = refs[-4:]
        else:
            numer_out, peak_out, total_out = [refs.pop(0) for _ in range(3)]
        score_ref, value_ref, key_ref, turned_ref = [refs.pop(0) for _ in range(4)]
        ones = jnp.ones((16, padded), jnp.bfloat16)
        if row_strides is not None:
            row = lax.broadcasted_iota(jnp.int32, (16, padded), 1)
            times = sum((row & (s - 1) == 0).astype(jnp.int32) for s in [1] + row_strides)
            ones = times.astype(jnp.float32).astype(jnp.bfloat16)
        key_chunks = [(low, min(KEY_CHUNK, keys - low)) for low in range(0, keys, KEY_CHUNK)]
        value_chunks = [(low, min(CHUNK, padded - low)) for low in range(0, padded, CHUNK)]

        def columns(pair, shift=0):
            return pl.ds(base + shift + pair * PAIR, PAIR)

        def head_queries(half):
            turned = turned_ref[...]
            row = lax.broadcasted_iota(jnp.int32, turned.shape, 0)
            own = (row < HEAD_DIM) if half == 0 else (row >= HEAD_DIM)
            return jnp.where(own, turned, jnp.zeros_like(turned))

        def load(pair):
            turned_ref[...] = query_ref[:, columns(pair)].T
            at = 0
            for (ref, _, _), size in zip(set_refs, sizes):
                key_ref[at : at + size, :] = ref[:, columns(pair)]
                at += size

        def score(half, query_head, chunk, running):
            low, count = chunk
            scores = jnp.dot(
                key_ref[low : low + count, :], query_head, preferred_element_type=jnp.float32
            )
            score_ref[half, low : low + count, :] = scores
            tallest = jnp.max(scores.reshape(count // 8, 8, tokens), axis=0)
            return tallest if running is None else jnp.maximum(running, tallest)

        def weigh(half, peak, weighted, chunk, gathered):
            low, size = chunk
            high = min(low + size, keys)
            pieces = []
            for first, last, times in row_runs:
                first, last = max(first, low), min(last, high)
                if first < last:
                    offset = peak - math.log2(times)
                    pieces.append(jnp.exp2(score_ref[half, first:last, :] * scale - offset))
            if low + size > keys:
                pieces.append(jnp.zeros((low + size - keys, tokens), jnp.float32))
            probs = (pieces[0] if len(pieces) == 1 else jnp.concatenate(pieces, axis=0)).astype(
                jnp.bfloat16
            )
            product = jnp.dot(
                weighted[:, low : low + size], probs, preferred_element_type=jnp.float32
            )
            return product if gathered is None else gathered + product

        def one_group(first_pair, last_pair, earlier, first_state):
            def local_rows(pair, half):
                start = (pair - first_state) * PAIR + half * HEAD_DIM
                return pl.ds(start, HEAD_DIM)

            def local_head(pair, half):
                return pl.ds(2 * (pair - first_state) + half, 1)

            def finish(pair, half, gathered, peak, before):
                numer, total = gathered[:HEAD_DIM], gathered[HEAD_DIM : HEAD_DIM + 1]
                if earlier is not None:
                    factor = jnp.exp2(before - peak)
                    numer = numer + factor * earlier[0][local_rows(pair, half), :]
                    total = total + factor * earlier[2][local_head(pair, half), :]
                rows = pl.ds(pair * PAIR + half * HEAD_DIM, HEAD_DIM)
                if final:
                    attended_ref[half] = (numer * (1.0 / total)).astype(jnp.bfloat16)
                    if half == 1:
                        both = attended_ref[...].reshape(PAIR, tokens)
                        out_ref[:, pl.ds(pair * PAIR, PAIR)] = both.T
                else:
                    head = pl.ds(2 * pair + half, 1)
                    numer_out[rows, :] = numer
                    peak_out[head, :] = peak
                    total_out[head, :] = total

            def overlap(pair, half, running, values_t, next_pair, next_half):
                peak = jnp.max(running, axis=0, keepdims=True) * scale
                before = None
                if earlier is not None:
                    before = earlier[1][local_head(pair, half), :]
                    peak = jnp.maximum(peak, before)
                weighted = jnp.concatenate(
                    [values_t[half * HEAD_DIM : (half + 1) * HEAD_DIM], ones], axis=0
                )
                ahead = next_pair < last_pair
                if ahead and next_half == 0:
                    load(next_pair)
                query_head = head_queries(next_half) if ahead else None
                next_running, gathered = None, None
                for step in range(max(len(key_chunks), len(value_chunks))):
                    if ahead and step < len(key_chunks):
                        next_running = score(
                            next_half, query_head, key_chunks[step], next_running
                        )
                    if step < len(value_chunks):
                        gathered = weigh(half, peak, weighted, value_chunks[step], gathered)
                finish(pair, half, gathered, peak, before)
                return next_running

            def pair_step(pair, running):
                at = 0
                for (_, ref, shift), size in zip(set_refs, sizes):
                    value_ref[at : at + size, :] = ref[:, columns(pair, shift)]
                    at += size
                if padded > keys:
                    value_ref[keys:, :] = jnp.zeros((padded - keys, PAIR), jnp.bfloat16)
                values_t = value_ref[...].T
                if row_strides is not None:
                    values_t = values_t * ones[:1]
                running = overlap(pair, 0, running, values_t, pair, 1)
                return overlap(pair, 1, running, values_t, pair + 1, 0)

            load(first_pair)
            first_head = head_queries(0)
            running = None
            for chunk in key_chunks:
                running = score(0, first_head, chunk, running)
            for pair in range(first_pair, last_pair):
                running = pair_step(pair, running)

        for group in range(groups):
            low, high = group * pairs // groups, (group + 1) * pairs // groups
            shared = len(states) == 1
            one_group(
                low, high, state_refs[0 if shared else group] if states else None, 0 if shared else low
            )
        if final:
            copies, step = [], tokens // 2
            for low in range(0, tokens, step):
                result_ref[low : low + step, :] = jnp.dot(
                    out_ref[low : low + step, :],
                    weight_ref[...],
                    preferred_element_type=jnp.float32,
                ).astype(jnp.bfloat16)
                for first in range(low, low + step, LANES):
                    rows = slice(first, first + LANES)
                    copies.append(
                        pltpu.make_async_copy(
                            result_ref.at[rows], out_hbm.at[rows], sems.at[len(copies)]
                        )
                    )
                    copies[-1].start()
            for copy in copies:
                copy.wait()

    if final:
        out_shape = jax.ShapeDtypeStruct((tokens, width), jnp.bfloat16)
    else:
        out_shape = [
            jax.ShapeDtypeStruct((width, tokens), jnp.float32),
            jax.ShapeDtypeStruct((heads, tokens), jnp.float32),
            jax.ShapeDtypeStruct((heads, tokens), jnp.float32),
        ]
    scratch = [
        pltpu.VMEM((2, padded, tokens), jnp.float32),
        pltpu.VMEM((padded, PAIR), jnp.bfloat16),
        pltpu.VMEM((padded, PAIR), jnp.bfloat16),
        pltpu.VMEM((PAIR, tokens), jnp.bfloat16),
    ]
    if final:
        scratch.append(pltpu.VMEM((2, HEAD_DIM, tokens), jnp.bfloat16))
        scratch += [pltpu.VMEM((tokens, width), jnp.bfloat16)] * 2
        scratch.append(pltpu.SemaphoreType.DMA((tokens // LANES,)))
    operands = [queries]
    for block, whole in zip(sets, joined):
        operands += [block] if whole else list(block)
    whole_spec = pl.BlockSpec(memory_space=pltpu.VMEM)
    specs = [whole_spec] * len(operands)
    for array in [array for state in states for array in state] + ([out_weight] if final else []):
        operands.append(array)
        specs.append(whole_spec)
    if wait is not None:
        operands.append(wait)
        specs.append(pl.BlockSpec(memory_space=pl.ANY))
    return pl.pallas_call(
        kernel,
        out_shape=out_shape,
        in_specs=specs,
        **({"out_specs": pl.BlockSpec(memory_space=pl.ANY)} if final else {}),
        scratch_shapes=scratch,
        compiler_params=pltpu.CompilerParams(
            vmem_limit_bytes=VMEM_BYTES
        ),
        cost_estimate=pl.CostEstimate(
            flops=16 * tokens * keys * width,
            bytes_accessed=(4 * keys * width + 4 * tokens * width),
            transcendentals=tokens * keys * heads,
        ),
    )(*operands)


def local(queries, key_rows, values, out_weight):
    query_rows, own_keys, own_values = queries[0], key_rows[0], values[0]
    tokens = query_rows.shape[0]
    n_inner, n_outer = lax.axis_size("inner"), lax.axis_size("outer")
    inner_bits = n_inner.bit_length() - 1
    strides = [1 << (bit + 1) for bit in range(inner_bits + 1)]
    sends = [tokens >> (bit + 1) for bit in range(inner_bits + 1)]
    n_global = tokens // GSTEP

    rows = np.arange(0, tokens, 2)
    rank = sum((rows % s == 0).astype(np.int64) for s in strides + [GSTEP])
    order = rows[np.lexsort((rows, -rank))]
    select = np.zeros((sends[0], tokens), np.float32)
    select[np.arange(sends[0]), order] = 1.0

    def prefix_counts(level, low, high):
        return sum((order[low:high] % s == 0).astype(np.int64) for s in strides[level:])

    first_a, first_b, far = order_rows(
        jnp.asarray(select, jnp.bfloat16),
        own_keys,
        own_values,
        [(0, sends[1]), (sends[1], sends[0]), (0, n_global)],
    )

    held = {0: (first_a, 0)}
    for bit in range(1, inner_bits):
        held[1 << bit] = (across(first_a[: sends[bit]], "inner", 1 << bit), 0)
    held[1] = (across(first_a, "inner", 1), 0)
    own_set = [(own_keys, own_values)]
    own_states, moved, flip = [], far, 2
    while flip < n_outer or len(own_states) < 2:
        if flip < n_outer:
            came = across(moved, "outer", flip)
            flip *= 2
        if len(own_states) < 2:
            own_states.append(
                attend(
                    query_rows,
                    own_set,
                    row_strides=strides,
                    part=(len(own_states), 2),
                    wait=moved if own_states else None,
                )
            )
        moved = join_after([(moved, 0, moved.shape[0]), (came, 0, came.shape[0])], own_states[-1][1])
    far = moved
    n_far = far.shape[0]
    fars = {0: (far, 0)}

    def first_rows(where, count):
        return (where[0], where[1], where[1] + count)

    near_b = across(first_b, "inner", 1)
    fars[1] = (across(far, "inner", 1), 0)
    own_done = far

    known = [0] + [1 << bit for bit in range(inner_bits)]
    late = [d for d in range(n_inner) if d not in known]
    last = sends[inner_bits]
    late_sets, late_counts = [], []
    for bit in range(1, inner_bits):
        count = sends[bit]
        others = range(1, 1 << bit)
        pieces = [first_rows(held[d], count) for d in others] + [first_rows(fars[0], n_far)]
        own_done = join_after(pieces, own_done)
        came = across(own_done, "inner", 1 << bit)
        for at, d in enumerate(others):
            held[d | 1 << bit] = (came, at * count)
        fars[1 << bit] = (came, len(others) * count)
        late_sets.append(came)
        late_counts += [prefix_counts(bit, 0, count)] * len(others) + [np.ones(n_far, np.int64)]
    for d in late:
        fars[d] = (across(far, "inner", d), 0)
    late_sets += [fars[d][0] for d in [0, 1] + late]
    late_counts.append(np.ones(n_far * (2 + len(late)), np.int64))

    early_sets = [held[1][0], near_b] + [held[d][0] for d in known[2:]]
    early_counts = [prefix_counts(0, 0, sends[0])]
    early_counts += [prefix_counts(bit, 0, sends[bit]) for bit in range(1, inner_bits)]
    state = attend(query_rows, early_sets, np.concatenate(early_counts), states=own_states)

    pieces = [first_rows(held[d], last) for d in range(n_inner)]
    pieces += [first_rows(fars[d], n_far) for d in range(n_inner)]
    core = across(join_after(pieces, state[1]), "outer", 1)
    state = attend(query_rows, late_sets, np.concatenate(late_counts), states=[state])
    result = attend(query_rows, [core], states=[state], out_weight=out_weight)
    return result[None]


def solution(mesh):
    placed = (P("outer", "inner", None), P("outer", "inner", None), P("outer", "inner", None), P())
    return jax.shard_map(
        local, mesh=mesh, in_specs=placed, out_specs=P("outer", "inner", None), check_vma=False
    )
```

```python
import math

import jax
import jax.numpy as jnp
import numpy as np
from jax import lax
from jax.experimental import pallas as pl
from jax.experimental.pallas import tpu as pltpu
from jax.sharding import PartitionSpec as P

HEAD_DIM = 64
GSTEP = 64
PAIR = 2 * HEAD_DIM
CHUNK = 512
KEY_CHUNK = 512
OWN_PARTS = 3
LANES = 128
LOG2E = math.log2(math.e)
VMEM_BYTES = 16 * 1024 * 1024
JOIN_VMEM_BYTES = 8 * 1024 * 1024
FETCH_VMEM_BYTES = 60 * 1024 * 1024


def across(block, axis, flip):
    return lax.ppermute(block, axis, [(i, i ^ flip) for i in range(lax.axis_size(axis))])


def after(block, *others):
    return lax.optimization_barrier((block, *others))[0]


def join_after(pieces, other):
    width = pieces[0][0].shape[1]
    total = sum(high - low for _, low, high in pieces)

    def kernel(*refs):
        out_ref, at = refs[-1], 0
        for ref, (_, low, high) in zip(refs, pieces):
            out_ref[at : at + high - low, :] = ref[low:high, :]
            at += high - low

    return pl.pallas_call(
        kernel,
        out_shape=jax.ShapeDtypeStruct((total, width), pieces[0][0].dtype),
        in_specs=[pl.BlockSpec(memory_space=pltpu.VMEM)] * len(pieces)
        + [pl.BlockSpec(memory_space=pl.ANY)],
        compiler_params=pltpu.CompilerParams(vmem_limit_bytes=JOIN_VMEM_BYTES),
        cost_estimate=pl.CostEstimate(
            flops=0, bytes_accessed=4 * total * width, transcendentals=0
        ),
    )(*[block for block, _, _ in pieces], other)


def runs(counts):
    found = []
    for at, value in enumerate(counts):
        if found and found[-1][2] == value:
            found[-1][1] = at + 1
        else:
            found.append([at, at + 1, int(value)])
    return [tuple(entry) for entry in found]


def order_rows(select, key_rows, values, prefixes):
    tokens, width = key_rows.shape

    def kernel(select_hbm, key_hbm, value_hbm, *refs):
        out_refs, (select_ref, row_ref, sems) = refs[: len(prefixes)], refs[len(prefixes) :]
        copies = [
            pltpu.make_async_copy(select_hbm, select_ref, sems.at[0]),
            pltpu.make_async_copy(key_hbm, row_ref.at[0], sems.at[1]),
            pltpu.make_async_copy(value_hbm, row_ref.at[1], sems.at[2]),
        ]
        for copy in copies:
            copy.start()
        copies[0].wait()
        for half in range(2):
            copies[1 + half].wait()
            moved = jnp.dot(
                select_ref[...], row_ref[half], preferred_element_type=jnp.float32
            ).astype(jnp.bfloat16)
            for (low, high), out_ref in zip(prefixes, out_refs):
                out_ref[:, half * width : (half + 1) * width] = moved[low:high]

    return pl.pallas_call(
        kernel,
        out_shape=[
            jax.ShapeDtypeStruct((high - low, 2 * width), jnp.bfloat16) for low, high in prefixes
        ],
        in_specs=[pl.BlockSpec(memory_space=pltpu.HBM)] * 3,
        scratch_shapes=[
            pltpu.VMEM(select.shape, jnp.bfloat16),
            pltpu.VMEM((2, tokens, width), jnp.bfloat16),
            pltpu.SemaphoreType.DMA((3,)),
        ],
        compiler_params=pltpu.CompilerParams(vmem_limit_bytes=FETCH_VMEM_BYTES),
        cost_estimate=pl.CostEstimate(
            flops=4 * select.size * width, bytes_accessed=6 * tokens * width, transcendentals=0
        ),
    )(select, key_rows, values)


def attend(queries, sets, counts=None, row_strides=None, part=(0, 1), states=(), out_weight=None, wait=None):
    tokens = queries.shape[0]
    full = queries.shape[1]
    width = full // part[1]
    base = part[0] * width
    heads, pairs = width // HEAD_DIM, width // PAIR
    joined = [not isinstance(block, tuple) for block in sets]
    sizes = [(block if whole else block[0]).shape[0] for block, whole in zip(sets, joined)]
    keys = sum(sizes)
    padded = -(-keys // LANES) * LANES
    row_runs = [(0, keys, 1)] if counts is None else runs(counts)
    scale = HEAD_DIM**-0.5 * LOG2E
    final = out_weight is not None
    groups = max(len(states), 1)

    def kernel(*refs):
        refs = list(refs)
        query_ref = refs.pop(0)
        set_refs = []
        for whole in joined:
            ref = refs.pop(0)
            set_refs.append((ref, ref, full) if whole else (ref, refs.pop(0), 0))
        state_refs = [[refs.pop(0) for _ in range(3)] for _ in states]
        if wait is not None:
            refs.pop(1 if final else 0)
        if final:
            weight_ref, out_hbm = refs.pop(0), refs.pop(0)
            attended_ref, out_ref, result_ref, sems = refs[-4:]
        else:
            numer_out, peak_out, total_out = [refs.pop(0) for _ in range(3)]
        score_ref, value_ref, key_ref, turned_ref = [refs.pop(0) for _ in range(4)]
        ones = jnp.ones((16, padded), jnp.bfloat16)
        if row_strides is not None:
            row = lax.broadcasted_iota(jnp.int32, (16, padded), 1)
            times = sum((row & (s - 1) == 0).astype(jnp.int32) for s in [1] + row_strides)
            ones = times.astype(jnp.float32).astype(jnp.bfloat16)
        key_chunks = [(low, min(KEY_CHUNK, keys - low)) for low in range(0, keys, KEY_CHUNK)]
        value_chunks = [(low, min(CHUNK, padded - low)) for low in range(0, padded, CHUNK)]

        def columns(pair, shift=0):
            return pl.ds(base + shift + pair * PAIR, PAIR)

        def head_queries(half):
            turned = turned_ref[...]
            row = lax.broadcasted_iota(jnp.int32, turned.shape, 0)
            own = (row < HEAD_DIM) if half == 0 else (row >= HEAD_DIM)
            return jnp.where(own, turned, jnp.zeros_like(turned))

        def load(pair):
            turned_ref[...] = query_ref[:, columns(pair)].T
            at = 0
            for (ref, _, _), size in zip(set_refs, sizes):
                key_ref[at : at + size, :] = ref[:, columns(pair)]
                at += size

        def score(half, query_head, chunk, running):
            low, count = chunk
            scores = jnp.dot(
                key_ref[low : low + count, :], query_head, preferred_element_type=jnp.float32
            )
            score_ref[half, low : low + count, :] = scores
            tallest = jnp.max(scores.reshape(count // 8, 8, tokens), axis=0)
            return tallest if running is None else jnp.maximum(running, tallest)

        def weigh(half, peak, weighted, chunk, gathered):
            low, size = chunk
            high = min(low + size, keys)
            pieces = []
            for first, last, times in row_runs:
                first, last = max(first, low), min(last, high)
                if first < last:
                    offset = peak - math.log2(times)
                    pieces.append(jnp.exp2(score_ref[half, first:last, :] * scale - offset))
            if low + size > keys:
                pieces.append(jnp.zeros((low + size - keys, tokens), jnp.float32))
            probs = (pieces[0] if len(pieces) == 1 else jnp.concatenate(pieces, axis=0)).astype(
                jnp.bfloat16
            )
            product = jnp.dot(
                weighted[:, low : low + size], probs, preferred_element_type=jnp.float32
            )
            return product if gathered is None else gathered + product

        def one_group(first_pair, last_pair, earlier, first_state):
            def local_rows(pair, half):
                start = (pair - first_state) * PAIR + half * HEAD_DIM
                return pl.ds(start, HEAD_DIM)

            def local_head(pair, half):
                return pl.ds(2 * (pair - first_state) + half, 1)

            def finish(pair, half, gathered, peak, before):
                numer, total = gathered[:HEAD_DIM], gathered[HEAD_DIM : HEAD_DIM + 1]
                if earlier is not None:
                    factor = jnp.exp2(before - peak)
                    numer = numer + factor * earlier[0][local_rows(pair, half), :]
                    total = total + factor * earlier[2][local_head(pair, half), :]
                rows = pl.ds(pair * PAIR + half * HEAD_DIM, HEAD_DIM)
                if final:
                    attended_ref[half] = (numer * (1.0 / total)).astype(jnp.bfloat16)
                    if half == 1:
                        both = attended_ref[...].reshape(PAIR, tokens)
                        out_ref[:, pl.ds(pair * PAIR, PAIR)] = both.T
                else:
                    head = pl.ds(2 * pair + half, 1)
                    numer_out[rows, :] = numer
                    peak_out[head, :] = peak
                    total_out[head, :] = total

            def overlap(pair, half, running, values_t, next_pair, next_half):
                peak = jnp.max(running, axis=0, keepdims=True) * scale
                before = None
                if earlier is not None:
                    before = earlier[1][local_head(pair, half), :]
                    peak = jnp.maximum(peak, before)
                weighted = jnp.concatenate(
                    [values_t[half * HEAD_DIM : (half + 1) * HEAD_DIM], ones], axis=0
                )
                ahead = next_pair < last_pair
                if ahead and next_half == 0:
                    load(next_pair)
                query_head = head_queries(next_half) if ahead else None
                next_running, gathered = None, None
                for step in range(max(len(key_chunks), len(value_chunks))):
                    if ahead and step < len(key_chunks):
                        next_running = score(
                            next_half, query_head, key_chunks[step], next_running
                        )
                    if step < len(value_chunks):
                        gathered = weigh(half, peak, weighted, value_chunks[step], gathered)
                finish(pair, half, gathered, peak, before)
                return next_running

            def pair_step(pair, running):
                at = 0
                for (_, ref, shift), size in zip(set_refs, sizes):
                    value_ref[at : at + size, :] = ref[:, columns(pair, shift)]
                    at += size
                if padded > keys:
                    value_ref[keys:, :] = jnp.zeros((padded - keys, PAIR), jnp.bfloat16)
                values_t = value_ref[...].T
                if row_strides is not None:
                    values_t = values_t * ones[:1]
                running = overlap(pair, 0, running, values_t, pair, 1)
                return overlap(pair, 1, running, values_t, pair + 1, 0)

            load(first_pair)
            first_head = head_queries(0)
            running = None
            for chunk in key_chunks:
                running = score(0, first_head, chunk, running)
            for pair in range(first_pair, last_pair):
                running = pair_step(pair, running)

        for group in range(groups):
            low, high = group * pairs // groups, (group + 1) * pairs // groups
            shared = len(states) == 1
            one_group(
                low, high, state_refs[0 if shared else group] if states else None, 0 if shared else low
            )
        if final:
            copies, step = [], tokens // 2
            for low in range(0, tokens, step):
                result_ref[low : low + step, :] = jnp.dot(
                    out_ref[low : low + step, :],
                    weight_ref[...],
                    preferred_element_type=jnp.float32,
                ).astype(jnp.bfloat16)
                for first in range(low, low + step, LANES):
                    rows = slice(first, first + LANES)
                    copies.append(
                        pltpu.make_async_copy(
                            result_ref.at[rows], out_hbm.at[rows], sems.at[len(copies)]
                        )
                    )
                    copies[-1].start()
            for copy in copies:
                copy.wait()

    if final:
        out_shape = jax.ShapeDtypeStruct((tokens, width), jnp.bfloat16)
    else:
        out_shape = [
            jax.ShapeDtypeStruct((width, tokens), jnp.float32),
            jax.ShapeDtypeStruct((heads, tokens), jnp.float32),
            jax.ShapeDtypeStruct((heads, tokens), jnp.float32),
        ]
    scratch = [
        pltpu.VMEM((2, padded, tokens), jnp.float32),
        pltpu.VMEM((padded, PAIR), jnp.bfloat16),
        pltpu.VMEM((padded, PAIR), jnp.bfloat16),
        pltpu.VMEM((PAIR, tokens), jnp.bfloat16),
    ]
    if final:
        scratch.append(pltpu.VMEM((2, HEAD_DIM, tokens), jnp.bfloat16))
        scratch += [pltpu.VMEM((tokens, width), jnp.bfloat16)] * 2
        scratch.append(pltpu.SemaphoreType.DMA((tokens // LANES,)))
    operands = [queries]
    for block, whole in zip(sets, joined):
        operands += [block] if whole else list(block)
    whole_spec = pl.BlockSpec(memory_space=pltpu.VMEM)
    specs = [whole_spec] * len(operands)
    for array in [array for state in states for array in state] + ([out_weight] if final else []):
        operands.append(array)
        specs.append(whole_spec)
    if wait is not None:
        operands.append(wait)
        specs.append(pl.BlockSpec(memory_space=pl.ANY))
    return pl.pallas_call(
        kernel,
        out_shape=out_shape,
        in_specs=specs,
        **({"out_specs": pl.BlockSpec(memory_space=pl.ANY)} if final else {}),
        scratch_shapes=scratch,
        compiler_params=pltpu.CompilerParams(
            vmem_limit_bytes=VMEM_BYTES
        ),
        cost_estimate=pl.CostEstimate(
            flops=16 * tokens * keys * width,
            bytes_accessed=(4 * keys * width + 4 * tokens * width),
            transcendentals=tokens * keys * heads,
        ),
    )(*operands)


def local(queries, key_rows, values, out_weight):
    query_rows, own_keys, own_values = queries[0], key_rows[0], values[0]
    tokens = query_rows.shape[0]
    n_inner, n_outer = lax.axis_size("inner"), lax.axis_size("outer")
    inner_bits = n_inner.bit_length() - 1
    strides = [1 << (bit + 1) for bit in range(inner_bits + 1)]
    sends = [tokens >> (bit + 1) for bit in range(inner_bits + 1)]
    n_global = tokens // GSTEP

    rows = np.arange(0, tokens, 2)
    rank = sum((rows % s == 0).astype(np.int64) for s in strides + [GSTEP])
    order = rows[np.lexsort((rows, -rank))]
    select = np.zeros((sends[0], tokens), np.float32)
    select[np.arange(sends[0]), order] = 1.0

    def prefix_counts(level, low, high):
        return sum((order[low:high] % s == 0).astype(np.int64) for s in strides[level:])

    first_a, first_b, far = order_rows(
        jnp.asarray(select, jnp.bfloat16),
        own_keys,
        own_values,
        [(0, sends[1]), (sends[1], sends[0]), (0, n_global)],
    )

    held = {0: (first_a, 0)}
    for bit in range(1, inner_bits):
        held[1 << bit] = (across(first_a[: sends[bit]], "inner", 1 << bit), 0)
    held[1] = (across(first_a, "inner", 1), 0)
    own_set = [(own_keys, own_values)]
    own_states, moved, flip = [], far, 2

    def own_part(wait):
        part = (len(own_states), OWN_PARTS)
        own_states.append(
            attend(query_rows, own_set, row_strides=strides, part=part, wait=wait)
        )

    while flip < n_outer:
        came = across(moved, "outer", flip)
        if len(own_states) < OWN_PARTS - 1:
            own_part(moved if own_states else None)
        moved = join_after([(moved, 0, moved.shape[0]), (came, 0, came.shape[0])], own_states[-1][1])
        flip *= 2
    far = moved
    n_far = far.shape[0]
    fars = {0: (far, 0)}

    def first_rows(where, count):
        return (where[0], where[1], where[1] + count)

    near_b = across(first_b, "inner", 1)
    fars[1] = (across(far, "inner", 1), 0)
    own_done = far

    known = [0] + [1 << bit for bit in range(inner_bits)]
    late = [d for d in range(n_inner) if d not in known]
    last = sends[inner_bits]
    late_sets, late_counts = [], []
    for bit in range(1, inner_bits):
        count = sends[bit]
        others = range(1, 1 << bit)
        pieces = [first_rows(held[d], count) for d in others] + [first_rows(fars[0], n_far)]
        own_done = join_after(pieces, own_done)
        came = across(own_done, "inner", 1 << bit)
        for at, d in enumerate(others):
            held[d | 1 << bit] = (came, at * count)
        fars[1 << bit] = (came, len(others) * count)
        late_sets.append(came)
        late_counts += [prefix_counts(bit, 0, count)] * len(others) + [np.ones(n_far, np.int64)]
    for d in late:
        fars[d] = (across(far, "inner", d), 0)
    late_sets += [fars[d][0] for d in [0, 1] + late]
    late_counts.append(np.ones(n_far * (2 + len(late)), np.int64))

    while len(own_states) < OWN_PARTS:
        own_part(own_done)
    early_sets = [held[1][0], near_b] + [held[d][0] for d in known[2:]]
    early_counts = [prefix_counts(0, 0, sends[0])]
    early_counts += [prefix_counts(bit, 0, sends[bit]) for bit in range(1, inner_bits)]
    state = attend(query_rows, early_sets, np.concatenate(early_counts), states=own_states)

    pieces = [first_rows(held[d], last) for d in range(n_inner)]
    pieces += [first_rows(fars[d], n_far) for d in range(n_inner)]
    core = across(join_after(pieces, state[1]), "outer", 1)
    state = attend(query_rows, late_sets, np.concatenate(late_counts), states=[state])
    result = attend(query_rows, [core], states=[state], out_weight=out_weight)
    return result[None]


def solution(mesh):
    placed = (P("outer", "inner", None), P("outer", "inner", None), P("outer", "inner", None), P())
    return jax.shard_map(
        local, mesh=mesh, in_specs=placed, out_specs=P("outer", "inner", None), check_vma=False
    )
```
